512 devices in a mesh: blk: 32 (over z_hi, x, core), rows: 16 (over z_lo, y).
Axes of the slice: x: 4, y: 8, z: 8 (z_hi: 4, z_lo: 2; z = z_hi * 2 + z_lo), core: 2. Of those that a mesh axis runs over, the one named last changes fastest.
Arguments:
- hidden_in: bfloat16 [128, 8192], P('rows', 'blk'), may hold values from -6 to 6
- norm_gain: bfloat16 [8192], P('blk'), may hold values from 0.25 to 1.75
- w_query: bfloat16 [8192, 8192], P('blk', 'rows'), may hold values from -0.0625 to 0.0625
- w_keyval: bfloat16 [8192, 2048], P('blk', 'rows'), may hold values from -0.25 to 0.25
- w_out: bfloat16 [8192, 8192], P('rows', 'blk'), may hold values from -0.0625 to 0.0625
- prefix_keys: bfloat16 [65536, 1024], P(('blk', 'rows')), may hold values from -60 to 60
- prefix_values: bfloat16 [65536, 1024], P(('blk', 'rows')), may hold values from -6 to 6
- own_keys: bfloat16 [128, 256, 1024], P('rows', 'blk'), may hold values from -12 to 12
- own_values: bfloat16 [128, 256, 1024], P('rows', 'blk'), may hold values from -6 to 6
- positions: int32 [128], replicated, may hold values from 65536 to 131071
- lengths: int32 [128], P('rows'), may hold values from 1 to 256, as said below
Outputs:
- hidden_out: bfloat16 [128, 8192], P('rows', 'blk')
The draws below stay inside these ranges and needn't reach their ends.
Inputs may be any that keep to these rules, and one draw needn't show every extreme that they name: `lengths`: own cache slots at or beyond a row's length are ignored; some row has exactly 256 live slots.
All inputs are finite; a program needn't handle non-finite values.
Results may differ from the reference program's by a relative error of at most 0.02.
Values may be sent and summed in bfloat16 or wider, within the bound.
No kernel may reach another device: no remote copies, remote signals or barrier semaphores. Data moves between devices by JAX's collectives and lax.ppermute only.
A program may use at most 64 MiB of HBM per device.

```python
import math
import jax
import jax.numpy as jnp
import numpy as np
from jax import lax

D = 8192
H = 64
KVH = 8
HD = 128
PRE_DEV = 128
ROWS = 128
PREFIX = 65536
SUF = 256
N_BLK = 32
N_ROWS = 16


def draw_prefix_keys(key, part):
    key = jax.random.fold_in(key, 11)
    first, second, third = jax.random.split(key, 3)
    spread = jnp.exp(jax.random.uniform(first, (PREFIX, 1), jnp.float32, math.log(0.3), math.log(3.0)))
    offset = jnp.where(jax.random.uniform(third, (1, KVH * HD), jnp.float32) < 0.5, -50.0, 50.0)
    base = jnp.clip(jax.random.normal(second, (PREFIX, KVH * HD), jnp.float32), -3.3, 3.3)
    return (offset + base * spread).astype(jnp.bfloat16)


def draw_lengths(key, part):
    key = jax.random.fold_in(key, 23)
    first, second, third = jax.random.split(key, 3)
    one_draw = jax.random.randint(first, (ROWS,), 1, SUF + 1, jnp.int32)
    two_draw = jax.random.randint(second, (ROWS,), 1, SUF + 1, jnp.int32)
    longest = jax.random.randint(third, (), 0, ROWS, jnp.int32)
    shorter = jnp.minimum(one_draw, two_draw)
    return jnp.where(jnp.arange(ROWS, dtype=jnp.int32) == longest, SUF, shorter).astype(jnp.int32)


def plant(values, key, low, high):
    shape = values.shape
    index_at = [jax.random.randint(jax.random.fold_in(key, axis), (), 0, shape[axis]) for axis in range(len(shape))]
    values = values.at[tuple(index_at)].set(low)
    longest = shape.index(max(shape))
    index_at[longest] = (index_at[longest] + 1) % shape[longest]
    return values.at[tuple(index_at)].set(high)


def levels(own_key, dims, shards, least, largest):
    loudness = 1.0
    for dim, parts in shards:
        draws = jax.random.uniform(jax.random.fold_in(jax.random.fold_in(own_key, 6), dim), (parts,), jnp.float32, least / len(shards), largest / len(shards))
        loudness = loudness * jnp.repeat(jnp.exp(draws), dims[dim] // parts).reshape((-1,) + (1,) * (len(dims) - 1 - dim))
    return loudness


def centred(own_key, shape, scale, bound, cuts=(), kind=jnp.bfloat16):
    level = levels(own_key, shape, cuts, -0.22, 0.18) if cuts else 1.0
    values = jax.random.normal(own_key, shape, jnp.float32) * scale * level
    return jnp.minimum(jnp.maximum(values, -bound), bound).astype(kind)


def setup_inputs(seed: int = 0) -> dict:
    keys = jax.random.split(jax.random.key(seed), 12)
    hidden_in = centred(keys[0], (ROWS, D), 1.0, 6.0, ((0, 16), (1, 32)))
    norm_gain = jnp.clip(1.0 + 0.15 * jax.random.normal(keys[1], (D,), jnp.float32), 0.25, 1.75).astype(jnp.bfloat16)
    w_query = centred(keys[2], (D, H * HD), D ** -0.5, 0.0625, ((0, 32), (1, 16)))
    w_keyval = centred(keys[3], (D, 2 * KVH * HD), (D // 16) ** -0.5, 0.25, ((0, 32), (1, 16)))
    w_out = centred(keys[4], (H * HD, D), (H * HD) ** -0.5, 0.0625, ((0, 16), (1, 32)))
    prefix_keys = draw_prefix_keys(jax.random.fold_in(keys[11], 71), 0)
    prefix_values = centred(keys[6], (PREFIX, KVH * HD), 1.0, 6.0, ((0, 512),))
    own_keys = centred(keys[7], (ROWS, SUF, KVH * HD), 3.0, 12.0, ((0, 16), (1, 32)))
    own_values = centred(keys[8], (ROWS, SUF, KVH * HD), 1.0, 6.0, ((0, 16), (1, 32)))
    positions = plant(jax.random.randint(keys[9], (ROWS,), PREFIX, 2 * PREFIX), jax.random.fold_in(keys[9], 1), PREFIX, (2 * PREFIX) - 1).astype(jnp.int32)
    lengths = draw_lengths(jax.random.fold_in(keys[11], 71), 0)
    return {"hidden_in": hidden_in, "norm_gain": norm_gain, "w_query": w_query, "w_keyval": w_keyval, "w_out": w_out, "prefix_keys": prefix_keys, "prefix_values": prefix_values, "own_keys": own_keys, "own_values": own_values, "positions": positions, "lengths": lengths}


def freq_table(width):
    return (1.0 / 500000.0 ** (np.arange(0, width, 2) / width)).astype(np.float32)

def rotate_pairs(values, positions):
    width = values.shape[-1]
    half_w = width // 2
    angles = positions.astype(jnp.float32)[:, None, None] * jnp.asarray(freq_table(width), jnp.float32)[None, None, :]
    cosine = jnp.cos(angles)
    sine = jnp.sin(angles)
    first = values[..., :half_w]
    second = values[..., half_w:]
    return jnp.concatenate([first * cosine - second * sine, second * cosine + first * sine], axis=-1)

def to_half(values):
    return lax.optimization_barrier(values.astype(jnp.bfloat16))

def reference(hidden_in, norm_gain, w_query, w_keyval, w_out, prefix_keys, prefix_values, own_keys, own_values, positions, lengths):
    inputs = hidden_in.astype(jnp.float32)
    mean_sq = lax.optimization_barrier(jnp.mean(inputs * inputs, axis=1, keepdims=True))
    normed = (inputs * lax.rsqrt(mean_sq + 1e-05) * norm_gain.astype(jnp.float32)[None, :]).astype(jnp.bfloat16)
    query_raw = to_half(jnp.dot(normed, w_query, preferred_element_type=jnp.float32))
    keyval_raw = to_half(jnp.dot(normed, w_keyval, preferred_element_type=jnp.float32))
    query = to_half(rotate_pairs(query_raw.astype(jnp.float32).reshape(ROWS, H, HD), positions))
    new_key = to_half(rotate_pairs(keyval_raw[:, :KVH * HD].astype(jnp.float32).reshape(ROWS, KVH, HD), positions))
    new_value = keyval_raw[:, KVH * HD:].reshape(ROWS, KVH, HD)
    grouped = query.astype(jnp.float32).reshape(ROWS, KVH, H // KVH, HD)
    scale = HD ** (-0.5)
    block_len = PRE_DEV * N_ROWS
    key_blocks = prefix_keys.reshape(N_BLK, block_len, KVH, HD)
    value_blocks = prefix_values.reshape(N_BLK, block_len, KVH, HD)

    def absorb(carry, block):
        peak, mass, accum = carry
        keys_b, values_b = block
        scores = jnp.einsum('rkgd,tkd->rkgt', grouped, keys_b.astype(jnp.float32)) * scale
        new_peak = jnp.maximum(peak, lax.optimization_barrier(jnp.max(scores, axis=-1)))
        weights = jnp.exp(scores - new_peak[..., None])
        shrink = jnp.exp(peak - new_peak)
        mass = mass * shrink + lax.optimization_barrier(jnp.sum(weights, axis=-1))
        accum = accum * shrink[..., None] + jnp.einsum('rkgt,tkd->rkgd', to_half(weights).astype(jnp.float32), values_b.astype(jnp.float32))
        return ((new_peak, mass, accum), None)
    start_peak = jnp.full((ROWS, KVH, H // KVH), -jnp.inf, jnp.float32)
    start_mass = jnp.zeros((ROWS, KVH, H // KVH), jnp.float32)
    start_accum = jnp.zeros((ROWS, KVH, H // KVH, HD), jnp.float32)
    (peak, mass, accum), _ = lax.scan(absorb, (start_peak, start_mass, start_accum), (key_blocks, value_blocks))
    own_k = own_keys.reshape(ROWS, SUF, KVH, HD).astype(jnp.float32)
    own_v = own_values.reshape(ROWS, SUF, KVH, HD).astype(jnp.float32)
    own_scores = jnp.einsum('rkgd,rtkd->rkgt', grouped, own_k) * scale
    valid = jnp.arange(SUF, dtype=jnp.int32)[None, :] < lengths[:, None]
    own_scores = jnp.where(valid[:, None, None, :], own_scores, -jnp.inf)
    new_scores = jnp.einsum('rkgd,rkd->rkg', grouped, new_key.astype(jnp.float32)) * scale
    top = jnp.maximum(jnp.maximum(peak, lax.optimization_barrier(jnp.max(own_scores, axis=-1))), new_scores)
    own_w = jnp.exp(own_scores - top[..., None])
    new_w = jnp.exp(new_scores - top)
    shrink = jnp.exp(peak - top)
    mass = mass * shrink + lax.optimization_barrier(jnp.sum(own_w, axis=-1)) + new_w
    accum = accum * shrink[..., None] + jnp.einsum('rkgt,rtkd->rkgd', to_half(own_w).astype(jnp.float32), own_v)
    accum = accum + to_half(new_w).astype(jnp.float32)[..., None] * new_value.astype(jnp.float32)[:, :, None, :]
    attended = (accum / mass[..., None]).reshape(ROWS, H * HD).astype(jnp.bfloat16)
    mixed = jnp.dot(attended, w_out, preferred_element_type=jnp.float32)
    return (inputs + mixed).astype(jnp.bfloat16)
```

```python
import jax
import jax.numpy as jnp
import numpy as np
from jax import lax
from jax.experimental import pallas as pl
from jax.experimental.pallas import tpu as pltpu
from jax.sharding import PartitionSpec as P

HD = 128
F32 = jnp.float32
BF = jnp.bfloat16
VM = pl.BlockSpec(memory_space=pltpu.VMEM)
SM = pl.BlockSpec(memory_space=pltpu.SMEM)
NT = (((1,), (1,)), ((), ()))
K0, V0, OK0, OV0, X0, L0, END = 0, 64, 128, 160, 192, 208, 224


def params():
    return pltpu.CompilerParams(vmem_limit_bytes=48 * 1024 * 1024)


def iota(shape, dim):
    return lax.broadcasted_iota(jnp.int32, shape, dim)


def pack_body(who, lens, keys, values, own_k, own_v, hidden, out):
    b, r = who[0], who[1]
    x = hidden[...].astype(F32)
    x_tile = jnp.concatenate([x[:, :HD], x[:, HD:]], axis=0).astype(BF)
    lane = iota((16, HD), 1) - 32 * lax.rem(r, 4)
    inside = (lane >= 0) & (lane < 32)
    slot = 8 * b + lax.rem(lane + HD, 8)
    which = lax.div(lane + HD, 8) - 16
    for p in range(2):
        live = jnp.zeros((16, HD), jnp.int32)
        for k in range(4):
            live = jnp.where(which == k, lens[4 * p + k], live)
        flags = jnp.where(inside & (slot < live), 1.0, 0.0).astype(BF)
        for h in range(8):
            col = slice(h * HD, (h + 1) * HD)
            d = 2 * h + p
            out[d, K0:V0, :] = keys[64 * p : 64 * p + 64, col]
            out[d, V0:OK0, :] = values[64 * p : 64 * p + 64, col]
            out[d, OK0:OV0, :] = own_k[32 * p : 32 * p + 32, col]
            out[d, OV0:X0, :] = own_v[32 * p : 32 * p + 32, col]
            out[d, X0:L0, :] = x_tile
            out[d, L0:END, :] = flags


def project_body(x_ref, gain, wq, wkv, out):
    xr = x_ref[...].astype(F32)
    x = jnp.concatenate(
        [xr[:, :8, :].reshape(128, HD), xr[:, 8:, :].reshape(128, HD)], axis=1
    )
    square = lax.dot_general(
        jnp.ones((8, 2 * HD), F32), x * x, NT,
        precision=lax.Precision.HIGHEST, preferred_element_type=F32,
    )
    high = square.astype(BF).astype(F32)
    sq_tile = jnp.where(iota((8, HD), 0) == 0, high, 0.0)
    sq_tile = jnp.where(iota((8, HD), 0) == 1, square - high, sq_tile)
    xg = (x * gain[...].astype(F32)).astype(BF)
    q = jnp.dot(xg, wq[...], preferred_element_type=F32)
    kv = jnp.dot(xg, wkv[...], preferred_element_type=F32)
    for g in range(8):
        for h in range(4):
            b = 4 * g + h
            out[b, 0:16, :] = q[16 * g : 16 * g + 16, HD * h : HD * h + HD].astype(BF)
            first = 8 * (b // 2)
            out[b, 16:32, :] = jnp.concatenate([kv[first : first + 8, :], sq_tile], axis=0).astype(BF)


def rotate(u, cosine, sine):
    return u * cosine + pltpu.roll(u, HD // 2, 1) * sine


def query_body(who, parts, cosine, sine, q_out, kv_out):
    b, r = who[0], who[1]
    total = jnp.sum(parts[...].astype(F32), axis=0)
    square = total[24:25, :] + total[25:26, :]
    inv = lax.rsqrt(square / 8192.0 + 1e-05)
    lane16, sub16 = iota((16, HD), 1), iota((16, HD), 0)
    col = jnp.sum(jnp.where(lane16 == 16 * lax.div(b, 4) + sub16, inv, 0.0), axis=1, keepdims=True)
    lane8, sub8 = iota((8, HD), 1), iota((8, HD), 0)
    col8 = jnp.sum(jnp.where(lane8 == 8 * lax.div(b, 2) + sub8, inv, 0.0), axis=1, keepdims=True)
    cos, sin = cosine[...], sine[...]
    raw = (total[0:16, :] * col).astype(BF).astype(F32)
    query = rotate(raw, cos, sin).astype(BF)
    for i in range(q_out.shape[0]):
        q_out[i, :, :] = query
    upper = lax.rem(lax.div(b, 2), 2) == 1
    cos8 = jnp.where(upper, cos[8:16, :], cos[0:8, :])
    sin8 = jnp.where(upper, sin[8:16, :], sin[0:8, :])
    raw8 = (total[16:24, :] * col8).astype(BF).astype(F32)
    new = jnp.where(r < 8, rotate(raw8, cos8, sin8), raw8)
    kv_out[...] = jnp.concatenate([new, jnp.zeros((8, HD), F32)], axis=0).astype(BF)


def attend_body(who, mine, other, q_ref, new_a, new_b, out):
    b, r = who[0], who[1]
    scale = HD ** (-0.5)
    even = lax.rem(r, 2) == 0
    fa, fb = new_a[...].astype(F32), new_b[...].astype(F32)
    new_k = jnp.where(even, fa, fb).astype(BF)
    new_v = jnp.where(even, fb, fa).astype(BF)
    sources = (mine, other)
    halves = (lax.rem(r, 2), 1 - lax.rem(r, 2))
    keys = [s[:, K0:V0, :].reshape(1024, HD) for s in sources]
    values = [s[:, V0:OK0, :].reshape(1024, HD) for s in sources]
    row_q = iota((128, HD), 0)
    row_q = 16 * (row_q // 64) + row_q % 16
    lane = iota((128, HD), 1)
    row_new = 8 * lax.div(b, 2) + iota((128, 16), 1)
    mine_new = (iota((128, 16), 1) // 4) == lax.rem(b, 2)
    lane_s = iota((128, HD), 1)
    for t in range(4):
        q = q_ref[8 * t : 8 * t + 8].reshape(128, HD)
        scores, vals = [], []
        for k, v in zip(keys, values):
            scores.append(lax.dot_general(q, k, NT, preferred_element_type=F32) * scale)
            vals.append(v)
        for s, half in zip(sources, halves):
            own_k = s[4 * t : 4 * t + 4, OK0:OV0, :].reshape(128, HD)
            own_v = s[4 * t : 4 * t + 4, OV0:X0, :].reshape(128, HD)
            live = jnp.sum(s[4 * t : 4 * t + 4, L0:END, :].astype(F32), axis=0)[0:1, :]
            row_k = 8 * (lane // 32) + 4 * half + (lane % 32) // 8
            good = (row_k == row_q) & (live > 0.5)
            sc = lax.dot_general(q, own_k, NT, preferred_element_type=F32) * scale
            scores.append(jnp.where(good, sc, -jnp.inf))
            vals.append(own_v)
        sc = lax.dot_general(q, new_k, NT, preferred_element_type=F32) * scale
        good = mine_new & (row_new == row_q[:, :16] + 32 * t)
        scores.append(jnp.where(good, sc, -jnp.inf))
        vals.append(new_v)
        peak = jnp.max(scores[0], axis=1, keepdims=True)
        for sc in scores[1:]:
            peak = jnp.maximum(peak, jnp.max(sc, axis=1, keepdims=True))
        high = peak.astype(BF).astype(F32)
        low = (peak - high).astype(BF).astype(F32)
        shift = high + low
        mass = jnp.zeros((128, 1), F32)
        acc = jnp.zeros((128, HD), F32)
        for sc, v in zip(scores, vals):
            w = jnp.exp(sc - shift)
            mass = mass + jnp.sum(w, axis=1, keepdims=True)
            acc = acc + jnp.dot(w.astype(BF), v, preferred_element_type=F32)
        mass_high = mass.astype(BF).astype(F32)
        stats = jnp.where(
            lane_s == 0, high,
            jnp.where(lane_s == 1, low, jnp.where(lane_s == 2, mass_high, jnp.where(lane_s == 3, mass - mass_high, 0.0))),
        )
        out[8 * t : 8 * t + 8, 0:16, :] = acc.astype(BF).reshape(8, 16, HD)
        out[8 * t : 8 * t + 8, 16:32, :] = stats.astype(BF).reshape(8, 16, HD)


def combine_body(parts, out):
    acc = parts[:, 0:16, :].astype(F32)
    stats = parts[:, 16:32, :].astype(F32)
    peak = stats[:, :, 0:1] + stats[:, :, 1:2]
    mass = stats[:, :, 2:3] + stats[:, :, 3:4]
    top = jnp.max(peak, axis=0, keepdims=True)
    shrink = jnp.exp(peak - top)
    whole = jnp.sum(mass * shrink, axis=0)
    summed = jnp.sum(acc * shrink, axis=0)
    attended = (summed / whole).astype(BF)
    for i in range(out.shape[0]):
        out[i, :, :] = attended


def output_body(att, w, out):
    groups = att[...].reshape(8, 4, 16, HD)
    total = jnp.zeros(out.shape, F32)
    for h in range(4):
        total = total + jnp.dot(
            groups[:, h].reshape(128, HD), w[HD * h : HD * h + HD, :], preferred_element_type=F32
        )
    out[...] = total.astype(BF)


def rotary_tables(positions):
    freq = (1.0 / 500000.0 ** (np.arange(0, HD, 2) / HD)).astype(np.float32)
    angles = positions.astype(F32)[:, None] * jnp.asarray(np.concatenate([freq, freq]), F32)[None, :]
    sign = np.concatenate([-np.ones(HD // 2), np.ones(HD // 2)]).astype(np.float32)
    return jnp.cos(angles), jnp.sin(angles) * jnp.asarray(sign)[None, :]


def on_device(
    hidden_in,
    norm_gain,
    w_query,
    w_keyval,
    w_out,
    prefix_keys,
    prefix_values,
    own_keys,
    own_values,
    positions,
    lengths,
):
    b, r = lax.axis_index("blk"), lax.axis_index("rows")
    who = jnp.stack([b, r]).astype(jnp.int32)
    sds = jax.ShapeDtypeStruct
    packed = pl.pallas_call(
        pack_body,
        out_shape=sds((16, END, HD), BF),
        in_specs=[SM, SM] + [VM] * 5,
        out_specs=VM,
        compiler_params=params(),
        name="pack",
    )(who, lengths, prefix_keys, prefix_values, own_keys.reshape(64, 1024), own_values.reshape(64, 1024), hidden_in)
    mine = lax.all_to_all(packed, "rows", 0, 0, tiled=True)
    other = lax.ppermute(mine, "rows", [(i, i ^ 1) for i in range(16)])
    parts = pl.pallas_call(
        project_body,
        grid=(1,),
        out_shape=sds((32, 32, HD), BF),
        in_specs=[
            pl.BlockSpec((16, L0 - X0, HD), lambda i: (0, X0 // 16, 0)),
            pl.BlockSpec((1, 256), lambda i: (0, 0)),
            pl.BlockSpec((256, 512), lambda i: (0, 0)),
            pl.BlockSpec((256, HD), lambda i: (0, 0)),
        ],
        out_specs=pl.BlockSpec((32, 32, HD), lambda i: (0, 0, 0)),
        compiler_params=params(),
        name="project",
    )(mine, norm_gain.reshape(1, 256), w_query, w_keyval)
    parts = lax.all_to_all(parts, "blk", 0, 0, tiled=True)
    cosine, sine = rotary_tables(lax.dynamic_slice_in_dim(positions, 16 * (b // 4), 16, 0))
    query, new = pl.pallas_call(
        query_body,
        out_shape=(sds((32, 16, HD), BF), sds((16, HD), BF)),
        in_specs=[SM, VM, VM, VM],
        out_specs=(VM, VM),
        compiler_params=params(),
        name="query",
    )(who, parts, cosine, sine)
    new_a = lax.ppermute(new, "rows", [(s, 2 * (s % 8) + s // 8) for s in range(16)])
    new_b = lax.ppermute(new, "rows", [(s, 2 * (s % 8) + 1 - s // 8) for s in range(16)])
    query = lax.all_to_all(query, "blk", 0, 0, tiled=True)
    partial = pl.pallas_call(
        attend_body,
        out_shape=sds((32, 32, HD), BF),
        in_specs=[SM] + [VM] * 5,
        out_specs=VM,
        compiler_params=params(),
        name="attend",
    )(who, mine, other, query, new_a, new_b)
    partial = lax.all_to_all(partial, "blk", 0, 0, tiled=True)
    attended = pl.pallas_call(
        combine_body,
        out_shape=sds((32, 16, HD), BF),
        in_specs=[VM],
        out_specs=VM,
        compiler_params=params(),
        name="combine",
    )(partial)
    attended = lax.all_to_all(attended, "blk", 0, 0, tiled=True)
    mixed = pl.pallas_call(
        output_body,
        out_shape=sds((128, 256), BF),
        in_specs=[VM, VM],
        out_specs=VM,
        compiler_params=params(),
        name="output",
    )(attended, w_out)
    mixed = lax.all_to_all(mixed.reshape(16, 8, 256), "rows", 0, 0, tiled=True)
    return (hidden_in.astype(F32) + jnp.sum(mixed.astype(F32), axis=0)).astype(BF)


def solution(mesh):
    return jax.shard_map(
        on_device,
        mesh=mesh,
        in_specs=(
            P("rows", "blk"),
            P("blk"),
            P("blk", "rows"),
            P("blk", "rows"),
            P("rows", "blk"),
            P(("blk", "rows"), None),
            P(("blk", "rows"), None),
            P("rows", "blk", None),
            P("rows", "blk", None),
            P(),
            P("rows"),
        ),
        out_specs=P("rows", "blk"),
        check_vma=False,
    )
```

```python
import jax
import jax.numpy as jnp
import numpy as np
from jax import lax
from jax.experimental import pallas as pl
from jax.experimental.pallas import tpu as pltpu
from jax.sharding import PartitionSpec as P

HD = 128
F32 = jnp.float32
BF = jnp.bfloat16
VM = pl.BlockSpec(memory_space=pltpu.VMEM)
SM = pl.BlockSpec(memory_space=pltpu.SMEM)
NT = (((1,), (1,)), ((), ()))
K0, V0, OK0, OV0, X0, END = 0, 64, 128, 160, 192, 208


def params(mib=48):
    return pltpu.CompilerParams(vmem_limit_bytes=mib * 1024 * 1024)


def iota(shape, dim):
    return lax.broadcasted_iota(jnp.int32, shape, dim)


def pack_body(who, lens, hidden, keys_hbm, values_hbm, own_k_hbm, own_v_hbm, out, keys, values, own_k, own_v, sems):
    copies = [
        pltpu.make_async_copy(src, dst, sems.at[i])
        for i, (src, dst) in enumerate(
            ((keys_hbm, keys), (values_hbm, values), (own_k_hbm, own_k), (own_v_hbm, own_v))
        )
    ]
    for copy in copies:
        copy.start()
    b = who[0]
    x = hidden[...].astype(F32)
    x_tile = jnp.concatenate([x[:, :HD], x[:, HD:]], axis=0).astype(BF)
    sub = iota((32, HD), 0)
    slot = 8 * b + sub % 8
    dead = []
    for p in range(2):
        live = jnp.zeros((32, HD), jnp.int32)
        for k in range(4):
            live = jnp.where(sub // 8 == k, lens[4 * p + k], live)
        dead.append(slot >= live)
    for copy in copies:
        copy.wait()
    for p in range(2):
        for h in range(8):
            col = slice(h * HD, (h + 1) * HD)
            d = 2 * h + p
            out[d, K0:V0, :] = keys[64 * p : 64 * p + 64, col]
            out[d, V0:OK0, :] = values[64 * p : 64 * p + 64, col]
            own = own_k[32 * p : 32 * p + 32, col].astype(F32)
            out[d, OK0:OV0, :] = jnp.where(dead[p], jnp.nan, own).astype(BF)
            out[d, OV0:X0, :] = own_v[32 * p : 32 * p + 32, col]
            out[d, X0:END, :] = x_tile


def project_body(who, x_ref, gain, wq, wa, wb, out):
    xr = x_ref[...].astype(F32)
    x = jnp.concatenate(
        [xr[:, :8, :].reshape(128, HD), xr[:, 8:, :].reshape(128, HD)], axis=1
    )
    square = lax.dot_general(
        jnp.ones((8, 2 * HD), F32), x * x, NT,
        precision=lax.Precision.HIGHEST, preferred_element_type=F32,
    )
    high = square.astype(BF).astype(F32)
    sq_tile = jnp.where(iota((8, HD), 0) == 0, high, 0.0)
    sq_tile = jnp.where(iota((8, HD), 0) == 1, square - high, sq_tile)
    xg = (x * gain[...].astype(F32)).astype(BF)
    q = jnp.dot(xg, wq[...], preferred_element_type=F32)
    even = lax.rem(who[1], 2) == 0
    first = jnp.dot(xg, wa[...], preferred_element_type=F32)
    second = jnp.dot(xg, wb[...], preferred_element_type=F32)
    key = jnp.where(even, first, second)
    value = jnp.where(even, second, first)
    for b in range(32):
        g, h = b // 4, b % 4
        out[b, 0:16, :] = q[16 * g : 16 * g + 16, HD * h : HD * h + HD].astype(BF)
        out[b, 16:32, :] = jnp.concatenate(
            [key[4 * b : 4 * b + 4, :], value[4 * b : 4 * b + 4, :], sq_tile], axis=0
        ).astype(BF)


def rotate(u, cosine, sine):
    return u * cosine + pltpu.roll(u, HD // 2, 1) * sine


def query_body(who, parts, cosine, sine, q_out, kv_out):
    b = who[0]
    total = jnp.sum(parts[...].astype(F32), axis=0)
    square = total[24:25, :] + total[25:26, :]
    inv = lax.rsqrt(square / 8192.0 + 1e-05)
    lane, sub = iota((24, HD), 1), iota((24, HD), 0)
    row = jnp.where(sub < 16, 16 * lax.div(b, 4) + sub, 4 * b + sub % 4)
    col = jnp.sum(jnp.where(lane == row, inv, 0.0), axis=1, keepdims=True)
    raw = (total[0:24, :] * col).astype(BF).astype(F32)
    turned = rotate(raw, cosine[...], sine[...])
    query = turned[0:16, :].astype(BF)
    for i in range(q_out.shape[0]):
        q_out[i, :, :] = query
    kv_out[...] = jnp.concatenate([turned[16:24, :], jnp.zeros((8, HD), F32)], axis=0).astype(BF)


def attend_body(who, mine, other, q_ref, new_ref, out):
    b, r = who[0], who[1]
    scale = HD ** (-0.5)
    new_k = new_ref[...]
    new_v = pltpu.roll(new_k.astype(F32), 12, 0).astype(BF)
    sources = (mine, other)
    halves = (lax.rem(r, 2), 1 - lax.rem(r, 2))
    keys = [s[:, K0:V0, :].reshape(1024, HD) for s in sources]
    values = [s[:, V0:OK0, :].reshape(1024, HD) for s in sources]
    row_q = iota((128, HD), 0)
    row_q = 16 * (row_q // 64) + row_q % 16
    lane = iota((128, HD), 1)
    new_id = iota((128, 16), 1)
    lane_s = iota((128, HD), 1)
    for t in range(4):
        q = q_ref[8 * t : 8 * t + 8].reshape(128, HD)
        scores, vals = [], []
        for k, v in zip(keys, values):
            scores.append(lax.dot_general(q, k, NT, preferred_element_type=F32) * scale)
            vals.append(v)
        for s, half in zip(sources, halves):
            own_k = s[4 * t : 4 * t + 4, OK0:OV0, :].reshape(128, HD)
            own_v = s[4 * t : 4 * t + 4, OV0:X0, :].reshape(128, HD)
            row_k = 8 * (lane // 32) + 4 * half + (lane % 32) // 8
            sc = lax.dot_general(q, own_k, NT, preferred_element_type=F32) * scale
            good = (row_k == row_q) & (sc == sc)
            scores.append(jnp.where(good, sc, -jnp.inf))
            vals.append(own_v)
        sc = lax.dot_general(q, new_k, NT, preferred_element_type=F32) * scale
        good = (new_id < 4) & (4 * b + new_id == row_q[:, :16] + 32 * t)
        scores.append(jnp.where(good, sc, -jnp.inf))
        vals.append(new_v)
        peak = jnp.max(scores[0], axis=1, keepdims=True)
        for sc in scores[1:]:
            peak = jnp.maximum(peak, jnp.max(sc, axis=1, keepdims=True))
        high = peak.astype(BF).astype(F32)
        low = (peak - high).astype(BF).astype(F32)
        shift = high + low
        mass = jnp.zeros((128, 1), F32)
        acc = jnp.zeros((128, HD), F32)
        for sc, v in zip(scores, vals):
            w = jnp.exp(sc - shift)
            mass = mass + jnp.sum(w, axis=1, keepdims=True)
            acc = acc + jnp.dot(w.astype(BF), v, preferred_element_type=F32)
        mass_high = mass.astype(BF).astype(F32)
        stats = jnp.where(
            lane_s == 0, high,
            jnp.where(lane_s == 1, low, jnp.where(lane_s == 2, mass_high, jnp.where(lane_s == 3, mass - mass_high, 0.0))),
        )
        out[8 * t : 8 * t + 8, 0:16, :] = acc.astype(BF).reshape(8, 16, HD)
        out[8 * t : 8 * t + 8, 16:32, :] = stats.astype(BF).reshape(8, 16, HD)


def combine_body(parts, out):
    acc = parts[:, 0:16, :].astype(F32)
    stats = parts[:, 16:32, :].astype(F32)
    peak = stats[:, :, 0:1] + stats[:, :, 1:2]
    mass = stats[:, :, 2:3] + stats[:, :, 3:4]
    top = jnp.max(peak, axis=0, keepdims=True)
    shrink = jnp.exp(peak - top)
    whole = jnp.sum(mass * shrink, axis=0)
    summed = jnp.sum(acc * shrink, axis=0)
    attended = (summed / whole).astype(BF)
    for i in range(out.shape[0]):
        out[i, :, :] = attended


def output_body(att, w, out):
    groups = att[...].reshape(8, 4, 16, HD)
    total = jnp.zeros(out.shape, F32)
    for h in range(4):
        total = total + jnp.dot(
            groups[:, h].reshape(128, HD), w[HD * h : HD * h + HD, :], preferred_element_type=F32
        )
    out[...] = total.astype(BF)


def rotary_tables(positions):
    freq = (1.0 / 500000.0 ** (np.arange(0, HD, 2) / HD)).astype(np.float32)
    angles = positions.astype(F32)[:, None] * jnp.asarray(np.concatenate([freq, freq]), F32)[None, :]
    sign = np.concatenate([-np.ones(HD // 2), np.ones(HD // 2)]).astype(np.float32)
    return jnp.cos(angles), jnp.sin(angles) * jnp.asarray(sign)[None, :]


def on_device(
    hidden_in,
    norm_gain,
    w_query,
    w_keyval,
    w_out,
    prefix_keys,
    prefix_values,
    own_keys,
    own_values,
    positions,
    lengths,
):
    b, r = lax.axis_index("blk"), lax.axis_index("rows")
    who = jnp.stack([b, r]).astype(jnp.int32)
    sds = jax.ShapeDtypeStruct
    first_w = lax.ppermute(w_keyval, "rows", [(s, 2 * (s % 8) + s // 8) for s in range(16)])
    second_w = lax.ppermute(w_keyval, "rows", [(s, 2 * (s % 8) + 1 - s // 8) for s in range(16)])
    packed = pl.pallas_call(
        pack_body,
        out_shape=sds((16, END, HD), BF),
        in_specs=[SM, SM, VM] + [pl.BlockSpec(memory_space=pltpu.HBM)] * 4,
        out_specs=VM,
        scratch_shapes=[
            pltpu.VMEM((128, 1024), BF),
            pltpu.VMEM((128, 1024), BF),
            pltpu.VMEM((64, 1024), BF),
            pltpu.VMEM((64, 1024), BF),
            pltpu.SemaphoreType.DMA((4,)),
        ],
        name="pack",
    )(who, lengths, hidden_in, prefix_keys, prefix_values, own_keys.reshape(64, 1024), own_values.reshape(64, 1024))
    mine = lax.all_to_all(packed, "rows", 0, 0, tiled=True)
    parts = pl.pallas_call(
        project_body,
        grid=(1,),
        out_shape=sds((32, 32, HD), BF),
        in_specs=[
            SM,
            pl.BlockSpec((16, END - X0, HD), lambda i: (0, X0 // 16, 0)),
            pl.BlockSpec((1, 256), lambda i: (0, 0)),
            pl.BlockSpec((256, 512), lambda i: (0, 0)),
            pl.BlockSpec((256, HD), lambda i: (0, 0)),
            pl.BlockSpec((256, HD), lambda i: (0, 0)),
        ],
        out_specs=pl.BlockSpec((32, 32, HD), lambda i: (0, 0, 0)),
        compiler_params=params(),
        name="project",
    )(who, mine, norm_gain.reshape(1, 256), w_query, first_w, second_w)
    positions, parts = lax.optimization_barrier((positions, parts))
    parts = lax.all_to_all(parts, "blk", 0, 0, tiled=True)
    places = jnp.concatenate(
        [
            lax.dynamic_slice_in_dim(positions, 16 * (b // 4), 16, 0),
            lax.dynamic_slice_in_dim(positions, 4 * b, 4, 0),
            jnp.zeros(4, positions.dtype),
        ]
    )
    cosine, sine = rotary_tables(places)
    mine, cosine = lax.optimization_barrier((mine, cosine))
    other = lax.ppermute(mine, "rows", [(i, i ^ 1) for i in range(16)])
    query, new = pl.pallas_call(
        query_body,
        out_shape=(sds((32, 16, HD), BF), sds((16, HD), BF)),
        in_specs=[SM, VM, VM, VM],
        out_specs=(VM, VM),
        compiler_params=params(),
        cost_estimate=pl.CostEstimate(flops=2 * 10**9, bytes_accessed=1 << 20, transcendentals=0),
        name="query",
    )(who, parts, cosine, sine)
    query = lax.all_to_all(query, "blk", 0, 0, tiled=True)
    partial = pl.pallas_call(
        attend_body,
        out_shape=sds((32, 32, HD), BF),
        in_specs=[SM] + [VM] * 4,
        out_specs=VM,
        compiler_params=params(),
        name="attend",
    )(who, mine, other, query, new)
    partial = lax.all_to_all(partial, "blk", 0, 0, tiled=True)
    attended = pl.pallas_call(
        combine_body,
        out_shape=sds((32, 16, HD), BF),
        in_specs=[VM],
        out_specs=VM,
        compiler_params=params(),
        name="combine",
    )(partial)
    attended = lax.all_to_all(attended, "blk", 0, 0, tiled=True)
    mixed = pl.pallas_call(
        output_body,
        out_shape=sds((128, 256), BF),
        in_specs=[VM, VM],
        out_specs=VM,
        compiler_params=params(),
        name="output",
    )(attended, w_out)
    mixed = lax.all_to_all(mixed.reshape(16, 8, 256), "rows", 0, 0, tiled=True)
    return (hidden_in.astype(F32) + jnp.sum(mixed.astype(F32), axis=0)).astype(BF)


def solution(mesh):
    return jax.shard_map(
        on_device,
        mesh=mesh,
        in_specs=(
            P("rows", "blk"),
            P("blk"),
            P("blk", "rows"),
            P("blk", "rows"),
            P("rows", "blk"),
            P(("blk", "rows"), None),
            P(("blk", "rows"), None),
            P("rows", "blk", None),
            P("rows", "blk", None),
            P(),
            P("rows"),
        ),
        out_specs=P("rows", "blk"),
        check_vma=False,
    )
```

```python
import jax
import jax.numpy as jnp
import numpy as np
from jax import lax
from jax.experimental import pallas as pl
from jax.experimental.pallas import tpu as pltpu
from jax.sharding import PartitionSpec as P

HD = 128
F32 = jnp.float32
BF = jnp.bfloat16
VM = pl.BlockSpec(memory_space=pltpu.VMEM)
SM = pl.BlockSpec(memory_space=pltpu.SMEM)
NT = (((1,), (1,)), ((), ()))
K0, V0, OK0, OV0, X0, END = 0, 64, 128, 160, 192, 208


def params(mib=48):
    return pltpu.CompilerParams(vmem_limit_bytes=mib * 1024 * 1024)


def iota(shape, dim):
    return lax.broadcasted_iota(jnp.int32, shape, dim)


def pack_body(who, lens, hidden, keys_hbm, values_hbm, own_k_hbm, own_v_hbm, out, keys, values, own_k, own_v, sems):
    copies = [
        pltpu.make_async_copy(src, dst, sems.at[i])
        for i, (src, dst) in enumerate(
            ((keys_hbm, keys), (values_hbm, values), (own_k_hbm, own_k), (own_v_hbm, own_v))
        )
    ]
    for copy in copies:
        copy.start()
    b = who[0]
    x = hidden[...].astype(F32)
    x_tile = jnp.concatenate([x[:, :HD], x[:, HD:]], axis=0).astype(BF)
    sub = iota((32, HD), 0)
    slot = 8 * b + sub % 8
    dead = []
    for p in range(2):
        live = jnp.zeros((32, HD), jnp.int32)
        for k in range(4):
            live = jnp.where(sub // 8 == k, lens[4 * p + k], live)
        dead.append(slot >= live)
    for copy in copies:
        copy.wait()
    for p in range(2):
        for h in range(8):
            col = slice(h * HD, (h + 1) * HD)
            d = 2 * h + p
            out[d, K0:V0, :] = keys[64 * p : 64 * p + 64, col]
            out[d, V0:OK0, :] = values[64 * p : 64 * p + 64, col]
            own = own_k[32 * p : 32 * p + 32, col].astype(F32)
            out[d, OK0:OV0, :] = jnp.where(dead[p], jnp.nan, own).astype(BF)
            out[d, OV0:X0, :] = own_v[32 * p : 32 * p + 32, col]
            out[d, X0:END, :] = x_tile


def half_swap(x):
    return pltpu.roll(x, 4, 1)


def project_body(x_ref, gain, wq, wkv, out):
    xr = x_ref[...].astype(F32)
    x = jnp.concatenate(
        [xr[:, :8, :].reshape(128, HD), xr[:, 8:, :].reshape(128, HD)], axis=1
    )
    square = lax.dot_general(
        jnp.ones((8, 2 * HD), F32), x * x, NT,
        precision=lax.Precision.HIGHEST, preferred_element_type=F32,
    )
    high = square.astype(BF).astype(F32)
    sub = iota((16, 8, HD), 1)
    squares = jnp.where(sub == 4, high[None], jnp.where(sub == 5, (square - high)[None], 0.0))
    xg = (x * gain[...].astype(F32)).astype(BF)
    q = jnp.dot(xg, wq[...], preferred_element_type=F32)
    kv = jnp.dot(xg, wkv[...], preferred_element_type=F32).reshape(16, 8, HD)
    heads = [q[:, HD * h : HD * h + HD].reshape(16, 8, HD) for h in range(4)]
    low = sub < 4
    for p in range(2):
        tiles = []
        for u in range(2):
            first, second = heads[2 * u], heads[2 * u + 1]
            if p == 0:
                tiles.append(jnp.where(low, first, half_swap(second)))
            else:
                tiles.append(jnp.where(low, half_swap(first), second))
        tiles.append(jnp.where(low, kv if p == 0 else half_swap(kv), squares))
        tiles.append(jnp.zeros((16, 8, HD), F32))
        chunks = jnp.concatenate(tiles, axis=1).astype(BF)
        for j in range(16):
            out[2 * j + p, :, :] = chunks[j]


def rotate(u, cosine, sine):
    return u * cosine + pltpu.roll(u, HD // 2, 1) * sine


def query_body(who, parts, cosine, sine, q_out, q_own, kv_out):
    total = jnp.sum(parts[...].astype(F32), axis=0)
    square = total[20:21, :] + total[21:22, :]
    inv = lax.rsqrt(square / 8192.0 + 1e-05)
    lane, sub = iota((24, HD), 1), iota((24, HD), 0)
    col = jnp.sum(jnp.where(lane == 4 * who[0] + sub % 4, inv, 0.0), axis=1, keepdims=True)
    raw = (total[0:24, :] * col).astype(BF).astype(F32)
    turned = rotate(raw, cosine[...], sine[...])
    query = turned[0:16, :].astype(BF)
    q_own[...] = query
    for i in range(q_out.shape[0]):
        q_out[i, :, :] = query
    kv_out[...] = jnp.concatenate([turned[16:24, :], jnp.zeros((8, HD), F32)], axis=0).astype(BF)


def attend_body(who, mine, other, q_ref, out):
    r = who[1]
    scale = HD ** (-0.5)
    sources = (mine, other)
    halves = (lax.rem(r, 2), 1 - lax.rem(r, 2))
    keys = [s[:, K0:V0, :].reshape(1024, HD) for s in sources]
    values = [s[:, V0:OK0, :].reshape(1024, HD) for s in sources]
    row_q = iota((128, HD), 0)
    row_q = 4 * (row_q // 16) + row_q % 4
    lane = iota((128, HD), 1)
    lane_s = iota((128, HD), 1)
    for t in range(4):
        q = q_ref[8 * t : 8 * t + 8].reshape(128, HD)
        scores, vals = [], []
        for k, v in zip(keys, values):
            scores.append(lax.dot_general(q, k, NT, preferred_element_type=F32) * scale)
            vals.append(v)
        for s, half in zip(sources, halves):
            own_k = s[4 * t : 4 * t + 4, OK0:OV0, :].reshape(128, HD)
            own_v = s[4 * t : 4 * t + 4, OV0:X0, :].reshape(128, HD)
            row_k = 8 * (lane // 32) + 4 * half + (lane % 32) // 8
            sc = lax.dot_general(q, own_k, NT, preferred_element_type=F32) * scale
            good = (row_k == row_q) & (sc == sc)
            scores.append(jnp.where(good, sc, -jnp.inf))
            vals.append(own_v)
        peak = jnp.max(scores[0], axis=1, keepdims=True)
        for sc in scores[1:]:
            peak = jnp.maximum(peak, jnp.max(sc, axis=1, keepdims=True))
        high = peak.astype(BF).astype(F32)
        low = (peak - high).astype(BF).astype(F32)
        shift = high + low
        mass = jnp.zeros((128, 1), F32)
        acc = jnp.zeros((128, HD), F32)
        for sc, v in zip(scores, vals):
            w = jnp.exp(sc - shift)
            mass = mass + jnp.sum(w, axis=1, keepdims=True)
            acc = acc + jnp.dot(w.astype(BF), v, preferred_element_type=F32)
        mass_high = mass.astype(BF).astype(F32)
        stats = jnp.where(
            lane_s == 0, high,
            jnp.where(lane_s == 1, low, jnp.where(lane_s == 2, mass_high, jnp.where(lane_s == 3, mass - mass_high, 0.0))),
        )
        out[8 * t : 8 * t + 8, 0:16, :] = acc.astype(BF).reshape(8, 16, HD)
        out[8 * t : 8 * t + 8, 16:32, :] = stats.astype(BF).reshape(8, 16, HD)


def combine_body(who, parts, q_own, new_a, new_b, out):
    even = lax.rem(who[1], 2) == 0
    first, second = new_a[...].astype(F32), new_b[...].astype(F32)
    new_k = jnp.concatenate([jnp.where(even, first, second)[0:4, :]] * 4, axis=0)
    new_v = jnp.concatenate([jnp.where(even, second, first)[0:4, :]] * 4, axis=0)
    new = jnp.sum(q_own[...].astype(F32) * new_k, axis=1, keepdims=True) * HD ** (-0.5)
    acc = parts[:, 0:16, :].astype(F32)
    stats = parts[:, 16:32, :].astype(F32)
    peak = stats[:, :, 0:1] + stats[:, :, 1:2]
    mass = stats[:, :, 2:3] + stats[:, :, 3:4]
    top = jnp.maximum(jnp.max(peak, axis=0), new)
    shrink = jnp.exp(peak - top[None])
    new_w = jnp.exp(new - top)
    whole = jnp.sum(mass * shrink, axis=0) + new_w
    summed = jnp.sum(acc * shrink, axis=0) + new_w * new_v
    attended = (summed / whole).astype(BF)
    for i in range(out.shape[0]):
        out[i, :, :] = attended


def output_body(att, w, out):
    tiles = att[...].astype(F32).reshape(16, 2, 2, 8, HD)
    low = iota((16, 8, HD), 1) < 4
    total = jnp.zeros(out.shape, F32)
    for h in range(4):
        first, second = tiles[:, 0, h // 2], tiles[:, 1, h // 2]
        if h % 2 == 0:
            rows = jnp.where(low, first, half_swap(second))
        else:
            rows = jnp.where(low, half_swap(first), second)
        total = total + jnp.dot(
            rows.reshape(128, HD).astype(BF), w[HD * h : HD * h + HD, :], preferred_element_type=F32
        )
    out[...] = total.astype(BF)


def rotary_tables(positions):
    freq = (1.0 / 500000.0 ** (np.arange(0, HD, 2) / HD)).astype(np.float32)
    angles = positions.astype(F32)[:, None] * jnp.asarray(np.concatenate([freq, freq]), F32)[None, :]
    sign = np.concatenate([-np.ones(HD // 2), np.ones(HD // 2)]).astype(np.float32)
    return jnp.cos(angles), jnp.sin(angles) * jnp.asarray(sign)[None, :]


def on_device(
    hidden_in,
    norm_gain,
    w_query,
    w_keyval,
    w_out,
    prefix_keys,
    prefix_values,
    own_keys,
    own_values,
    positions,
    lengths,
):
    b, r = lax.axis_index("blk"), lax.axis_index("rows")
    who = jnp.stack([b, r]).astype(jnp.int32)
    sds = jax.ShapeDtypeStruct
    packed = pl.pallas_call(
        pack_body,
        out_shape=sds((16, END, HD), BF),
        in_specs=[SM, SM, VM] + [pl.BlockSpec(memory_space=pltpu.HBM)] * 4,
        out_specs=VM,
        scratch_shapes=[
            pltpu.VMEM((128, 1024), BF),
            pltpu.VMEM((128, 1024), BF),
            pltpu.VMEM((64, 1024), BF),
            pltpu.VMEM((64, 1024), BF),
            pltpu.SemaphoreType.DMA((4,)),
        ],
        name="pack",
    )(who, lengths, hidden_in, prefix_keys, prefix_values, own_keys.reshape(64, 1024), own_values.reshape(64, 1024))
    mine = lax.all_to_all(packed, "rows", 0, 0, tiled=True)
    parts = pl.pallas_call(
        project_body,
        grid=(1,),
        out_shape=sds((32, 32, HD), BF),
        in_specs=[
            pl.BlockSpec((16, END - X0, HD), lambda i: (0, X0 // 16, 0)),
            pl.BlockSpec((1, 256), lambda i: (0, 0)),
            pl.BlockSpec((256, 512), lambda i: (0, 0)),
            pl.BlockSpec((256, HD), lambda i: (0, 0)),
        ],
        out_specs=pl.BlockSpec((32, 32, HD), lambda i: (0, 0, 0)),
        compiler_params=params(),
        name="project",
    )(mine, norm_gain.reshape(1, 256), w_query, w_keyval)
    positions, parts = lax.optimization_barrier((positions, parts))
    parts = lax.all_to_all(parts, "blk", 0, 0, tiled=True)
    places = lax.dynamic_slice_in_dim(positions, 4 * b, 4, 0)
    still = jnp.zeros_like(places)
    places = jnp.concatenate([places] * 4 + [jnp.where(r < 8, places, still), still])
    cosine, sine = rotary_tables(places)
    mine, cosine = lax.optimization_barrier((mine, cosine))
    other = lax.ppermute(mine, "rows", [(i, i ^ 1) for i in range(16)])
    query, q_own, new = pl.pallas_call(
        query_body,
        out_shape=(sds((32, 16, HD), BF), sds((16, HD), BF), sds((16, HD), BF)),
        in_specs=[SM, VM, VM, VM],
        out_specs=(VM, VM, VM),
        compiler_params=params(),
        cost_estimate=pl.CostEstimate(flops=2 * 10**9, bytes_accessed=1 << 20, transcendentals=0),
        name="query",
    )(who, parts, cosine, sine)
    new_a = lax.ppermute(new, "rows", [(s, 2 * (s % 8) + s // 8) for s in range(16)])
    new_b = lax.ppermute(new, "rows", [(s, 2 * (s % 8) + 1 - s // 8) for s in range(16)])
    query = lax.all_to_all(query, "blk", 0, 0, tiled=True)
    partial = pl.pallas_call(
        attend_body,
        out_shape=sds((32, 32, HD), BF),
        in_specs=[SM] + [VM] * 3,
        out_specs=VM,
        compiler_params=params(),
        name="attend",
    )(who, mine, other, query)
    partial = lax.all_to_all(partial, "blk", 0, 0, tiled=True)
    attended = pl.pallas_call(
        combine_body,
        out_shape=sds((32, 16, HD), BF),
        in_specs=[SM] + [VM] * 4,
        out_specs=VM,
        compiler_params=params(),
        name="combine",
    )(who, partial, q_own, new_a, new_b)
    attended = lax.all_to_all(attended, "blk", 0, 0, tiled=True)
    mixed = pl.pallas_call(
        output_body,
        out_shape=sds((128, 256), BF),
        in_specs=[VM, VM],
        out_specs=VM,
        compiler_params=params(),
        name="output",
    )(attended, w_out)
    mixed = lax.all_to_all(mixed.reshape(16, 8, 256), "rows", 0, 0, tiled=True)
    return (hidden_in.astype(F32) + jnp.sum(mixed.astype(F32), axis=0)).astype(BF)


def solution(mesh):
    return jax.shard_map(
        on_device,
        mesh=mesh,
        in_specs=(
            P("rows", "blk"),
            P("blk"),
            P("blk", "rows"),
            P("blk", "rows"),
            P("rows", "blk"),
            P(("blk", "rows"), None),
            P(("blk", "rows"), None),
            P("rows", "blk", None),
            P("rows", "blk", None),
            P(),
            P("rows"),
        ),
        out_specs=P("rows", "blk"),
        check_vma=False,
    )
```

```python
import jax
import jax.numpy as jnp
import numpy as np
from jax import lax
from jax.experimental import pallas as pl
from jax.experimental.pallas import tpu as pltpu
from jax.sharding import PartitionSpec as P

HD = 128
F32 = jnp.float32
BF = jnp.bfloat16
VM = pl.BlockSpec(memory_space=pltpu.VMEM)
SM = pl.BlockSpec(memory_space=pltpu.SMEM)
NT = (((1,), (1,)), ((), ()))
K0, V0, OK0, OV0, X0, END = 0, 64, 128, 160, 192, 208


def params(mib=48):
    return pltpu.CompilerParams(vmem_limit_bytes=mib * 1024 * 1024)


def iota(shape, dim):
    return lax.broadcasted_iota(jnp.int32, shape, dim)


def pack_body(who, lens, hidden, keys_hbm, values_hbm, own_k_hbm, own_v_hbm, out, keys, values, own_k, own_v, sems):
    copies = [
        pltpu.make_async_copy(src, dst, sems.at[i])
        for i, (src, dst) in enumerate(
            ((keys_hbm, keys), (values_hbm, values), (own_k_hbm, own_k), (own_v_hbm, own_v))
        )
    ]
    for copy in copies:
        copy.start()
    b = who[0]
    x = hidden[...].astype(F32)
    x_tile = jnp.concatenate([x[:, :HD], x[:, HD:]], axis=0).astype(BF)
    sub = iota((32, HD), 0)
    slot = 8 * b + sub % 8
    dead = []
    for p in range(2):
        live = jnp.zeros((32, HD), jnp.int32)
        for k in range(4):
            live = jnp.where(sub // 8 == k, lens[4 * p + k], live)
        dead.append(slot >= live)
    for copy in copies:
        copy.wait()
    for p in range(2):
        for h in range(8):
            col = slice(h * HD, (h + 1) * HD)
            d = 2 * h + p
            out[d, K0:V0, :] = keys[64 * p : 64 * p + 64, col]
            out[d, V0:OK0, :] = values[64 * p : 64 * p + 64, col]
            own = own_k[32 * p : 32 * p + 32, col].astype(F32)
            out[d, OK0:OV0, :] = jnp.where(dead[p], jnp.nan, own).astype(BF)
            out[d, OV0:X0, :] = own_v[32 * p : 32 * p + 32, col]
            out[d, X0:END, :] = x_tile


def half_swap(x):
    return pltpu.roll(x, 4, 1)


def project_body(x_ref, gain, wq, wkv, out):
    xr = x_ref[...].astype(F32)
    x = jnp.concatenate(
        [xr[:, :8, :].reshape(128, HD), xr[:, 8:, :].reshape(128, HD)], axis=1
    )
    square = lax.dot_general(
        jnp.ones((8, 2 * HD), F32), x * x, NT,
        precision=lax.Precision.HIGHEST, preferred_element_type=F32,
    )
    high = square.astype(BF).astype(F32)
    sub = iota((16, 8, HD), 1)
    squares = jnp.where(sub == 4, high[None], jnp.where(sub == 5, (square - high)[None], 0.0))
    xg = (x * gain[...].astype(F32)).astype(BF)
    q = jnp.dot(xg, wq[...], preferred_element_type=F32)
    kv = jnp.dot(xg, wkv[...], preferred_element_type=F32).reshape(16, 8, HD)
    heads = [q[:, HD * h : HD * h + HD].reshape(16, 8, HD) for h in range(4)]
    low = sub < 4
    for p in range(2):
        tiles = []
        for u in range(2):
            first, second = heads[2 * u], heads[2 * u + 1]
            if p == 0:
                tiles.append(jnp.where(low, first, half_swap(second)))
            else:
                tiles.append(jnp.where(low, half_swap(first), second))
        tiles.append(jnp.where(low, kv if p == 0 else half_swap(kv), squares))
        tiles.append(jnp.zeros((16, 8, HD), F32))
        chunks = jnp.concatenate(tiles, axis=1).astype(BF)
        for j in range(16):
            out[2 * j + p, :, :] = chunks[j]


def rotate(u, cosine, sine):
    return u * cosine + pltpu.roll(u, HD // 2, 1) * sine


def query_body(who, parts, cosine, sine, q_out, q_own, kv_out):
    total = jnp.sum(parts[...].astype(F32), axis=0)
    square = total[20:21, :] + total[21:22, :]
    inv = lax.rsqrt(square / 8192.0 + 1e-05)
    lane, sub = iota((24, HD), 1), iota((24, HD), 0)
    col = jnp.sum(jnp.where(lane == 4 * who[0] + sub % 4, inv, 0.0), axis=1, keepdims=True)
    raw = (total[0:24, :] * col).astype(BF).astype(F32)
    turned = rotate(raw, cosine[...], sine[...])
    query = turned[0:16, :].astype(BF)
    q_own[...] = query
    for i in range(q_out.shape[0]):
        q_out[i, :, :] = query
    kv_out[...] = jnp.concatenate([turned[16:24, :], jnp.zeros((8, HD), F32)], axis=0).astype(BF)


def attend_body(who, mine, other, q_ref, out):
    r = who[1]
    scale = HD ** (-0.5)
    sources = (mine, other)
    halves = (lax.rem(r, 2), 1 - lax.rem(r, 2))
    keys = [s[:, K0:V0, :].reshape(1024, HD) for s in sources]
    values = [s[:, V0:OK0, :].reshape(1024, HD) for s in sources]
    row_q = iota((128, HD), 0)
    row_q = 4 * (row_q // 16) + row_q % 4
    lane = iota((128, HD), 1)
    lane_s = iota((128, HD), 1)
    for t in range(4):
        q = q_ref[8 * t : 8 * t + 8].reshape(128, HD)
        scores, vals = [], []
        for k, v in zip(keys, values):
            scores.append(lax.dot_general(q, k, NT, preferred_element_type=F32) * scale)
            vals.append(v)
        for s, half in zip(sources, halves):
            own_k = s[4 * t : 4 * t + 4, OK0:OV0, :].reshape(128, HD)
            own_v = s[4 * t : 4 * t + 4, OV0:X0, :].reshape(128, HD)
            row_k = 8 * (lane // 32) + 4 * half + (lane % 32) // 8
            sc = lax.dot_general(q, own_k, NT, preferred_element_type=F32) * scale
            good = (row_k == row_q) & (sc == sc)
            scores.append(jnp.where(good, sc, -jnp.inf))
            vals.append(own_v)
        peak = jnp.max(scores[0], axis=1, keepdims=True)
        for sc in scores[1:]:
            peak = jnp.maximum(peak, jnp.max(sc, axis=1, keepdims=True))
        high = peak.astype(BF).astype(F32)
        low = (peak - high).astype(BF).astype(F32)
        shift = high + low
        mass = jnp.zeros((128, 1), F32)
        acc = jnp.zeros((128, HD), F32)
        for sc, v in zip(scores, vals):
            w = jnp.exp(sc - shift)
            mass = mass + jnp.sum(w, axis=1, keepdims=True)
            acc = acc + jnp.dot(w.astype(BF), v, preferred_element_type=F32)
        mass_high = mass.astype(BF).astype(F32)
        stats = jnp.where(
            lane_s == 0, high,
            jnp.where(lane_s == 1, low, jnp.where(lane_s == 2, mass_high, jnp.where(lane_s == 3, mass - mass_high, 0.0))),
        )
        out[8 * t : 8 * t + 8, 0:16, :] = acc.astype(BF).reshape(8, 16, HD)
        out[8 * t : 8 * t + 8, 16:32, :] = stats.astype(BF).reshape(8, 16, HD)


def combine_body(who, parts, q_own, new_a, new_b, out):
    even = lax.rem(who[1], 2) == 0
    first, second = new_a[...].astype(F32), new_b[...].astype(F32)
    new_k = jnp.concatenate([jnp.where(even, first, second)[0:4, :]] * 4, axis=0)
    new_v = jnp.concatenate([jnp.where(even, second, first)[0:4, :]] * 4, axis=0)
    new = jnp.sum(q_own[...].astype(F32) * new_k, axis=1, keepdims=True) * HD ** (-0.5)
    acc = parts[:, 0:16, :].astype(F32)
    stats = parts[:, 16:32, :].astype(F32)
    peak = stats[:, :, 0:1] + stats[:, :, 1:2]
    mass = stats[:, :, 2:3] + stats[:, :, 3:4]
    top = jnp.maximum(jnp.max(peak, axis=0), new)
    shrink = jnp.exp(peak - top[None])
    new_w = jnp.exp(new - top)
    whole = jnp.sum(mass * shrink, axis=0) + new_w
    summed = jnp.sum(acc * shrink, axis=0) + new_w * new_v
    attended = (summed / whole).astype(BF)
    for i in range(out.shape[0]):
        out[i, :, :] = attended


def output_body(att, w, out):
    tiles = att[...].astype(F32).reshape(16, 2, 2, 8, HD)
    low = iota((16, 8, HD), 1) < 4
    total = jnp.zeros(out.shape, F32)
    for h in range(4):
        first, second = tiles[:, 0, h // 2], tiles[:, 1, h // 2]
        if h % 2 == 0:
            rows = jnp.where(low, first, half_swap(second))
        else:
            rows = jnp.where(low, half_swap(first), second)
        total = total + jnp.dot(
            rows.reshape(128, HD).astype(BF), w[HD * h : HD * h + HD, :], preferred_element_type=F32
        )
    out[...] = total.astype(BF)


def rotary_tables(positions):
    freq = (1.0 / 500000.0 ** (np.arange(0, HD, 2) / HD)).astype(np.float32)
    angles = positions.astype(F32)[:, None] * jnp.asarray(np.concatenate([freq, freq]), F32)[None, :]
    sign = np.concatenate([-np.ones(HD // 2), np.ones(HD // 2)]).astype(np.float32)
    return jnp.cos(angles), jnp.sin(angles) * jnp.asarray(sign)[None, :]


def on_device(
    hidden_in,
    norm_gain,
    w_query,
    w_keyval,
    w_out,
    prefix_keys,
    prefix_values,
    own_keys,
    own_values,
    positions,
    lengths,
):
    b, r = lax.axis_index("blk"), lax.axis_index("rows")
    who = jnp.stack([b, r]).astype(jnp.int32)
    sds = jax.ShapeDtypeStruct
    packed = pl.pallas_call(
        pack_body,
        out_shape=sds((16, END, HD), BF),
        in_specs=[SM, SM, VM] + [pl.BlockSpec(memory_space=pltpu.HBM)] * 4,
        out_specs=VM,
        scratch_shapes=[
            pltpu.VMEM((128, 1024), BF),
            pltpu.VMEM((128, 1024), BF),
            pltpu.VMEM((64, 1024), BF),
            pltpu.VMEM((64, 1024), BF),
            pltpu.SemaphoreType.DMA((4,)),
        ],
        name="pack",
    )(who, lengths, hidden_in, prefix_keys, prefix_values, own_keys.reshape(64, 1024), own_values.reshape(64, 1024))
    mine = lax.all_to_all(packed, "rows", 0, 0, tiled=True)
    parts = pl.pallas_call(
        project_body,
        grid=(1,),
        out_shape=sds((32, 32, HD), BF),
        in_specs=[
            pl.BlockSpec((16, END - X0, HD), lambda i: (0, X0 // 16, 0)),
            pl.BlockSpec((1, 256), lambda i: (0, 0)),
            pl.BlockSpec((256, 512), lambda i: (0, 0)),
            pl.BlockSpec((256, HD), lambda i: (0, 0)),
        ],
        out_specs=pl.BlockSpec((32, 32, HD), lambda i: (0, 0, 0)),
        compiler_params=params(),
        name="project",
    )(mine, norm_gain.reshape(1, 256), w_query, w_keyval)
    positions, parts = lax.optimization_barrier((positions, parts))
    parts = lax.all_to_all(parts, "blk", 0, 0, tiled=True)
    places = lax.dynamic_slice_in_dim(positions, 4 * b, 4, 0)
    still = jnp.zeros_like(places)
    places = jnp.concatenate([places] * 4 + [jnp.where(r < 8, places, still), still])
    cosine, sine = rotary_tables(places)
    mine, cosine = lax.optimization_barrier((mine, cosine))
    other = lax.ppermute(mine, "rows", [(i, i ^ 1) for i in range(16)])
    query, q_own, new = pl.pallas_call(
        query_body,
        out_shape=(sds((32, 16, HD), BF), sds((16, HD), BF), sds((16, HD), BF)),
        in_specs=[SM, VM, VM, VM],
        out_specs=(VM, VM, VM),
        compiler_params=params(),
        cost_estimate=pl.CostEstimate(flops=2 * 10**9, bytes_accessed=1 << 20, transcendentals=0),
        name="query",
    )(who, parts, cosine, sine)
    new_a = lax.ppermute(new, "rows", [(s, 2 * (s % 8) + s // 8) for s in range(16)])
    query = lax.all_to_all(query, "blk", 0, 0, tiled=True)
    query, new_a = lax.optimization_barrier((query, new_a))
    partial = pl.pallas_call(
        attend_body,
        out_shape=sds((32, 32, HD), BF),
        in_specs=[SM] + [VM] * 3,
        out_specs=VM,
        compiler_params=params(),
        name="attend",
    )(who, mine, other, query)
    partial, new = lax.optimization_barrier((partial, new))
    new_b = lax.ppermute(new, "rows", [(s, 2 * (s % 8) + 1 - s // 8) for s in range(16)])
    partial = lax.all_to_all(partial, "blk", 0, 0, tiled=True)
    attended = pl.pallas_call(
        combine_body,
        out_shape=sds((32, 16, HD), BF),
        in_specs=[SM] + [VM] * 4,
        out_specs=VM,
        compiler_params=params(),
        name="combine",
    )(who, partial, q_own, new_a, new_b)
    attended = lax.all_to_all(attended, "blk", 0, 0, tiled=True)
    mixed = pl.pallas_call(
        output_body,
        out_shape=sds((128, 256), BF),
        in_specs=[VM, VM],
        out_specs=VM,
        compiler_params=params(),
        name="output",
    )(attended, w_out)
    mixed = lax.all_to_all(mixed.reshape(16, 8, 256), "rows", 0, 0, tiled=True)
    return (hidden_in.astype(F32) + jnp.sum(mixed.astype(F32), axis=0)).astype(BF)


def solution(mesh):
    return jax.shard_map(
        on_device,
        mesh=mesh,
        in_specs=(
            P("rows", "blk"),
            P("blk"),
            P("blk", "rows"),
            P("blk", "rows"),
            P("rows", "blk"),
            P(("blk", "rows"), None),
            P(("blk", "rows"), None),
            P("rows", "blk", None),
            P("rows", "blk", None),
            P(),
            P("rows"),
        ),
        out_specs=P("rows", "blk"),
        check_vma=False,
    )
```

```python
import jax
import jax.numpy as jnp
import numpy as np
from jax import lax
from jax.experimental import pallas as pl
from jax.experimental.pallas import tpu as pltpu
from jax.sharding import PartitionSpec as P

HD = 128
F32 = jnp.float32
BF = jnp.bfloat16
VM = pl.BlockSpec(memory_space=pltpu.VMEM)
SM = pl.BlockSpec(memory_space=pltpu.SMEM)
NT = (((1,), (1,)), ((), ()))
K0, V0, OK0, OV0, X0, END = 0, 64, 128, 160, 192, 208


def params(mib=48):
    return pltpu.CompilerParams(vmem_limit_bytes=mib * 1024 * 1024)


def iota(shape, dim):
    return lax.broadcasted_iota(jnp.int32, shape, dim)


def pack_body(who, lens, hidden, keys_hbm, values_hbm, own_k_hbm, own_v_hbm, out, keys, values, own_k, own_v, sems):
    copies = [
        pltpu.make_async_copy(src, dst, sems.at[i])
        for i, (src, dst) in enumerate(
            ((keys_hbm, keys), (values_hbm, values), (own_k_hbm, own_k), (own_v_hbm, own_v))
        )
    ]
    for copy in copies:
        copy.start()
    b = who[0]
    x = hidden[...].astype(F32)
    x_tile = jnp.concatenate([x[:, :HD], x[:, HD:]], axis=0).astype(BF)
    sub = iota((32, HD), 0)
    slot = 8 * b + sub % 8
    dead = []
    for p in range(2):
        live = jnp.zeros((32, HD), jnp.int32)
        for k in range(4):
            live = jnp.where(sub // 8 == k, lens[4 * p + k], live)
        dead.append(slot >= live)
    for copy in copies:
        copy.wait()
    for p in range(2):
        for h in range(8):
            col = slice(h * HD, (h + 1) * HD)
            d = 2 * h + p
            out[d, K0:V0, :] = keys[64 * p : 64 * p + 64, col]
            out[d, V0:OK0, :] = values[64 * p : 64 * p + 64, col]
            own = own_k[32 * p : 32 * p + 32, col].astype(F32)
            out[d, OK0:OV0, :] = jnp.where(dead[p], jnp.nan, own).astype(BF)
            out[d, OV0:X0, :] = own_v[32 * p : 32 * p + 32, col]
            out[d, X0:END, :] = x_tile


def half_swap(x):
    return pltpu.roll(x, 4, 1)


def half_swap(x):
    return pltpu.roll(x, 4, 1)


def gathered_rows(x_ref):
    xr = x_ref[...].astype(F32)
    return jnp.concatenate(
        [xr[:, :8, :].reshape(128, HD), xr[:, 8:, :].reshape(128, HD)], axis=1
    )


def by_rows_of_four(blocks, p):
    blocks = [block.reshape(16, 8, HD) for block in blocks]
    low = iota((16, 8, HD), 1) < 4
    tiles = []
    for u in range(2):
        first, second = blocks[2 * u], blocks[2 * u + 1]
        if p == 0:
            tiles.append(jnp.where(low, first, half_swap(second)))
        else:
            tiles.append(jnp.where(low, half_swap(first), second))
    return tiles


def project_body(x_ref, gain, wq, out):
    x = gathered_rows(x_ref)
    square = lax.dot_general(
        jnp.ones((8, 2 * HD), F32), x * x, NT,
        precision=lax.Precision.HIGHEST, preferred_element_type=F32,
    )
    high = square.astype(BF).astype(F32)
    sub = iota((8, HD), 0)
    squares = jnp.where(sub == 0, high, jnp.where(sub == 1, square - high, 0.0))
    squares = jnp.concatenate([squares, jnp.zeros((8, HD), F32)], axis=0).astype(BF)
    xg = (x * gain[...].astype(F32)).astype(BF)
    q = jnp.dot(xg, wq[...], preferred_element_type=F32)
    heads = [q[:, HD * h : HD * h + HD] for h in range(4)]
    for p in range(2):
        chunks = jnp.concatenate(by_rows_of_four(heads, p), axis=1).astype(BF)
        for j in range(16):
            out[2 * j + p, 0:16, :] = chunks[j]
            out[2 * j + p, 16:32, :] = squares


def keyval_body(who, x_ref, gain, wa, wb, out):
    xg = (gathered_rows(x_ref) * gain[...].astype(F32)).astype(BF)
    even = lax.rem(who[1], 2) == 0
    first = jnp.dot(xg, wa[...], preferred_element_type=F32)
    second = jnp.dot(xg, wb[...], preferred_element_type=F32)
    key = jnp.where(even, first, second)
    value = jnp.where(even, second, first)
    lane = iota((128, HD), 1)
    blocks = []
    for j in range(4):
        moved_k = pltpu.roll(key, (32 - 32 * j) % HD, 1)
        moved_v = pltpu.roll(value, (64 - 32 * j) % HD, 1)
        block = jnp.where(lane < 64, moved_k, moved_v)
        blocks.append(jnp.where((lane >= 32) & (lane < 96), block, 0.0))
    for p in range(2):
        chunks = jnp.concatenate(by_rows_of_four(blocks, p), axis=1).astype(BF)
        for j in range(16):
            out[2 * j + p, :, :] = chunks[j]


def rotate(u, cosine, sine):
    return u * cosine + pltpu.roll(u, HD // 2, 1) * sine


def query_body(who, parts, cosine, sine, q_out, q_own, scale_out):
    total = jnp.sum(parts[...].astype(F32), axis=0)
    square = total[16:17, :] + total[17:18, :]
    inv = lax.rsqrt(square / 8192.0 + 1e-05)
    lane, sub = iota((16, HD), 1), iota((16, HD), 0)
    col = jnp.sum(jnp.where(lane == 4 * who[0] + sub % 4, inv, 0.0), axis=1, keepdims=True)
    scale_out[...] = jnp.broadcast_to(col, (16, HD))
    raw = (total[0:16, :] * col).astype(BF).astype(F32)
    query = rotate(raw, cosine[...], sine[...]).astype(BF)
    q_own[...] = query
    for i in range(q_out.shape[0]):
        q_out[i, :, :] = query


def attend_body(who, mine, other, q_ref, kv_part, out):
    r = who[1]
    scale = HD ** (-0.5)
    sources = (mine, other)
    halves = (lax.rem(r, 2), 1 - lax.rem(r, 2))
    keys = [s[:, K0:V0, :].reshape(1024, HD) for s in sources]
    values = [s[:, V0:OK0, :].reshape(1024, HD) for s in sources]
    row_q = iota((128, HD), 0)
    row_q = 4 * (row_q // 16) + row_q % 4
    lane = iota((128, HD), 1)
    lane_s = iota((128, HD), 1)
    for t in range(4):
        q = q_ref[8 * t : 8 * t + 8].reshape(128, HD)
        scores, vals = [], []
        for k, v in zip(keys, values):
            scores.append(lax.dot_general(q, k, NT, preferred_element_type=F32) * scale)
            vals.append(v)
        for s, half in zip(sources, halves):
            own_k = s[4 * t : 4 * t + 4, OK0:OV0, :].reshape(128, HD)
            own_v = s[4 * t : 4 * t + 4, OV0:X0, :].reshape(128, HD)
            row_k = 8 * (lane // 32) + 4 * half + (lane % 32) // 8
            sc = lax.dot_general(q, own_k, NT, preferred_element_type=F32) * scale
            good = (row_k == row_q) & (sc == sc)
            scores.append(jnp.where(good, sc, -jnp.inf))
            vals.append(own_v)
        peak = jnp.max(scores[0], axis=1, keepdims=True)
        for sc in scores[1:]:
            peak = jnp.maximum(peak, jnp.max(sc, axis=1, keepdims=True))
        high = peak.astype(BF).astype(F32)
        low = (peak - high).astype(BF).astype(F32)
        shift = high + low
        mass = jnp.zeros((128, 1), F32)
        acc = jnp.zeros((128, HD), F32)
        for sc, v in zip(scores, vals):
            w = jnp.exp(sc - shift)
            mass = mass + jnp.sum(w, axis=1, keepdims=True)
            acc = acc + jnp.dot(w.astype(BF), v, preferred_element_type=F32)
        mass_high = mass.astype(BF).astype(F32)
        stats = jnp.where(
            lane_s == 0, high,
            jnp.where(lane_s == 1, low, jnp.where(lane_s == 2, mass_high, jnp.where(lane_s == 3, mass - mass_high, 0.0))),
        )
        out[8 * t : 8 * t + 8, 0:16, :] = acc.astype(BF).reshape(8, 16, HD)
        rest = kv_part[8 * t : 8 * t + 8].reshape(128, HD).astype(F32)
        stats = jnp.where(lane_s < 32, stats, rest)
        out[8 * t : 8 * t + 8, 16:32, :] = stats.astype(BF).reshape(8, 16, HD)


def to_every_head(total, start):
    lane, sub = iota((16, HD), 1), iota((16, HD), 0)
    whole = jnp.zeros((16, HD), F32)
    for j in range(4):
        block = jnp.where(sub // 4 == j, total, 0.0)
        block = block + pltpu.roll(block, 8, 0)
        block = block + pltpu.roll(block, 4, 0)
        block = pltpu.roll(block, (32 * j - start) % HD, 1)
        whole = jnp.where(lane // 32 == j, block, whole)
    return whole


def combine_body(parts, q_own, scale, cosine, sine, out):
    stats = parts[:, 16:32, :].astype(F32)
    total = jnp.sum(stats, axis=0)
    new_k = (to_every_head(total, 32) * scale[...]).astype(BF).astype(F32)
    new_k = rotate(new_k, cosine[...], sine[...]).astype(BF).astype(F32)
    new_v = (to_every_head(total, 64) * scale[...]).astype(BF).astype(F32)
    new = jnp.sum(q_own[...].astype(F32) * new_k, axis=1, keepdims=True) * HD ** (-0.5)
    acc = parts[:, 0:16, :].astype(F32)
    peak = stats[:, :, 0:1] + stats[:, :, 1:2]
    mass = stats[:, :, 2:3] + stats[:, :, 3:4]
    top = jnp.maximum(jnp.max(peak, axis=0), new)
    shrink = jnp.exp(peak - top[None])
    new_w = jnp.exp(new - top)
    whole = jnp.sum(mass * shrink, axis=0) + new_w
    summed = jnp.sum(acc * shrink, axis=0) + new_w * new_v
    attended = (summed / whole).astype(BF)
    for i in range(out.shape[0]):
        out[i, :, :] = attended


def output_body(att, w, out):
    tiles = att[...].astype(F32).reshape(16, 2, 2, 8, HD)
    low = iota((16, 8, HD), 1) < 4
    total = jnp.zeros(out.shape, F32)
    for h in range(4):
        first, second = tiles[:, 0, h // 2], tiles[:, 1, h // 2]
        if h % 2 == 0:
            rows = jnp.where(low, first, half_swap(second))
        else:
            rows = jnp.where(low, half_swap(first), second)
        total = total + jnp.dot(
            rows.reshape(128, HD).astype(BF), w[HD * h : HD * h + HD, :], preferred_element_type=F32
        )
    out[...] = total.astype(BF)


def rotary_tables(positions):
    freq = (1.0 / 500000.0 ** (np.arange(0, HD, 2) / HD)).astype(np.float32)
    angles = positions.astype(F32)[:, None] * jnp.asarray(np.concatenate([freq, freq]), F32)[None, :]
    sign = np.concatenate([-np.ones(HD // 2), np.ones(HD // 2)]).astype(np.float32)
    return jnp.cos(angles), jnp.sin(angles) * jnp.asarray(sign)[None, :]


def on_device(
    hidden_in,
    norm_gain,
    w_query,
    w_keyval,
    w_out,
    prefix_keys,
    prefix_values,
    own_keys,
    own_values,
    positions,
    lengths,
):
    b, r = lax.axis_index("blk"), lax.axis_index("rows")
    who = jnp.stack([b, r]).astype(jnp.int32)
    sds = jax.ShapeDtypeStruct
    first_w = lax.ppermute(w_keyval, "rows", [(s, 2 * (s % 8) + s // 8) for s in range(16)])
    second_w = lax.ppermute(w_keyval, "rows", [(s, 2 * (s % 8) + 1 - s // 8) for s in range(16)])
    packed = pl.pallas_call(
        pack_body,
        out_shape=sds((16, END, HD), BF),
        in_specs=[SM, SM, VM] + [pl.BlockSpec(memory_space=pltpu.HBM)] * 4,
        out_specs=VM,
        scratch_shapes=[
            pltpu.VMEM((128, 1024), BF),
            pltpu.VMEM((128, 1024), BF),
            pltpu.VMEM((64, 1024), BF),
            pltpu.VMEM((64, 1024), BF),
            pltpu.SemaphoreType.DMA((4,)),
        ],
        name="pack",
    )(who, lengths, hidden_in, prefix_keys, prefix_values, own_keys.reshape(64, 1024), own_values.reshape(64, 1024))
    mine = lax.all_to_all(packed, "rows", 0, 0, tiled=True)
    gain = norm_gain.reshape(1, 256)
    x_spec = pl.BlockSpec((16, END - X0, HD), lambda i: (0, X0 // 16, 0))
    gain_spec = pl.BlockSpec((1, 256), lambda i: (0, 0))
    parts = pl.pallas_call(
        project_body,
        grid=(1,),
        out_shape=sds((32, 32, HD), BF),
        in_specs=[x_spec, gain_spec, pl.BlockSpec((256, 512), lambda i: (0, 0))],
        out_specs=pl.BlockSpec((32, 32, HD), lambda i: (0, 0, 0)),
        compiler_params=params(),
        name="project",
    )(mine, gain, w_query)
    positions, parts = lax.optimization_barrier((positions, parts))
    parts = lax.all_to_all(parts, "blk", 0, 0, tiled=True)
    cosine, sine = rotary_tables(jnp.concatenate([lax.dynamic_slice_in_dim(positions, 4 * b, 4, 0)] * 4))
    mine, cosine, first_w, second_w = lax.optimization_barrier((mine, cosine, first_w, second_w))
    other = lax.ppermute(mine, "rows", [(i, i ^ 1) for i in range(16)])
    kv_part = pl.pallas_call(
        keyval_body,
        grid=(1,),
        out_shape=sds((32, 16, HD), BF),
        in_specs=[SM, x_spec, gain_spec] + [pl.BlockSpec((256, HD), lambda i: (0, 0))] * 2,
        out_specs=pl.BlockSpec((32, 16, HD), lambda i: (0, 0, 0)),
        compiler_params=params(),
        name="keyval",
    )(who, mine, gain, first_w, second_w)
    query, q_own, row_scale = pl.pallas_call(
        query_body,
        out_shape=(sds((32, 16, HD), BF), sds((16, HD), BF), sds((16, HD), F32)),
        in_specs=[SM, VM, VM, VM],
        out_specs=(VM, VM, VM),
        compiler_params=params(),
        cost_estimate=pl.CostEstimate(flops=2 * 10**9, bytes_accessed=1 << 20, transcendentals=0),
        name="query",
    )(who, parts, cosine, sine)
    query = lax.all_to_all(query, "blk", 0, 0, tiled=True)
    partial = pl.pallas_call(
        attend_body,
        out_shape=sds((32, 32, HD), BF),
        in_specs=[SM] + [VM] * 4,
        out_specs=VM,
        compiler_params=params(),
        name="attend",
    )(who, mine, other, query, kv_part)
    partial = lax.all_to_all(partial, "blk", 0, 0, tiled=True)
    attended = pl.pallas_call(
        combine_body,
        out_shape=sds((32, 16, HD), BF),
        in_specs=[VM] * 5,
        out_specs=VM,
        compiler_params=params(),
        name="combine",
    )(partial, q_own, row_scale, cosine, sine)
    attended = lax.all_to_all(attended, "blk", 0, 0, tiled=True)
    mixed = pl.pallas_call(
        output_body,
        out_shape=sds((128, 256), BF),
        in_specs=[VM, VM],
        out_specs=VM,
        compiler_params=params(),
        name="output",
    )(attended, w_out)
    mixed = lax.all_to_all(mixed.reshape(16, 8, 256), "rows", 0, 0, tiled=True)
    return (hidden_in.astype(F32) + jnp.sum(mixed.astype(F32), axis=0)).astype(BF)


def solution(mesh):
    return jax.shard_map(
        on_device,
        mesh=mesh,
        in_specs=(
            P("rows", "blk"),
            P("blk"),
            P("blk", "rows"),
            P("blk", "rows"),
            P("rows", "blk"),
            P(("blk", "rows"), None),
            P(("blk", "rows"), None),
            P("rows", "blk", None),
            P("rows", "blk", None),
            P(),
            P("rows"),
        ),
        out_specs=P("rows", "blk"),
        check_vma=False,
    )
```

```python
import jax
import jax.numpy as jnp
import numpy as np
from jax import lax
from jax.experimental import pallas as pl
from jax.experimental.pallas import tpu as pltpu
from jax.sharding import PartitionSpec as P

HD = 128
LOG2E = float(np.log2(np.e))
F32 = jnp.float32
BF = jnp.bfloat16
VM = pl.BlockSpec(memory_space=pltpu.VMEM)
SM = pl.BlockSpec(memory_space=pltpu.SMEM)
NT = (((1,), (1,)), ((), ()))
K0, V0, OK0, OV0, X0, END = 0, 64, 128, 160, 192, 208


def params(mib=48):
    return pltpu.CompilerParams(vmem_limit_bytes=mib * 1024 * 1024)


def iota(shape, dim):
    return lax.broadcasted_iota(jnp.int32, shape, dim)


def pack_body(lens, hidden, keys_hbm, values_hbm, own_k_hbm, own_v_hbm, out, keys, values, own_k, own_v, packed, sems):
    inward = [
        pltpu.make_async_copy(src, dst, sems.at[i])
        for i, (src, dst) in enumerate(
            ((own_k_hbm, own_k), (keys_hbm, keys), (values_hbm, values), (own_v_hbm, own_v))
        )
    ]
    for copy in inward:
        copy.start()
    outward = [
        pltpu.make_async_copy(packed.at[:, first:last, :], out.at[:, first:last, :], sems.at[4 + i])
        for i, (first, last) in enumerate(((OK0, OV0), (K0, V0), (V0, OK0), (OV0, END)))
    ]
    b = lax.axis_index("blk")
    x = hidden[...].astype(F32)
    x_tile = jnp.concatenate([x[:, :HD], x[:, HD:]], axis=0).astype(BF)
    sub = iota((32, HD), 0)
    slot = 8 * b + sub % 8
    dead = []
    for p in range(2):
        live = jnp.zeros((32, HD), jnp.int32)
        for k in range(4):
            live = jnp.where(sub // 8 == k, lens[4 * p + k], live)
        dead.append(slot >= live)
    for step in range(4):
        inward[step].wait()
        for p in range(2):
            for h in range(8):
                col = slice(h * HD, (h + 1) * HD)
                d = 2 * h + p
                if step == 0:
                    own = own_k[32 * p : 32 * p + 32, col].astype(F32)
                    packed[d, OK0:OV0, :] = jnp.where(dead[p], jnp.nan, own).astype(BF)
                elif step == 1:
                    packed[d, K0:V0, :] = keys[64 * p : 64 * p + 64, col]
                elif step == 2:
                    packed[d, V0:OK0, :] = values[64 * p : 64 * p + 64, col]
                else:
                    packed[d, OV0:X0, :] = own_v[32 * p : 32 * p + 32, col]
                    packed[d, X0:END, :] = x_tile
        outward[step].start()
    for copy in outward:
        copy.wait()


def half_swap(x):
    return pltpu.roll(x, 4, 1)


def half_swap(x):
    return pltpu.roll(x, 4, 1)


def gathered_rows(x_ref):
    xr = x_ref[...].astype(F32)
    return jnp.concatenate(
        [xr[:, :8, :].reshape(128, HD), xr[:, 8:, :].reshape(128, HD)], axis=1
    )


def by_rows_of_four(blocks, p):
    blocks = [block.reshape(16, 8, HD) for block in blocks]
    low = iota((16, 8, HD), 1) < 4
    tiles = []
    for u in range(2):
        first, second = blocks[2 * u], blocks[2 * u + 1]
        if p == 0:
            tiles.append(jnp.where(low, first, half_swap(second)))
        else:
            tiles.append(jnp.where(low, half_swap(first), second))
    return tiles


def project_body(x_ref, gain, wq, out):
    x = gathered_rows(x_ref)
    square = lax.dot_general(
        jnp.ones((8, 2 * HD), F32), x * x, NT,
        precision=lax.Precision.HIGHEST, preferred_element_type=F32,
    )
    high = square.astype(BF).astype(F32)
    sub = iota((8, HD), 0)
    squares = jnp.where(sub == 0, high, jnp.where(sub == 1, square - high, 0.0))
    squares = jnp.broadcast_to(squares[None], (16, 8, HD))
    xg = (x * gain[...].astype(F32)).astype(BF)
    q = jnp.dot(xg, wq[...], preferred_element_type=F32)
    heads = [q[:, HD * h : HD * h + HD] for h in range(4)]
    for p in range(2):
        chunks = jnp.concatenate(by_rows_of_four(heads, p) + [squares], axis=1).astype(BF)
        for j in range(16):
            out[2 * j + p, :, :] = chunks[j]


def keyval_body(who, x_ref, gain, wa, wb, out):
    xg = (gathered_rows(x_ref) * gain[...].astype(F32)).astype(BF)
    even = lax.rem(who[1], 2) == 0
    first = jnp.dot(xg, wa[...], preferred_element_type=F32)
    second = jnp.dot(xg, wb[...], preferred_element_type=F32)
    key = jnp.where(even, first, second)
    value = jnp.where(even, second, first)
    lane = iota((128, HD), 1)
    blocks = []
    for j in range(4):
        moved_k = pltpu.roll(key, (32 - 32 * j) % HD, 1)
        moved_v = pltpu.roll(value, (64 - 32 * j) % HD, 1)
        block = jnp.where(lane < 64, moved_k, moved_v)
        blocks.append(jnp.where((lane >= 32) & (lane < 96), block, 0.0))
    for p in range(2):
        chunks = jnp.concatenate(by_rows_of_four(blocks, p), axis=1).astype(BF)
        for j in range(16):
            out[2 * j + p, :, :] = chunks[j]


def rotate(u, cosine, sine):
    return u * cosine + pltpu.roll(u, HD // 2, 1) * sine


def query_body(who, parts, cosine, sine, q_out, q_own, scale_out):
    total = jnp.sum(parts[...].astype(F32), axis=0)
    square = total[16:17, :] + total[17:18, :]
    inv = lax.rsqrt(square / 8192.0 + 1e-05)
    lane, sub = iota((16, HD), 1), iota((16, HD), 0)
    col = jnp.sum(jnp.where(lane == 4 * who[0] + sub % 4, inv, 0.0), axis=1, keepdims=True)
    scale_out[...] = jnp.broadcast_to(col, (16, HD))
    raw = (total[0:16, :] * col).astype(BF).astype(F32)
    query = rotate(raw, cosine[...], sine[...]).astype(BF)
    q_own[...] = query
    for i in range(q_out.shape[0]):
        q_out[i, :, :] = query


def attend_body(who, mine, other, q_ref, kv_part, out):
    r = who[1]
    scale = HD ** (-0.5) * LOG2E
    sources = (mine, other)
    halves = (lax.rem(r, 2), 1 - lax.rem(r, 2))
    keys = [s[:, K0:V0, :].reshape(1024, HD) for s in sources]
    values = [s[:, V0:OK0, :].reshape(1024, HD) for s in sources]
    row_q = iota((128, HD), 0)
    row_q = 4 * (row_q // 16) + row_q % 4
    lane = iota((128, HD), 1)
    lane_s = iota((128, HD), 1)
    for t in range(4):
        q = q_ref[8 * t : 8 * t + 8].reshape(128, HD)
        scores, vals = [], []
        for k, v in zip(keys, values):
            scores.append(lax.dot_general(q, k, NT, preferred_element_type=F32))
            vals.append(v)
        for s, half in zip(sources, halves):
            own_k = s[4 * t : 4 * t + 4, OK0:OV0, :].reshape(128, HD)
            own_v = s[4 * t : 4 * t + 4, OV0:X0, :].reshape(128, HD)
            row_k = 8 * (lane // 32) + 4 * half + (lane % 32) // 8
            sc = lax.dot_general(q, own_k, NT, preferred_element_type=F32)
            good = (row_k == row_q) & (sc == sc)
            scores.append(jnp.where(good, sc, -jnp.inf))
            vals.append(own_v)
        peak = jnp.max(scores[0], axis=1, keepdims=True)
        for sc in scores[1:]:
            peak = jnp.maximum(peak, jnp.max(sc, axis=1, keepdims=True))
        peak = peak * scale
        high = peak.astype(BF).astype(F32)
        low = (peak - high).astype(BF).astype(F32)
        shift = high + low
        mass = jnp.zeros((128, 1), F32)
        acc = jnp.zeros((128, HD), F32)
        for sc, v in zip(scores, vals):
            w = jnp.exp2(sc * scale - shift)
            mass = mass + jnp.sum(w, axis=1, keepdims=True)
            acc = acc + jnp.dot(w.astype(BF), v, preferred_element_type=F32)
        mass_high = mass.astype(BF).astype(F32)
        stats = jnp.where(
            lane_s == 0, high,
            jnp.where(lane_s == 1, low, jnp.where(lane_s == 2, mass_high, jnp.where(lane_s == 3, mass - mass_high, 0.0))),
        )
        out[8 * t : 8 * t + 8, 0:16, :] = acc.astype(BF).reshape(8, 16, HD)
        rest = kv_part[8 * t : 8 * t + 8].reshape(128, HD).astype(F32)
        stats = jnp.where(lane_s < 32, stats, rest)
        out[8 * t : 8 * t + 8, 16:32, :] = stats.astype(BF).reshape(8, 16, HD)


def to_every_head(total, start):
    lane, sub = iota((16, HD), 1), iota((16, HD), 0)
    whole = jnp.zeros((16, HD), F32)
    for j in range(4):
        block = jnp.where(sub // 4 == j, total, 0.0)
        block = block + pltpu.roll(block, 8, 0)
        block = block + pltpu.roll(block, 4, 0)
        block = pltpu.roll(block, (32 * j - start) % HD, 1)
        whole = jnp.where(lane // 32 == j, block, whole)
    return whole


def combine_body(parts, q_own, scale, cosine, sine, out):
    stats = parts[:, 16:32, :].astype(F32)
    total = jnp.sum(stats, axis=0)
    new_k = (to_every_head(total, 32) * scale[...]).astype(BF).astype(F32)
    new_k = rotate(new_k, cosine[...], sine[...]).astype(BF).astype(F32)
    new_v = (to_every_head(total, 64) * scale[...]).astype(BF).astype(F32)
    new = jnp.sum(q_own[...].astype(F32) * new_k, axis=1, keepdims=True) * (HD ** (-0.5) * LOG2E)
    acc = parts[:, 0:16, :].astype(F32)
    peak = stats[:, :, 0:1] + stats[:, :, 1:2]
    mass = stats[:, :, 2:3] + stats[:, :, 3:4]
    top = jnp.maximum(jnp.max(peak, axis=0), new)
    shrink = jnp.exp2(peak - top[None])
    new_w = jnp.exp2(new - top)
    whole = jnp.sum(mass * shrink, axis=0) + new_w
    summed = jnp.sum(acc * shrink, axis=0) + new_w * new_v
    attended = (summed / whole).astype(BF)
    for i in range(out.shape[0]):
        out[i, :, :] = attended


def output_body(att, w, hidden, out, kept):
    kept[...] = hidden[...].astype(F32)
    tiles = att[...].astype(F32).reshape(16, 2, 2, 8, HD)
    low = iota((16, 8, HD), 1) < 4
    total = jnp.zeros(out.shape, F32)
    for h in range(4):
        first, second = tiles[:, 0, h // 2], tiles[:, 1, h // 2]
        if h % 2 == 0:
            rows = jnp.where(low, first, half_swap(second))
        else:
            rows = jnp.where(low, half_swap(first), second)
        total = total + jnp.dot(
            rows.reshape(128, HD).astype(BF), w[HD * h : HD * h + HD, :], preferred_element_type=F32
        )
    out[...] = total.astype(BF)


def rotary_tables(positions):
    freq = (1.0 / 500000.0 ** (np.arange(0, HD, 2) / HD)).astype(np.float32)
    angles = positions.astype(F32)[:, None] * jnp.asarray(np.concatenate([freq, freq]), F32)[None, :]
    sign = np.concatenate([-np.ones(HD // 2), np.ones(HD // 2)]).astype(np.float32)
    return jnp.cos(angles), jnp.sin(angles) * jnp.asarray(sign)[None, :]


def on_device(
    hidden_in,
    norm_gain,
    w_query,
    w_keyval,
    w_out,
    prefix_keys,
    prefix_values,
    own_keys,
    own_values,
    positions,
    lengths,
):
    b, r = lax.axis_index("blk"), lax.axis_index("rows")
    who = jnp.stack([b, r]).astype(jnp.int32)
    sds = jax.ShapeDtypeStruct
    first_w = lax.ppermute(w_keyval, "rows", [(s, 2 * (s % 8) + s // 8) for s in range(16)])
    second_w = lax.ppermute(w_keyval, "rows", [(s, 2 * (s % 8) + 1 - s // 8) for s in range(16)])
    packed = pl.pallas_call(
        pack_body,
        out_shape=sds((16, END, HD), BF),
        in_specs=[SM, VM] + [pl.BlockSpec(memory_space=pltpu.HBM)] * 4,
        out_specs=pl.BlockSpec(memory_space=pltpu.HBM),
        scratch_shapes=[
            pltpu.VMEM((128, 1024), BF),
            pltpu.VMEM((128, 1024), BF),
            pltpu.VMEM((64, 1024), BF),
            pltpu.VMEM((64, 1024), BF),
            pltpu.VMEM((16, END, HD), BF),
            pltpu.SemaphoreType.DMA((8,)),
        ],
        name="pack",
    )(lengths, hidden_in, prefix_keys, prefix_values, own_keys.reshape(64, 1024), own_values.reshape(64, 1024))
    mine = lax.all_to_all(packed, "rows", 0, 0, tiled=True)
    gain = norm_gain.reshape(1, 256)
    x_spec = pl.BlockSpec((16, END - X0, HD), lambda i: (0, X0 // 16, 0))
    gain_spec = pl.BlockSpec((1, 256), lambda i: (0, 0))
    parts = pl.pallas_call(
        project_body,
        grid=(1,),
        out_shape=sds((32, 24, HD), BF),
        in_specs=[x_spec, gain_spec, pl.BlockSpec((256, 512), lambda i: (0, 0))],
        out_specs=pl.BlockSpec((32, 24, HD), lambda i: (0, 0, 0)),
        compiler_params=params(),
        name="project",
    )(mine, gain, w_query)
    positions, parts = lax.optimization_barrier((positions, parts))
    parts = lax.all_to_all(parts, "blk", 0, 0, tiled=True)
    cosine, sine = rotary_tables(jnp.concatenate([lax.dynamic_slice_in_dim(positions, 4 * b, 4, 0)] * 4))
    mine, cosine, first_w, second_w = lax.optimization_barrier((mine, cosine, first_w, second_w))
    other = lax.ppermute(mine, "rows", [(i, i ^ 1) for i in range(16)])
    kv_part = pl.pallas_call(
        keyval_body,
        grid=(1,),
        out_shape=sds((32, 16, HD), BF),
        in_specs=[SM, x_spec, gain_spec] + [pl.BlockSpec((256, HD), lambda i: (0, 0))] * 2,
        out_specs=pl.BlockSpec((32, 16, HD), lambda i: (0, 0, 0)),
        compiler_params=params(),
        cost_estimate=pl.CostEstimate(flops=10**9, bytes_accessed=1 << 18, transcendentals=0),
        name="keyval",
    )(who, mine, gain, first_w, second_w)
    cosine, kv_part = lax.optimization_barrier((cosine, kv_part))
    query, q_own, row_scale = pl.pallas_call(
        query_body,
        out_shape=(sds((32, 16, HD), BF), sds((16, HD), BF), sds((16, HD), F32)),
        in_specs=[SM, VM, VM, VM],
        out_specs=(VM, VM, VM),
        compiler_params=params(),
        cost_estimate=pl.CostEstimate(flops=2 * 10**10, bytes_accessed=1 << 20, transcendentals=0),
        name="query",
    )(who, parts, cosine, sine)
    query = lax.all_to_all(query, "blk", 0, 0, tiled=True)
    partial = pl.pallas_call(
        attend_body,
        out_shape=sds((32, 32, HD), BF),
        in_specs=[SM] + [VM] * 4,
        out_specs=VM,
        compiler_params=params(),
        name="attend",
    )(who, mine, other, query, kv_part)
    partial = lax.all_to_all(partial, "blk", 0, 0, tiled=True)
    attended = pl.pallas_call(
        combine_body,
        out_shape=sds((32, 16, HD), BF),
        in_specs=[VM] * 5,
        out_specs=VM,
        compiler_params=params(),
        name="combine",
    )(partial, q_own, row_scale, cosine, sine)
    attended = lax.all_to_all(attended, "blk", 0, 0, tiled=True)
    mixed, kept = pl.pallas_call(
        output_body,
        out_shape=(sds((128, 256), BF), sds((8, 256), F32)),
        in_specs=[VM] * 3,
        out_specs=(VM, VM),
        compiler_params=params(),
        name="output",
    )(attended, w_out, hidden_in)
    mixed = lax.all_to_all(mixed.reshape(16, 8, 256), "rows", 0, 0, tiled=True)
    return (kept + jnp.sum(mixed.astype(F32), axis=0)).astype(BF)


def solution(mesh):
    return jax.shard_map(
        on_device,
        mesh=mesh,
        in_specs=(
            P("rows", "blk"),
            P("blk"),
            P("blk", "rows"),
            P("blk", "rows"),
            P("rows", "blk"),
            P(("blk", "rows"), None),
            P(("blk", "rows"), None),
            P("rows", "blk", None),
            P("rows", "blk", None),
            P(),
            P("rows"),
        ),
        out_specs=P("rows", "blk"),
        check_vma=False,
    )
```

```python
import jax
import jax.numpy as jnp
import numpy as np
from jax import lax
from jax.experimental import pallas as pl
from jax.experimental.pallas import tpu as pltpu
from jax.sharding import PartitionSpec as P

HD = 128
LOG2E = float(np.log2(np.e))
F32 = jnp.float32
BF = jnp.bfloat16
VM = pl.BlockSpec(memory_space=pltpu.VMEM)
SM = pl.BlockSpec(memory_space=pltpu.SMEM)
NT = (((1,), (1,)), ((), ()))
K0, V0, OK0, OV0, X0, END = 0, 64, 128, 160, 192, 208


def params(mib=48):
    return pltpu.CompilerParams(vmem_limit_bytes=mib * 1024 * 1024)


def iota(shape, dim):
    return lax.broadcasted_iota(jnp.int32, shape, dim)


def pack_body(lens, hidden_hbm, keys_hbm, values_hbm, own_k_hbm, own_v_hbm, out, keys, values, own_k, own_v, packed, rows_x, sems):
    inward = [
        pltpu.make_async_copy(src, dst, sems.at[i])
        for i, (src, dst) in enumerate(
            ((own_k_hbm, own_k), (keys_hbm, keys), (values_hbm, values), (own_v_hbm, own_v), (hidden_hbm, rows_x))
        )
    ]
    for copy in inward:
        copy.start()
    outward = [
        pltpu.make_async_copy(packed.at[:, first:last, :], out.at[:, first:last, :], sems.at[5 + i])
        for i, (first, last) in enumerate(((OK0, OV0), (K0, V0), (V0, OK0), (OV0, END)))
    ]
    b = lax.axis_index("blk")
    sub = iota((32, HD), 0)
    slot = 8 * b + sub % 8
    dead = []
    for p in range(2):
        live = jnp.zeros((32, HD), jnp.int32)
        for k in range(4):
            live = jnp.where(sub // 8 == k, lens[4 * p + k], live)
        dead.append(slot >= live)
    for step in range(4):
        inward[step].wait()
        if step == 3:
            inward[4].wait()
            x = rows_x[...].astype(F32)
            x_tile = jnp.concatenate([x[:, :HD], x[:, HD:]], axis=0).astype(BF)
        for p in range(2):
            for h in range(8):
                col = slice(h * HD, (h + 1) * HD)
                d = 2 * h + p
                if step == 0:
                    own = own_k[32 * p : 32 * p + 32, col].astype(F32)
                    packed[d, OK0:OV0, :] = jnp.where(dead[p], jnp.nan, own).astype(BF)
                elif step == 1:
                    packed[d, K0:V0, :] = keys[64 * p : 64 * p + 64, col]
                elif step == 2:
                    packed[d, V0:OK0, :] = values[64 * p : 64 * p + 64, col]
                else:
                    packed[d, OV0:X0, :] = own_v[32 * p : 32 * p + 32, col]
                    packed[d, X0:END, :] = x_tile
        outward[step].start()
    for copy in outward:
        copy.wait()


def half_swap(x):
    return pltpu.roll(x, 4, 1)


def half_swap(x):
    return pltpu.roll(x, 4, 1)


def gathered_rows(x_ref):
    xr = x_ref[...].astype(F32)
    return jnp.concatenate(
        [xr[:, :8, :].reshape(128, HD), xr[:, 8:, :].reshape(128, HD)], axis=1
    )


def by_rows_of_four(blocks, p):
    blocks = [block.reshape(16, 8, HD) for block in blocks]
    low = iota((16, 8, HD), 1) < 4
    tiles = []
    for u in range(2):
        first, second = blocks[2 * u], blocks[2 * u + 1]
        if p == 0:
            tiles.append(jnp.where(low, first, half_swap(second)))
        else:
            tiles.append(jnp.where(low, half_swap(first), second))
    return tiles


def project_body(x_ref, gain, wq, out):
    x = gathered_rows(x_ref)
    square = lax.dot_general(
        jnp.ones((8, 2 * HD), F32), x * x, NT,
        precision=lax.Precision.HIGHEST, preferred_element_type=F32,
    )
    high = square.astype(BF).astype(F32)
    sub = iota((8, HD), 0)
    squares = jnp.where(sub == 0, high, jnp.where(sub == 1, square - high, 0.0))
    squares = jnp.broadcast_to(squares[None], (16, 8, HD))
    xg = (x * gain[...].astype(F32)).astype(BF)
    q = jnp.dot(xg, wq[...], preferred_element_type=F32)
    heads = [q[:, HD * h : HD * h + HD] for h in range(4)]
    for p in range(2):
        chunks = jnp.concatenate(by_rows_of_four(heads, p) + [squares], axis=1).astype(BF)
        for j in range(16):
            out[2 * j + p, :, :] = chunks[j]


def keyval_body(who, x_ref, gain, wa, wb, out):
    xg = (gathered_rows(x_ref) * gain[...].astype(F32)).astype(BF)
    even = lax.rem(who[1], 2) == 0
    first = jnp.dot(xg, wa[...], preferred_element_type=F32)
    second = jnp.dot(xg, wb[...], preferred_element_type=F32)
    key = jnp.where(even, first, second)
    value = jnp.where(even, second, first)
    lane = iota((128, HD), 1)
    blocks = []
    for j in range(4):
        moved_k = pltpu.roll(key, (32 - 32 * j) % HD, 1)
        moved_v = pltpu.roll(value, (64 - 32 * j) % HD, 1)
        block = jnp.where(lane < 64, moved_k, moved_v)
        blocks.append(jnp.where((lane >= 32) & (lane < 96), block, 0.0))
    for p in range(2):
        chunks = jnp.concatenate(by_rows_of_four(blocks, p), axis=1).astype(BF)
        for j in range(16):
            out[2 * j + p, :, :] = chunks[j]


def rotate(u, cosine, sine):
    return u * cosine + pltpu.roll(u, HD // 2, 1) * sine


def query_body(who, parts, cosine, sine, q_out, q_own, scale_out):
    total = jnp.sum(parts[...].astype(F32), axis=0)
    square = total[16:17, :] + total[17:18, :]
    inv = lax.rsqrt(square / 8192.0 + 1e-05)
    lane, sub = iota((16, HD), 1), iota((16, HD), 0)
    col = jnp.sum(jnp.where(lane == 4 * who[0] + sub % 4, inv, 0.0), axis=1, keepdims=True)
    scale_out[...] = jnp.broadcast_to(col, (16, HD))
    raw = (total[0:16, :] * col).astype(BF).astype(F32)
    query = rotate(raw, cosine[...], sine[...]).astype(BF)
    q_own[...] = query
    for i in range(q_out.shape[0]):
        q_out[i, :, :] = query


def attend_body(who, mine, other, q_ref, kv_part, out):
    r = who[1]
    scale = HD ** (-0.5) * LOG2E
    sources = (mine, other)
    halves = (lax.rem(r, 2), 1 - lax.rem(r, 2))
    rows = 256
    row_q, lane = iota((128, HD), 0), iota((128, HD), 1)
    row_q = 4 * (row_q // 16) + row_q % 4
    lane_s = iota((rows, HD), 1)
    for t in range(512 // rows):
        part = slice(rows // 16 * t, rows // 16 * (t + 1))
        q = q_ref[part].reshape(rows, HD)
        scores, vals = [], []
        for s in sources:
            k = s[:, K0:V0, :].reshape(1024, HD)
            scores.append(lax.dot_general(q, k, NT, preferred_element_type=F32))
            vals.append(s[:, V0:OK0, :].reshape(1024, HD))
        own_scores, own_vals = [], []
        for s, half in zip(sources, halves):
            row_k = 8 * (lane // 32) + 4 * half + (lane % 32) // 8
            blocks, block_vals = [], []
            for u in range(rows // 128):
                first = 4 * (t * (rows // 128) + u)
                k = s[first : first + 4, OK0:OV0, :].reshape(128, HD)
                block_vals.append(s[first : first + 4, OV0:X0, :].reshape(128, HD))
                sc = lax.dot_general(q[128 * u : 128 * u + 128], k, NT, preferred_element_type=F32)
                blocks.append(jnp.where((row_k == row_q) & (sc == sc), sc, -jnp.inf))
            own_scores.append(jnp.concatenate(blocks, axis=0))
            own_vals.append(block_vals)
        peak = jnp.max(scores[0], axis=1, keepdims=True)
        for sc in scores[1:] + own_scores:
            peak = jnp.maximum(peak, jnp.max(sc, axis=1, keepdims=True))
        peak = peak * scale
        high = peak.astype(BF).astype(F32)
        low = (peak - high).astype(BF).astype(F32)
        shift = high + low
        mass = jnp.zeros((rows, 1), F32)
        acc = jnp.zeros((rows, HD), F32)
        for sc, v in zip(scores, vals):
            w = jnp.exp2(sc * scale - shift)
            mass = mass + jnp.sum(w, axis=1, keepdims=True)
            acc = acc + jnp.dot(w.astype(BF), v, preferred_element_type=F32)
        for sc, block_vals in zip(own_scores, own_vals):
            w = jnp.exp2(sc * scale - shift)
            mass = mass + jnp.sum(w, axis=1, keepdims=True)
            w = w.astype(BF)
            acc = acc + jnp.concatenate(
                [
                    jnp.dot(w[128 * u : 128 * u + 128], v, preferred_element_type=F32)
                    for u, v in enumerate(block_vals)
                ],
                axis=0,
            )
        mass_high = mass.astype(BF).astype(F32)
        stats = jnp.where(
            lane_s == 0, high, jnp.where(lane_s == 1, low, jnp.where(lane_s == 2, mass_high, mass - mass_high))
        )
        stats = jnp.where(lane_s < 32, stats, kv_part[part].reshape(rows, HD).astype(F32))
        out[part, 0:16, :] = acc.astype(BF).reshape(rows // 16, 16, HD)
        out[part, 16:32, :] = stats.astype(BF).reshape(rows // 16, 16, HD)


def to_every_head(total, start):
    lane, sub = iota((16, HD), 1), iota((16, HD), 0)
    whole = jnp.zeros((16, HD), F32)
    for j in range(4):
        block = jnp.where(sub // 4 == j, total, 0.0)
        block = block + pltpu.roll(block, 8, 0)
        block = block + pltpu.roll(block, 4, 0)
        block = pltpu.roll(block, (32 * j - start) % HD, 1)
        whole = jnp.where(lane // 32 == j, block, whole)
    return whole


def combine_body(parts, q_own, scale, cosine, sine, out):
    stats = parts[:, 16:32, :].astype(F32)
    total = jnp.sum(stats, axis=0)
    new_k = (to_every_head(total, 32) * scale[...]).astype(BF).astype(F32)
    new_k = rotate(new_k, cosine[...], sine[...]).astype(BF).astype(F32)
    new_v = (to_every_head(total, 64) * scale[...]).astype(BF).astype(F32)
    new = jnp.sum(q_own[...].astype(F32) * new_k, axis=1, keepdims=True) * (HD ** (-0.5) * LOG2E)
    acc = parts[:, 0:16, :].astype(F32)
    peak = stats[:, :, 0:1] + stats[:, :, 1:2]
    mass = stats[:, :, 2:3] + stats[:, :, 3:4]
    top = jnp.maximum(jnp.max(peak, axis=0), new)
    shrink = jnp.exp2(peak - top[None])
    new_w = jnp.exp2(new - top)
    whole = jnp.sum(mass * shrink, axis=0) + new_w
    summed = jnp.sum(acc * shrink, axis=0) + new_w * new_v
    attended = (summed / whole).astype(BF)
    for i in range(out.shape[0]):
        out[i, :, :] = attended


def output_body(att, w, hidden, out, kept):
    kept[...] = hidden[...].astype(F32)
    tiles = att[...].astype(F32).reshape(16, 2, 2, 8, HD)
    low = iota((16, 8, HD), 1) < 4
    total = jnp.zeros(out.shape, F32)
    for h in range(4):
        first, second = tiles[:, 0, h // 2], tiles[:, 1, h // 2]
        if h % 2 == 0:
            rows = jnp.where(low, first, half_swap(second))
        else:
            rows = jnp.where(low, half_swap(first), second)
        total = total + jnp.dot(
            rows.reshape(128, HD).astype(BF), w[HD * h : HD * h + HD, :], preferred_element_type=F32
        )
    out[...] = total.astype(BF)


def rotary_tables(positions):
    freq = (1.0 / 500000.0 ** (np.arange(0, HD, 2) / HD)).astype(np.float32)
    angles = positions.astype(F32)[:, None] * jnp.asarray(np.concatenate([freq, freq]), F32)[None, :]
    sign = np.concatenate([-np.ones(HD // 2), np.ones(HD // 2)]).astype(np.float32)
    return jnp.cos(angles), jnp.sin(angles) * jnp.asarray(sign)[None, :]


def on_device(
    hidden_in,
    norm_gain,
    w_query,
    w_keyval,
    w_out,
    prefix_keys,
    prefix_values,
    own_keys,
    own_values,
    positions,
    lengths,
):
    b, r = lax.axis_index("blk"), lax.axis_index("rows")
    who = jnp.stack([b, r]).astype(jnp.int32)
    sds = jax.ShapeDtypeStruct
    first_w = lax.ppermute(w_keyval, "rows", [(s, 2 * (s % 8) + s // 8) for s in range(16)])
    second_w = lax.ppermute(w_keyval, "rows", [(s, 2 * (s % 8) + 1 - s // 8) for s in range(16)])
    packed = pl.pallas_call(
        pack_body,
        out_shape=sds((16, END, HD), BF),
        in_specs=[SM] + [pl.BlockSpec(memory_space=pltpu.HBM)] * 5,
        out_specs=pl.BlockSpec(memory_space=pltpu.HBM),
        scratch_shapes=[
            pltpu.VMEM((128, 1024), BF),
            pltpu.VMEM((128, 1024), BF),
            pltpu.VMEM((64, 1024), BF),
            pltpu.VMEM((64, 1024), BF),
            pltpu.VMEM((16, END, HD), BF),
            pltpu.VMEM((8, 256), BF),
            pltpu.SemaphoreType.DMA((9,)),
        ],
        name="pack",
    )(lengths, hidden_in, prefix_keys, prefix_values, own_keys.reshape(64, 1024), own_values.reshape(64, 1024))
    mine = lax.all_to_all(packed, "rows", 0, 0, tiled=True)
    gain = norm_gain.reshape(1, 256)
    x_spec = pl.BlockSpec((16, END - X0, HD), lambda i: (0, X0 // 16, 0))
    gain_spec = pl.BlockSpec((1, 256), lambda i: (0, 0))
    parts = pl.pallas_call(
        project_body,
        grid=(1,),
        out_shape=sds((32, 24, HD), BF),
        in_specs=[x_spec, gain_spec, pl.BlockSpec((256, 512), lambda i: (0, 0))],
        out_specs=pl.BlockSpec((32, 24, HD), lambda i: (0, 0, 0)),
        compiler_params=params(),
        name="project",
    )(mine, gain, w_query)
    positions, parts, mine = lax.optimization_barrier((positions, parts, mine))
    parts = lax.all_to_all(parts, "blk", 0, 0, tiled=True)
    cosine, sine = rotary_tables(jnp.concatenate([lax.dynamic_slice_in_dim(positions, 4 * b, 4, 0)] * 4))
    half, first_w, second_w = lax.optimization_barrier((mine[:, :X0, :], first_w, second_w))
    other = lax.ppermute(half, "rows", [(i, i ^ 1) for i in range(16)])
    kv_part = pl.pallas_call(
        keyval_body,
        grid=(1,),
        out_shape=sds((32, 16, HD), BF),
        in_specs=[SM, x_spec, gain_spec] + [pl.BlockSpec((256, HD), lambda i: (0, 0))] * 2,
        out_specs=pl.BlockSpec((32, 16, HD), lambda i: (0, 0, 0)),
        compiler_params=params(),
        cost_estimate=pl.CostEstimate(flops=10**9, bytes_accessed=1 << 18, transcendentals=0),
        name="keyval",
    )(who, mine, gain, first_w, second_w)
    cosine, kv_part = lax.optimization_barrier((cosine, kv_part))
    query, q_own, row_scale = pl.pallas_call(
        query_body,
        out_shape=(sds((32, 16, HD), BF), sds((16, HD), BF), sds((16, HD), F32)),
        in_specs=[SM, VM, VM, VM],
        out_specs=(VM, VM, VM),
        compiler_params=params(),
        cost_estimate=pl.CostEstimate(flops=4*10**9, bytes_accessed=1 << 20, transcendentals=0),
        name="query",
    )(who, parts, cosine, sine)
    query = lax.all_to_all(query, "blk", 0, 0, tiled=True)
    partial = pl.pallas_call(
        attend_body,
        out_shape=sds((32, 32, HD), BF),
        in_specs=[SM] + [VM] * 4,
        out_specs=VM,
        compiler_params=params(),
        name="attend",
    )(who, mine, other, query, kv_part)
    partial = lax.all_to_all(partial, "blk", 0, 0, tiled=True)
    attended = pl.pallas_call(
        combine_body,
        out_shape=sds((32, 16, HD), BF),
        in_specs=[VM] * 5,
        out_specs=VM,
        compiler_params=params(),
        name="combine",
    )(partial, q_own, row_scale, cosine, sine)
    attended = lax.all_to_all(attended, "blk", 0, 0, tiled=True)
    mixed, kept = pl.pallas_call(
        output_body,
        out_shape=(sds((128, 256), BF), sds((8, 256), F32)),
        in_specs=[VM] * 3,
        out_specs=(VM, VM),
        compiler_params=params(),
        name="output",
    )(attended, w_out, hidden_in)
    mixed = lax.all_to_all(mixed.reshape(16, 8, 256), "rows", 0, 0, tiled=True)
    return (kept + jnp.sum(mixed.astype(F32), axis=0)).astype(BF)


def solution(mesh):
    return jax.shard_map(
        on_device,
        mesh=mesh,
        in_specs=(
            P("rows", "blk"),
            P("blk"),
            P("blk", "rows"),
            P("blk", "rows"),
            P("rows", "blk"),
            P(("blk", "rows"), None),
            P(("blk", "rows"), None),
            P("rows", "blk", None),
            P("rows", "blk", None),
            P(),
            P("rows"),
        ),
        out_specs=P("rows", "blk"),
        check_vma=False,
    )
```

```python
import jax
import jax.numpy as jnp
import numpy as np
from jax import lax
from jax.experimental import pallas as pl
from jax.experimental.pallas import tpu as pltpu
from jax.sharding import PartitionSpec as P

HD = 128
LOG2E = float(np.log2(np.e))
F32 = jnp.float32
BF = jnp.bfloat16
VM = pl.BlockSpec(memory_space=pltpu.VMEM)
SM = pl.BlockSpec(memory_space=pltpu.SMEM)
NT = (((1,), (1,)), ((), ()))
K0, V0, OK0, OV0, X0, END = 0, 64, 128, 160, 192, 208


def params(mib=48):
    return pltpu.CompilerParams(vmem_limit_bytes=mib * 1024 * 1024)


def iota(shape, dim):
    return lax.broadcasted_iota(jnp.int32, shape, dim)


def pack_body(lens, hidden_hbm, keys_hbm, values_hbm, own_k_hbm, own_v_hbm, out, keys, values, own_k, own_v, packed, rows_x, sems):
    inward = [
        pltpu.make_async_copy(src, dst, sems.at[i])
        for i, (src, dst) in enumerate(
            ((own_k_hbm, own_k), (keys_hbm, keys), (values_hbm, values), (own_v_hbm, own_v), (hidden_hbm, rows_x))
        )
    ]
    for copy in inward:
        copy.start()
    outward = [
        pltpu.make_async_copy(packed.at[:, first:last, :], out.at[:, first:last, :], sems.at[5 + i])
        for i, (first, last) in enumerate(((OK0, OV0), (K0, V0), (V0, OK0), (OV0, END)))
    ]
    b = lax.axis_index("blk")
    sub = iota((32, HD), 0)
    slot = 8 * b + sub % 8
    dead = []
    for p in range(2):
        live = jnp.zeros((32, HD), jnp.int32)
        for k in range(4):
            live = jnp.where(sub // 8 == k, lens[4 * p + k], live)
        dead.append(slot >= live)
    for step in range(4):
        inward[step].wait()
        if step == 3:
            inward[4].wait()
            x = rows_x[...].astype(F32)
            x_tile = jnp.concatenate([x[:, :HD], x[:, HD:]], axis=0).astype(BF)
        for p in range(2):
            for h in range(8):
                col = slice(h * HD, (h + 1) * HD)
                d = 2 * h + p
                if step == 0:
                    own = own_k[32 * p : 32 * p + 32, col].astype(F32)
                    packed[d, OK0:OV0, :] = jnp.where(dead[p], jnp.nan, own).astype(BF)
                elif step == 1:
                    packed[d, K0:V0, :] = keys[64 * p : 64 * p + 64, col]
                elif step == 2:
                    packed[d, V0:OK0, :] = values[64 * p : 64 * p + 64, col]
                else:
                    packed[d, OV0:X0, :] = own_v[32 * p : 32 * p + 32, col]
                    packed[d, X0:END, :] = x_tile
        outward[step].start()
    for copy in outward:
        copy.wait()


def half_swap(x):
    return pltpu.roll(x, 4, 1)


def half_swap(x):
    return pltpu.roll(x, 4, 1)


def gathered_rows(x_ref):
    xr = x_ref[...].astype(F32)
    return jnp.concatenate(
        [xr[:, :8, :].reshape(128, HD), xr[:, 8:, :].reshape(128, HD)], axis=1
    )


def by_rows_of_four(blocks, p):
    blocks = [block.reshape(16, 8, HD) for block in blocks]
    low = iota((16, 8, HD), 1) < 4
    tiles = []
    for u in range(2):
        first, second = blocks[2 * u], blocks[2 * u + 1]
        if p == 0:
            tiles.append(jnp.where(low, first, half_swap(second)))
        else:
            tiles.append(jnp.where(low, half_swap(first), second))
    return tiles


def project_body(x_ref, gain, wq, out):
    x = gathered_rows(x_ref)
    square = lax.dot_general(
        jnp.ones((8, 2 * HD), F32), x * x, NT,
        precision=lax.Precision.HIGHEST, preferred_element_type=F32,
    )
    high = square.astype(BF).astype(F32)
    sub = iota((8, HD), 0)
    squares = jnp.where(sub == 0, high, jnp.where(sub == 1, square - high, 0.0))
    squares = jnp.broadcast_to(squares[None], (16, 8, HD))
    xg = (x * gain[...].astype(F32)).astype(BF)
    q = jnp.dot(xg, wq[...], preferred_element_type=F32)
    heads = [q[:, HD * h : HD * h + HD] for h in range(4)]
    for p in range(2):
        chunks = jnp.concatenate(by_rows_of_four(heads, p) + [squares], axis=1).astype(BF)
        for j in range(16):
            out[2 * j + p, :, :] = chunks[j]


def keyval_body(who, x_ref, gain, wa, wb, keep, give):
    xg = (gathered_rows(x_ref) * gain[...].astype(F32)).astype(BF)
    first = jnp.dot(xg, wa[...], preferred_element_type=F32)
    second = jnp.dot(xg, wb[...], preferred_element_type=F32)
    same = lax.rem(who[0], 2) == lax.rem(who[1], 2)
    keep[...] = jnp.where(same, first, second)
    give[...] = jnp.where(same, second, first).astype(BF)


def rotate(u, cosine, sine):
    return u * cosine + pltpu.roll(u, HD // 2, 1) * sine


def query_body(who, parts, cosine, sine, q_out, q_own, scale_out):
    total = jnp.sum(parts[...].astype(F32), axis=0)
    square = total[16:17, :] + total[17:18, :]
    inv = lax.rsqrt(square / 8192.0 + 1e-05)
    lane, sub = iota((16, HD), 1), iota((16, HD), 0)
    col = jnp.sum(jnp.where(lane == 4 * who[0] + sub % 4, inv, 0.0), axis=1, keepdims=True)
    scale_out[...] = jnp.broadcast_to(col, (16, HD))
    raw = (total[0:16, :] * col).astype(BF).astype(F32)
    query = rotate(raw, cosine[...], sine[...]).astype(BF)
    q_own[...] = query
    for i in range(q_out.shape[0]):
        q_out[i, :, :] = query


def attend_body(who, mine, other, q_ref, keep, given, out):
    r = who[1]
    scale = HD ** (-0.5) * LOG2E
    sources = (mine, other)
    halves = (lax.rem(r, 2), 1 - lax.rem(r, 2))
    rows = 256
    row_q, lane = iota((128, HD), 0), iota((128, HD), 1)
    row_q = 4 * (row_q // 16) + row_q % 4
    lane_s = iota((rows, HD), 1)
    sub_s = iota((8, HD), 0)
    kv = (keep[...] + given[...].astype(F32)).reshape(16, 8, HD)
    kv_swapped = half_swap(kv)
    for t in range(512 // rows):
        part = slice(rows // 16 * t, rows // 16 * (t + 1))
        q = q_ref[part].reshape(rows, HD)
        scores, vals = [], []
        for s in sources:
            k = s[:, K0:V0, :].reshape(1024, HD)
            scores.append(lax.dot_general(q, k, NT, preferred_element_type=F32))
            vals.append(s[:, V0:OK0, :].reshape(1024, HD))
        own_scores, own_vals = [], []
        for s, half in zip(sources, halves):
            row_k = 8 * (lane // 32) + 4 * half + (lane % 32) // 8
            blocks, block_vals = [], []
            for u in range(rows // 128):
                first = 4 * (t * (rows // 128) + u)
                k = s[first : first + 4, OK0:OV0, :].reshape(128, HD)
                block_vals.append(s[first : first + 4, OV0:X0, :].reshape(128, HD))
                sc = lax.dot_general(q[128 * u : 128 * u + 128], k, NT, preferred_element_type=F32)
                blocks.append(jnp.where((row_k == row_q) & (sc == sc), sc, -jnp.inf))
            own_scores.append(jnp.concatenate(blocks, axis=0))
            own_vals.append(block_vals)
        peak = jnp.max(scores[0], axis=1, keepdims=True)
        for sc in scores[1:] + own_scores:
            peak = jnp.maximum(peak, jnp.max(sc, axis=1, keepdims=True))
        peak = peak * scale
        high = peak.astype(BF).astype(F32)
        low = (peak - high).astype(BF).astype(F32)
        shift = high + low
        mass = jnp.zeros((rows, 1), F32)
        acc = jnp.zeros((rows, HD), F32)
        for sc, v in zip(scores, vals):
            w = jnp.exp2(sc * scale - shift)
            mass = mass + jnp.sum(w, axis=1, keepdims=True)
            acc = acc + jnp.dot(w.astype(BF), v, preferred_element_type=F32)
        for sc, block_vals in zip(own_scores, own_vals):
            w = jnp.exp2(sc * scale - shift)
            mass = mass + jnp.sum(w, axis=1, keepdims=True)
            w = w.astype(BF)
            acc = acc + jnp.concatenate(
                [
                    jnp.dot(w[128 * u : 128 * u + 128], v, preferred_element_type=F32)
                    for u, v in enumerate(block_vals)
                ],
                axis=0,
            )
        mass_high = mass.astype(BF).astype(F32)
        stats = jnp.where(
            lane_s == 0, high, jnp.where(lane_s == 1, low, jnp.where(lane_s == 2, mass_high, mass - mass_high))
        )
        stats = jnp.where(lane_s < 4, stats, 0.0)
        for u in range(rows // 128):
            turned = pltpu.roll(stats[128 * u : 128 * u + 128, :].T[0:8, :], 4, 0)
            for i in range(8):
                chunk = rows // 16 * t + 8 * u + i
                part_kv = kv[chunk // 2] if chunk % 2 == 0 else kv_swapped[chunk // 2]
                rest = jnp.where(sub_s < 4, part_kv, turned)
                whole = jnp.concatenate([acc[128 * u + 16 * i : 128 * u + 16 * i + 16, :], rest], axis=0)
                out[chunk, :, :] = whole.astype(BF)


def twice(tile):
    tile = jnp.where(iota((8, HD), 0) < 4, tile, pltpu.roll(tile, 4, 0))
    return jnp.concatenate([tile, tile], axis=0)


def combine_body(who, parts, q_own, scale, cosine, sine, out):
    rest = parts[:, 16:24, :].astype(F32).reshape(16, 2, 8, HD)
    new_k = (twice(jnp.sum(rest[:, 0], axis=0)) * scale[...]).astype(BF).astype(F32)
    new_k = rotate(new_k, cosine[...], sine[...]).astype(BF).astype(F32)
    new_v = (twice(jnp.sum(rest[:, 1], axis=0)) * scale[...]).astype(BF).astype(F32)
    new = jnp.sum(q_own[...].astype(F32) * new_k, axis=1, keepdims=True) * (HD ** (-0.5) * LOG2E)
    mine = iota((16, HD), 1) == 16 * lax.rem(who[0], 8) + iota((16, HD), 0)
    new = jnp.sum(jnp.where(mine, new, 0.0), axis=0, keepdims=True)
    rest = rest.reshape(32, 8, HD)
    peak = rest[:, 4:5, :] + rest[:, 5:6, :]
    mass = rest[:, 6:7, :] + rest[:, 7:8, :]
    top = jnp.maximum(jnp.max(peak, axis=0), new)
    shrink = jnp.exp2(peak - top[None])
    new_w = jnp.exp2(new - top)
    whole = jnp.sum(mass * shrink, axis=0) + new_w
    share = jnp.sum(jnp.where(mine[None], shrink / whole[None], 0.0), axis=2, keepdims=True)
    new_share = jnp.sum(jnp.where(mine, new_w / whole, 0.0), axis=1, keepdims=True)
    summed = jnp.sum(parts[:, 0:16, :].astype(F32) * share, axis=0) + new_share * new_v
    attended = summed.astype(BF)
    for i in range(out.shape[0]):
        out[i, :, :] = attended


def output_body(att, w, hidden, out, kept):
    kept[...] = hidden[...].astype(F32)
    tiles = att[...].astype(F32).reshape(16, 2, 2, 8, HD)
    low = iota((16, 8, HD), 1) < 4
    total = jnp.zeros(out.shape, F32)
    for h in range(4):
        first, second = tiles[:, 0, h // 2], tiles[:, 1, h // 2]
        if h % 2 == 0:
            rows = jnp.where(low, first, half_swap(second))
        else:
            rows = jnp.where(low, half_swap(first), second)
        total = total + jnp.dot(
            rows.reshape(128, HD).astype(BF), w[HD * h : HD * h + HD, :], preferred_element_type=F32
        )
    out[...] = total.astype(BF)


def rotary_tables(positions):
    freq = (1.0 / 500000.0 ** (np.arange(0, HD, 2) / HD)).astype(np.float32)
    angles = positions.astype(F32)[:, None] * jnp.asarray(np.concatenate([freq, freq]), F32)[None, :]
    sign = np.concatenate([-np.ones(HD // 2), np.ones(HD // 2)]).astype(np.float32)
    return jnp.cos(angles), jnp.sin(angles) * jnp.asarray(sign)[None, :]


def on_device(
    hidden_in,
    norm_gain,
    w_query,
    w_keyval,
    w_out,
    prefix_keys,
    prefix_values,
    own_keys,
    own_values,
    positions,
    lengths,
):
    b, r = lax.axis_index("blk"), lax.axis_index("rows")
    who = jnp.stack([b, r]).astype(jnp.int32)
    sds = jax.ShapeDtypeStruct
    first_w = lax.ppermute(w_keyval, "rows", [(s, 2 * (s % 8) + s // 8) for s in range(16)])
    second_w = lax.ppermute(w_keyval, "rows", [(s, 2 * (s % 8) + 1 - s // 8) for s in range(16)])
    packed = pl.pallas_call(
        pack_body,
        out_shape=sds((16, END, HD), BF),
        in_specs=[SM] + [pl.BlockSpec(memory_space=pltpu.HBM)] * 5,
        out_specs=pl.BlockSpec(memory_space=pltpu.HBM),
        scratch_shapes=[
            pltpu.VMEM((128, 1024), BF),
            pltpu.VMEM((128, 1024), BF),
            pltpu.VMEM((64, 1024), BF),
            pltpu.VMEM((64, 1024), BF),
            pltpu.VMEM((16, END, HD), BF),
            pltpu.VMEM((8, 256), BF),
            pltpu.SemaphoreType.DMA((9,)),
        ],
        name="pack",
    )(lengths, hidden_in, prefix_keys, prefix_values, own_keys.reshape(64, 1024), own_values.reshape(64, 1024))
    mine = lax.all_to_all(packed, "rows", 0, 0, tiled=True)
    gain = norm_gain.reshape(1, 256)
    x_spec = pl.BlockSpec((16, END - X0, HD), lambda i: (0, X0 // 16, 0))
    gain_spec = pl.BlockSpec((1, 256), lambda i: (0, 0))
    parts = pl.pallas_call(
        project_body,
        grid=(1,),
        out_shape=sds((32, 24, HD), BF),
        in_specs=[x_spec, gain_spec, pl.BlockSpec((256, 512), lambda i: (0, 0))],
        out_specs=pl.BlockSpec((32, 24, HD), lambda i: (0, 0, 0)),
        compiler_params=params(),
        name="project",
    )(mine, gain, w_query)
    positions, parts, mine = lax.optimization_barrier((positions, parts, mine))
    parts = lax.all_to_all(parts, "blk", 0, 0, tiled=True)
    cosine, sine = rotary_tables(jnp.concatenate([lax.dynamic_slice_in_dim(positions, 4 * b, 4, 0)] * 4))
    half, first_w, second_w = lax.optimization_barrier((mine[:, :X0, :], first_w, second_w))
    other = lax.ppermute(half, "rows", [(i, i ^ 1) for i in range(16)])
    keep, give = pl.pallas_call(
        keyval_body,
        grid=(1,),
        out_shape=(sds((128, HD), F32), sds((128, HD), BF)),
        in_specs=[SM, x_spec, gain_spec] + [pl.BlockSpec((256, HD), lambda i: (0, 0))] * 2,
        out_specs=[pl.BlockSpec((128, HD), lambda i: (0, 0))] * 2,
        compiler_params=params(),
        cost_estimate=pl.CostEstimate(flops=10**9, bytes_accessed=1 << 18, transcendentals=0),
        name="keyval",
    )(who, mine, gain, first_w, second_w)
    given = lax.ppermute(give, "blk", [(i, i ^ 1) for i in range(32)])
    cosine, given = lax.optimization_barrier((cosine, given))
    query, q_own, row_scale = pl.pallas_call(
        query_body,
        out_shape=(sds((32, 16, HD), BF), sds((16, HD), BF), sds((16, HD), F32)),
        in_specs=[SM, VM, VM, VM],
        out_specs=(VM, VM, VM),
        compiler_params=params(),
        cost_estimate=pl.CostEstimate(flops=3*10**9, bytes_accessed=1 << 20, transcendentals=0),
        name="query",
    )(who, parts, cosine, sine)
    query = lax.all_to_all(query, "blk", 0, 0, tiled=True)
    partial = pl.pallas_call(
        attend_body,
        out_shape=sds((32, 24, HD), BF),
        in_specs=[SM] + [VM] * 5,
        out_specs=VM,
        compiler_params=params(),
        name="attend",
    )(who, mine, other, query, keep, given)
    partial = lax.all_to_all(partial, "blk", 0, 0, tiled=True)
    attended = pl.pallas_call(
        combine_body,
        out_shape=sds((32, 16, HD), BF),
        in_specs=[SM] + [VM] * 5,
        out_specs=VM,
        compiler_params=params(),
        name="combine",
    )(who, partial, q_own, row_scale, cosine, sine)
    attended = lax.all_to_all(attended, "blk", 0, 0, tiled=True)
    mixed, kept = pl.pallas_call(
        output_body,
        out_shape=(sds((128, 256), BF), sds((8, 256), F32)),
        in_specs=[VM] * 3,
        out_specs=(VM, VM),
        compiler_params=params(),
        name="output",
    )(attended, w_out, hidden_in)
    mixed = lax.all_to_all(mixed.reshape(16, 8, 256), "rows", 0, 0, tiled=True)
    return (kept + jnp.sum(mixed.astype(F32), axis=0)).astype(BF)


def solution(mesh):
    return jax.shard_map(
        on_device,
        mesh=mesh,
        in_specs=(
            P("rows", "blk"),
            P("blk"),
            P("blk", "rows"),
            P("blk", "rows"),
            P("rows", "blk"),
            P(("blk", "rows"), None),
            P(("blk", "rows"), None),
            P("rows", "blk", None),
            P("rows", "blk", None),
            P(),
            P("rows"),
        ),
        out_specs=P("rows", "blk"),
        check_vma=False,
    )
```

```python
import jax
import jax.numpy as jnp
import numpy as np
from jax import lax
from jax.experimental import pallas as pl
from jax.experimental.pallas import tpu as pltpu
from jax.sharding import PartitionSpec as P

HD = 128
LOG2E = float(np.log2(np.e))
F32 = jnp.float32
BF = jnp.bfloat16
VM = pl.BlockSpec(memory_space=pltpu.VMEM)
SM = pl.BlockSpec(memory_space=pltpu.SMEM)
NT = (((1,), (1,)), ((), ()))
K0, V0, OK0, OV0, X0, END = 0, 64, 128, 160, 192, 208


def params(mib=48):
    return pltpu.CompilerParams(vmem_limit_bytes=mib * 1024 * 1024)


def iota(shape, dim):
    return lax.broadcasted_iota(jnp.int32, shape, dim)


def pack_body(lens, hidden_hbm, keys_hbm, values_hbm, own_k_hbm, own_v_hbm, out, keys, values, own_k, own_v, packed, rows_x, sems):
    inward = [
        pltpu.make_async_copy(src, dst, sems.at[i])
        for i, (src, dst) in enumerate(
            ((own_k_hbm, own_k), (keys_hbm, keys), (values_hbm, values), (own_v_hbm, own_v), (hidden_hbm, rows_x))
        )
    ]
    for copy in inward:
        copy.start()
    outward = [
        pltpu.make_async_copy(packed.at[:, first:last, :], out.at[:, first:last, :], sems.at[5 + i])
        for i, (first, last) in enumerate(((OK0, OV0), (K0, V0), (V0, OK0), (OV0, END)))
    ]
    b = lax.axis_index("blk")
    sub = iota((32, HD), 0)
    slot = 8 * b + sub % 8
    dead = []
    for p in range(2):
        live = jnp.zeros((32, HD), jnp.int32)
        for k in range(4):
            live = jnp.where(sub // 8 == k, lens[4 * p + k], live)
        dead.append(slot >= live)
    for step in range(4):
        inward[step].wait()
        if step == 3:
            inward[4].wait()
            x = rows_x[...].astype(F32)
            x_tile = jnp.concatenate([x[:, :HD], x[:, HD:]], axis=0).astype(BF)
        for p in range(2):
            for h in range(8):
                col = slice(h * HD, (h + 1) * HD)
                d = 2 * h + p
                if step == 0:
                    own = own_k[32 * p : 32 * p + 32, col].astype(F32)
                    packed[d, OK0:OV0, :] = jnp.where(dead[p], jnp.nan, own).astype(BF)
                elif step == 1:
                    packed[d, K0:V0, :] = keys[64 * p : 64 * p + 64, col]
                elif step == 2:
                    packed[d, V0:OK0, :] = values[64 * p : 64 * p + 64, col]
                else:
                    packed[d, OV0:X0, :] = own_v[32 * p : 32 * p + 32, col]
                    packed[d, X0:END, :] = x_tile
        outward[step].start()
    for copy in outward:
        copy.wait()


def half_swap(x):
    return pltpu.roll(x, 4, 1)


def half_swap(x):
    return pltpu.roll(x, 4, 1)


def gathered_rows(x_ref):
    xr = x_ref[...].astype(F32)
    return jnp.concatenate(
        [xr[:, :8, :].reshape(128, HD), xr[:, 8:, :].reshape(128, HD)], axis=1
    )


def by_rows_of_four(blocks, p):
    blocks = [block.reshape(16, 8, HD) for block in blocks]
    low = iota((16, 8, HD), 1) < 4
    tiles = []
    for u in range(2):
        first, second = blocks[2 * u], blocks[2 * u + 1]
        if p == 0:
            tiles.append(jnp.where(low, first, half_swap(second)))
        else:
            tiles.append(jnp.where(low, half_swap(first), second))
    return tiles


def project_body(x_ref, gain, wq, out):
    x = gathered_rows(x_ref)
    square = lax.dot_general(
        jnp.ones((8, 2 * HD), F32), x * x, NT,
        precision=lax.Precision.HIGHEST, preferred_element_type=F32,
    )
    high = square.astype(BF).astype(F32)
    sub = iota((8, HD), 0)
    squares = jnp.where(sub == 0, high, jnp.where(sub == 1, square - high, 0.0))
    squares = jnp.broadcast_to(squares[None], (16, 8, HD))
    xg = (x * gain[...].astype(F32)).astype(BF)
    q = jnp.dot(xg, wq[...], preferred_element_type=F32)
    heads = [q[:, HD * h : HD * h + HD] for h in range(4)]
    for p in range(2):
        chunks = jnp.concatenate(by_rows_of_four(heads, p) + [squares], axis=1).astype(BF)
        for j in range(16):
            out[2 * j + p, :, :] = chunks[j]


def keyval_body(who, x_ref, gain, wa, wb, keep, give):
    xg = (gathered_rows(x_ref) * gain[...].astype(F32)).astype(BF)
    first = jnp.dot(xg, wa[...], preferred_element_type=F32)
    second = jnp.dot(xg, wb[...], preferred_element_type=F32)
    same = lax.rem(who[0], 2) == lax.rem(who[1], 2)
    keep[...] = jnp.where(same, first, second)
    give[...] = jnp.where(same, second, first).astype(BF)


def rotate(u, cosine, sine):
    return u * cosine + pltpu.roll(u, HD // 2, 1) * sine


def query_body(who, parts, cosine, sine, q_out, q_own, scale_out):
    total = jnp.sum(parts[...].astype(F32), axis=0)
    square = total[16:17, :] + total[17:18, :]
    inv = lax.rsqrt(square / 8192.0 + 1e-05)
    lane, sub = iota((16, HD), 1), iota((16, HD), 0)
    col = jnp.sum(jnp.where(lane == 4 * who[0] + sub % 4, inv, 0.0), axis=1, keepdims=True)
    scale_out[...] = jnp.broadcast_to(col, (16, HD))
    raw = (total[0:16, :] * col).astype(BF).astype(F32)
    query = rotate(raw, cosine[...], sine[...]).astype(BF)
    q_own[...] = query
    for i in range(q_out.shape[0]):
        q_out[i, :, :] = query


def attend_body(who, mine, other, q_ref, keep, given, out):
    r = who[1]
    scale = HD ** (-0.5) * LOG2E
    sources = (mine, other)
    halves = (lax.rem(r, 2), 1 - lax.rem(r, 2))
    rows = 256
    row_q, lane = iota((128, HD), 0), iota((128, HD), 1)
    row_q = 4 * (row_q // 16) + row_q % 4
    lane_s = iota((rows, HD), 1)
    sub_s = iota((8, HD), 0)
    kv = (keep[...] + given[...].astype(F32)).reshape(16, 8, HD)
    kv_swapped = half_swap(kv)
    for t in range(512 // rows):
        part = slice(rows // 16 * t, rows // 16 * (t + 1))
        q = q_ref[part].reshape(rows, HD)
        scores, vals = [], []
        for s in sources:
            k = s[:, K0:V0, :].reshape(1024, HD)
            scores.append(lax.dot_general(q, k, NT, preferred_element_type=F32))
            vals.append(s[:, V0:OK0, :].reshape(1024, HD))
        own_scores, own_vals = [], []
        for s, half in zip(sources, halves):
            row_k = 8 * (lane // 32) + 4 * half + (lane % 32) // 8
            blocks, block_vals = [], []
            for u in range(rows // 128):
                first = 4 * (t * (rows // 128) + u)
                k = s[first : first + 4, OK0:OV0, :].reshape(128, HD)
                block_vals.append(s[first : first + 4, OV0:X0, :].reshape(128, HD))
                sc = lax.dot_general(q[128 * u : 128 * u + 128], k, NT, preferred_element_type=F32)
                blocks.append(jnp.where((row_k == row_q) & (sc == sc), sc, -jnp.inf))
            own_scores.append(jnp.concatenate(blocks, axis=0))
            own_vals.append(block_vals)
        peak = jnp.max(scores[0], axis=1, keepdims=True)
        for sc in scores[1:] + own_scores:
            peak = jnp.maximum(peak, jnp.max(sc, axis=1, keepdims=True))
        peak = peak * scale
        high = peak.astype(BF).astype(F32)
        low = (peak - high).astype(BF).astype(F32)
        shift = high + low
        mass = jnp.zeros((rows, 1), F32)
        acc = jnp.zeros((rows, HD), F32)
        for sc, v in zip(scores, vals):
            w = jnp.exp2(sc * scale - shift)
            mass = mass + jnp.sum(w, axis=1, keepdims=True)
            acc = acc + jnp.dot(w.astype(BF), v, preferred_element_type=F32)
        for sc, block_vals in zip(own_scores, own_vals):
            w = jnp.exp2(sc * scale - shift)
            mass = mass + jnp.sum(w, axis=1, keepdims=True)
            w = w.astype(BF)
            acc = acc + jnp.concatenate(
                [
                    jnp.dot(w[128 * u : 128 * u + 128], v, preferred_element_type=F32)
                    for u, v in enumerate(block_vals)
                ],
                axis=0,
            )
        mass_high = mass.astype(BF).astype(F32)
        stats = jnp.where(
            lane_s == 0, high, jnp.where(lane_s == 1, low, jnp.where(lane_s == 2, mass_high, mass - mass_high))
        )
        stats = jnp.where(lane_s < 4, stats, 0.0)
        for u in range(rows // 128):
            turned = pltpu.roll(stats[128 * u : 128 * u + 128, :].T[0:8, :], 4, 0)
            for i in range(8):
                chunk = rows // 16 * t + 8 * u + i
                part_kv = kv[chunk // 2] if chunk % 2 == 0 else kv_swapped[chunk // 2]
                rest = jnp.where(sub_s < 4, part_kv, turned)
                whole = jnp.concatenate([acc[128 * u + 16 * i : 128 * u + 16 * i + 16, :], rest], axis=0)
                out[chunk, :, :] = whole.astype(BF)


def twice(tile):
    tile = jnp.where(iota((8, HD), 0) < 4, tile, pltpu.roll(tile, 4, 0))
    return jnp.concatenate([tile, tile], axis=0)


def combine_body(who, parts, q_own, scale, cosine, sine, out):
    rest = parts[:, 16:24, :].astype(F32).reshape(16, 2, 8, HD)
    new_k = (twice(jnp.sum(rest[:, 0], axis=0)) * scale[...]).astype(BF).astype(F32)
    new_k = rotate(new_k, cosine[...], sine[...]).astype(BF).astype(F32)
    new_v = (twice(jnp.sum(rest[:, 1], axis=0)) * scale[...]).astype(BF).astype(F32)
    new = jnp.sum(q_own[...].astype(F32) * new_k, axis=1, keepdims=True) * (HD ** (-0.5) * LOG2E)
    mine = iota((16, HD), 1) == 16 * lax.rem(who[0], 8) + iota((16, HD), 0)
    new = jnp.sum(jnp.where(mine, new, 0.0), axis=0, keepdims=True)
    rest = rest.reshape(32, 8, HD)
    peak = rest[:, 4:5, :] + rest[:, 5:6, :]
    mass = rest[:, 6:7, :] + rest[:, 7:8, :]
    top = jnp.maximum(jnp.max(peak, axis=0), new)
    shrink = jnp.exp2(peak - top[None])
    new_w = jnp.exp2(new - top)
    whole = jnp.sum(mass * shrink, axis=0) + new_w
    share = jnp.sum(jnp.where(mine[None], shrink / whole[None], 0.0), axis=2, keepdims=True)
    new_share = jnp.sum(jnp.where(mine, new_w / whole, 0.0), axis=1, keepdims=True)
    summed = jnp.sum(parts[:, 0:16, :].astype(F32) * share, axis=0) + new_share * new_v
    attended = summed.astype(BF)
    for i in range(out.shape[0]):
        out[i, :, :] = attended


def output_body(att, w, hidden, out, kept):
    kept[...] = hidden[...].astype(F32)
    tiles = att[...].astype(F32).reshape(16, 2, 2, 8, HD)
    low = iota((16, 8, HD), 1) < 4
    total = jnp.zeros(out.shape, F32)
    for h in range(4):
        first, second = tiles[:, 0, h // 2], tiles[:, 1, h // 2]
        if h % 2 == 0:
            rows = jnp.where(low, first, half_swap(second))
        else:
            rows = jnp.where(low, half_swap(first), second)
        total = total + jnp.dot(
            rows.reshape(128, HD).astype(BF), w[HD * h : HD * h + HD, :], preferred_element_type=F32
        )
    out[...] = total.astype(BF)


def rotary_tables(positions):
    freq = (1.0 / 500000.0 ** (np.arange(0, HD, 2) / HD)).astype(np.float32)
    angles = positions.astype(F32)[:, None] * jnp.asarray(np.concatenate([freq, freq]), F32)[None, :]
    sign = np.concatenate([-np.ones(HD // 2), np.ones(HD // 2)]).astype(np.float32)
    return jnp.cos(angles), jnp.sin(angles) * jnp.asarray(sign)[None, :]


def on_device(
    hidden_in,
    norm_gain,
    w_query,
    w_keyval,
    w_out,
    prefix_keys,
    prefix_values,
    own_keys,
    own_values,
    positions,
    lengths,
):
    b, r = lax.axis_index("blk"), lax.axis_index("rows")
    who = jnp.stack([b, r]).astype(jnp.int32)
    sds = jax.ShapeDtypeStruct
    first_w = lax.ppermute(w_keyval, "rows", [(s, 2 * (s % 8) + s // 8) for s in range(16)])
    second_w = lax.ppermute(w_keyval, "rows", [(s, 2 * (s % 8) + 1 - s // 8) for s in range(16)])
    packed = pl.pallas_call(
        pack_body,
        out_shape=sds((16, END, HD), BF),
        in_specs=[SM] + [pl.BlockSpec(memory_space=pltpu.HBM)] * 5,
        out_specs=pl.BlockSpec(memory_space=pltpu.HBM),
        scratch_shapes=[
            pltpu.VMEM((128, 1024), BF),
            pltpu.VMEM((128, 1024), BF),
            pltpu.VMEM((64, 1024), BF),
            pltpu.VMEM((64, 1024), BF),
            pltpu.VMEM((16, END, HD), BF),
            pltpu.VMEM((8, 256), BF),
            pltpu.SemaphoreType.DMA((9,)),
        ],
        name="pack",
    )(lengths, hidden_in, prefix_keys, prefix_values, own_keys.reshape(64, 1024), own_values.reshape(64, 1024))
    mine = lax.all_to_all(packed, "rows", 0, 0, tiled=True)
    gain = norm_gain.reshape(1, 256)
    x_spec = pl.BlockSpec((16, END - X0, HD), lambda i: (0, X0 // 16, 0))
    gain_spec = pl.BlockSpec((1, 256), lambda i: (0, 0))
    parts = pl.pallas_call(
        project_body,
        grid=(1,),
        out_shape=sds((32, 24, HD), BF),
        in_specs=[x_spec, gain_spec, pl.BlockSpec((256, 512), lambda i: (0, 0))],
        out_specs=pl.BlockSpec((32, 24, HD), lambda i: (0, 0, 0)),
        compiler_params=params(),
        name="project",
    )(mine, gain, w_query)
    positions, parts, mine = lax.optimization_barrier((positions, parts, mine))
    parts = lax.all_to_all(parts, "blk", 0, 0, tiled=True)
    cosine, sine = rotary_tables(jnp.concatenate([lax.dynamic_slice_in_dim(positions, 4 * b, 4, 0)] * 4))
    half, first_w, second_w = lax.optimization_barrier((mine[:, :X0, :], first_w, second_w))
    other = lax.ppermute(half, "rows", [(i, i ^ 1) for i in range(16)])
    keep, give = pl.pallas_call(
        keyval_body,
        grid=(1,),
        out_shape=(sds((128, HD), F32), sds((128, HD), BF)),
        in_specs=[SM, x_spec, gain_spec] + [pl.BlockSpec((256, HD), lambda i: (0, 0))] * 2,
        out_specs=[pl.BlockSpec((128, HD), lambda i: (0, 0))] * 2,
        compiler_params=params(),
        cost_estimate=pl.CostEstimate(flops=10**9, bytes_accessed=1 << 18, transcendentals=0),
        name="keyval",
    )(who, mine, gain, first_w, second_w)
    given = lax.ppermute(give, "blk", [(i, i ^ 1) for i in range(32)])
    query, q_own, row_scale = pl.pallas_call(
        query_body,
        out_shape=(sds((32, 16, HD), BF), sds((16, HD), BF), sds((16, HD), F32)),
        in_specs=[SM, VM, VM, VM],
        out_specs=(VM, VM, VM),
        compiler_params=params(),
        cost_estimate=pl.CostEstimate(flops=3*10**9, bytes_accessed=1 << 20, transcendentals=0),
        name="query",
    )(who, parts, cosine, sine)
    query = lax.all_to_all(query, "blk", 0, 0, tiled=True)
    partial = pl.pallas_call(
        attend_body,
        out_shape=sds((32, 24, HD), BF),
        in_specs=[SM] + [VM] * 5,
        out_specs=VM,
        compiler_params=params(),
        name="attend",
    )(who, mine, other, query, keep, given)
    partial = lax.all_to_all(partial, "blk", 0, 0, tiled=True)
    attended = pl.pallas_call(
        combine_body,
        out_shape=sds((32, 16, HD), BF),
        in_specs=[SM] + [VM] * 5,
        out_specs=VM,
        compiler_params=params(),
        name="combine",
    )(who, partial, q_own, row_scale, cosine, sine)
    attended = lax.all_to_all(attended, "blk", 0, 0, tiled=True)
    mixed, kept = pl.pallas_call(
        output_body,
        out_shape=(sds((128, 256), BF), sds((8, 256), F32)),
        in_specs=[VM] * 3,
        out_specs=(VM, VM),
        compiler_params=params(),
        name="output",
    )(attended, w_out, hidden_in)
    mixed = lax.all_to_all(mixed.reshape(16, 8, 256), "rows", 0, 0, tiled=True)
    return (kept + jnp.sum(mixed.astype(F32), axis=0)).astype(BF)


def solution(mesh):
    return jax.shard_map(
        on_device,
        mesh=mesh,
        in_specs=(
            P("rows", "blk"),
            P("blk"),
            P("blk", "rows"),
            P("blk", "rows"),
            P("rows", "blk"),
            P(("blk", "rows"), None),
            P(("blk", "rows"), None),
            P("rows", "blk", None),
            P("rows", "blk", None),
            P(),
            P("rows"),
        ),
        out_specs=P("rows", "blk"),
        check_vma=False,
    )
```

```python
import jax
import jax.numpy as jnp
import numpy as np
from jax import lax
from jax.experimental import pallas as pl
from jax.experimental.pallas import tpu as pltpu
from jax.sharding import PartitionSpec as P

HD = 128
LOG2E = float(np.log2(np.e))
F32 = jnp.float32
BF = jnp.bfloat16
VM = pl.BlockSpec(memory_space=pltpu.VMEM)
SM = pl.BlockSpec(memory_space=pltpu.SMEM)
NT = (((1,), (1,)), ((), ()))
K0, V0, OK0, OV0, X0, END = 0, 64, 128, 160, 192, 208


def params(mib=48):
    return pltpu.CompilerParams(vmem_limit_bytes=mib * 1024 * 1024)


def iota(shape, dim):
    return lax.broadcasted_iota(jnp.int32, shape, dim)


def pack_body(lens, hidden, keys_hbm, values_hbm, own_k_hbm, own_v_hbm, out, keys, values, own_k, own_v, packed, sems):
    inward = [
        pltpu.make_async_copy(src, dst, sems.at[i])
        for i, (src, dst) in enumerate(
            ((own_k_hbm, own_k), (keys_hbm, keys), (values_hbm, values), (own_v_hbm, own_v))
        )
    ]
    for copy in inward:
        copy.start()
    outward = [
        pltpu.make_async_copy(packed.at[:, first:last, :], out.at[:, first:last, :], sems.at[4 + i])
        for i, (first, last) in enumerate(((OK0, OV0), (K0, V0), (V0, OK0), (OV0, END)))
    ]
    b = lax.axis_index("blk")
    x = hidden[...].astype(F32)
    x_tile = jnp.concatenate([x[:, :HD], x[:, HD:]], axis=0).astype(BF)
    sub = iota((32, HD), 0)
    slot = 8 * b + sub % 8
    dead = []
    for p in range(2):
        live = jnp.zeros((32, HD), jnp.int32)
        for k in range(4):
            live = jnp.where(sub // 8 == k, lens[4 * p + k], live)
        dead.append(slot >= live)
    for step in range(4):
        inward[step].wait()
        for p in range(2):
            for h in range(8):
                col = slice(h * HD, (h + 1) * HD)
                d = 2 * h + p
                if step == 0:
                    own = own_k[32 * p : 32 * p + 32, col].astype(F32)
                    packed[d, OK0:OV0, :] = jnp.where(dead[p], jnp.nan, own).astype(BF)
                elif step == 1:
                    packed[d, K0:V0, :] = keys[64 * p : 64 * p + 64, col]
                elif step == 2:
                    packed[d, V0:OK0, :] = values[64 * p : 64 * p + 64, col]
                else:
                    packed[d, OV0:X0, :] = own_v[32 * p : 32 * p + 32, col]
                    packed[d, X0:END, :] = x_tile
        outward[step].start()
    for copy in outward:
        copy.wait()


def half_swap(x):
    return pltpu.roll(x, 4, 1)


def half_swap(x):
    return pltpu.roll(x, 4, 1)


def gathered_rows(x_ref):
    xr = x_ref[...].astype(F32)
    return jnp.concatenate(
        [xr[:, :8, :].reshape(128, HD), xr[:, 8:, :].reshape(128, HD)], axis=1
    )


def by_rows_of_four(blocks, p):
    blocks = [block.reshape(16, 8, HD) for block in blocks]
    low = iota((16, 8, HD), 1) < 4
    tiles = []
    for u in range(2):
        first, second = blocks[2 * u], blocks[2 * u + 1]
        if p == 0:
            tiles.append(jnp.where(low, first, half_swap(second)))
        else:
            tiles.append(jnp.where(low, half_swap(first), second))
    return tiles


def project_body(x_ref, gain, wq, out):
    x = gathered_rows(x_ref)
    square = lax.dot_general(
        jnp.ones((8, 2 * HD), F32), x * x, NT,
        precision=lax.Precision.HIGHEST, preferred_element_type=F32,
    )
    high = square.astype(BF).astype(F32)
    sub = iota((8, HD), 0)
    squares = jnp.where(sub == 0, high, jnp.where(sub == 1, square - high, 0.0))
    squares = jnp.broadcast_to(squares[None], (16, 8, HD))
    xg = (x * gain[...].astype(F32)).astype(BF)
    q = jnp.dot(xg, wq[...], preferred_element_type=F32)
    heads = [q[:, HD * h : HD * h + HD] for h in range(4)]
    tiles = by_rows_of_four(heads, 0) + [squares] + by_rows_of_four(heads, 1) + [squares]
    out[...] = jnp.concatenate(tiles, axis=1).reshape(768, HD).astype(BF)


def keyval_body(who, x_ref, gain, wa, wb, keep, give):
    xg = (gathered_rows(x_ref) * gain[...].astype(F32)).astype(BF)
    first = jnp.dot(xg, wa[...], preferred_element_type=F32)
    second = jnp.dot(xg, wb[...], preferred_element_type=F32)
    same = lax.rem(who[0], 2) == lax.rem(who[1], 2)
    keep[...] = jnp.where(same, first, second)
    give[...] = jnp.where(same, second, first).astype(BF)


def rotate(u, cosine, sine):
    return u * cosine + pltpu.roll(u, HD // 2, 1) * sine


def query_body(who, parts, cosine, sine, q_out, q_own, scale_out):
    total = jnp.sum(parts[...].astype(F32).reshape(32, 24, HD), axis=0)
    square = total[16:17, :] + total[17:18, :]
    inv = lax.rsqrt(square / 8192.0 + 1e-05)
    lane, sub = iota((16, HD), 1), iota((16, HD), 0)
    col = jnp.sum(jnp.where(lane == 4 * who[0] + sub % 4, inv, 0.0), axis=1, keepdims=True)
    scale_out[...] = jnp.broadcast_to(col, (16, HD))
    raw = (total[0:16, :] * col).astype(BF).astype(F32)
    query = rotate(raw, cosine[...], sine[...]).astype(BF)
    q_own[...] = query
    for i in range(q_out.shape[0]):
        q_out[i, :, :] = query


def attend_body(who, mine, other, q_ref, keep, given, out):
    r = who[1]
    scale = HD ** (-0.5) * LOG2E
    sources = (mine, other)
    halves = (lax.rem(r, 2), 1 - lax.rem(r, 2))
    rows = 256
    row_q, lane = iota((128, HD), 0), iota((128, HD), 1)
    row_q = 4 * (row_q // 16) + row_q % 4
    lane_s = iota((rows, HD), 1)
    sub_s = iota((8, HD), 0)
    kv = (keep[...] + given[...].astype(F32)).reshape(16, 8, HD)
    kv_swapped = half_swap(kv)
    for t in range(512 // rows):
        part = slice(rows // 16 * t, rows // 16 * (t + 1))
        q = q_ref[part].reshape(rows, HD)
        scores, vals = [], []
        for s in sources:
            k = s[:, K0:V0, :].reshape(1024, HD)
            scores.append(lax.dot_general(q, k, NT, preferred_element_type=F32))
            vals.append(s[:, V0:OK0, :].reshape(1024, HD))
        own_scores, own_vals = [], []
        for s, half in zip(sources, halves):
            row_k = 8 * (lane // 32) + 4 * half + (lane % 32) // 8
            blocks, block_vals = [], []
            for u in range(rows // 128):
                first = 4 * (t * (rows // 128) + u)
                k = s[first : first + 4, OK0:OV0, :].reshape(128, HD)
                block_vals.append(s[first : first + 4, OV0:X0, :].reshape(128, HD))
                sc = lax.dot_general(q[128 * u : 128 * u + 128], k, NT, preferred_element_type=F32)
                blocks.append(jnp.where((row_k == row_q) & (sc == sc), sc, -jnp.inf))
            own_scores.append(jnp.concatenate(blocks, axis=0))
            own_vals.append(block_vals)
        peak = jnp.max(scores[0], axis=1, keepdims=True)
        for sc in scores[1:] + own_scores:
            peak = jnp.maximum(peak, jnp.max(sc, axis=1, keepdims=True))
        peak = peak * scale
        high = peak.astype(BF).astype(F32)
        low = (peak - high).astype(BF).astype(F32)
        shift = high + low
        mass = jnp.zeros((rows, 1), F32)
        acc = jnp.zeros((rows, HD), F32)
        for sc, v in zip(scores, vals):
            w = jnp.exp2(sc * scale - shift)
            mass = mass + jnp.sum(w, axis=1, keepdims=True)
            acc = acc + jnp.dot(w.astype(BF), v, preferred_element_type=F32)
        for sc, block_vals in zip(own_scores, own_vals):
            w = jnp.exp2(sc * scale - shift)
            mass = mass + jnp.sum(w, axis=1, keepdims=True)
            w = w.astype(BF)
            acc = acc + jnp.concatenate(
                [
                    jnp.dot(w[128 * u : 128 * u + 128], v, preferred_element_type=F32)
                    for u, v in enumerate(block_vals)
                ],
                axis=0,
            )
        mass_high = mass.astype(BF).astype(F32)
        stats = jnp.where(
            lane_s == 0, high, jnp.where(lane_s == 1, low, jnp.where(lane_s == 2, mass_high, mass - mass_high))
        )
        stats = jnp.where(lane_s < 4, stats, 0.0)
        for u in range(rows // 128):
            turned = pltpu.roll(stats[128 * u : 128 * u + 128, :].T[0:8, :], 4, 0)
            for i in range(4):
                pair = rows // 32 * t + 4 * u + i
                first = 128 * u + 32 * i
                tiles = [
                    acc[first : first + 16, :],
                    jnp.where(sub_s < 4, kv[pair], turned),
                    acc[first + 16 : first + 32, :],
                    jnp.where(sub_s < 4, kv_swapped[pair], turned),
                ]
                out[48 * pair : 48 * pair + 48, :] = jnp.concatenate(tiles, axis=0).astype(BF)


def twice(tile):
    tile = jnp.where(iota((8, HD), 0) < 4, tile, pltpu.roll(tile, 4, 0))
    return jnp.concatenate([tile, tile], axis=0)


def combine_body(who, parts, q_own, scale, cosine, sine, out):
    parts = parts[...].astype(F32).reshape(32, 24, HD)
    rest = parts[:, 16:24, :].reshape(16, 2, 8, HD)
    new_k = (twice(jnp.sum(rest[:, 0], axis=0)) * scale[...]).astype(BF).astype(F32)
    new_k = rotate(new_k, cosine[...], sine[...]).astype(BF).astype(F32)
    new_v = (twice(jnp.sum(rest[:, 1], axis=0)) * scale[...]).astype(BF).astype(F32)
    new = jnp.sum(q_own[...].astype(F32) * new_k, axis=1, keepdims=True) * (HD ** (-0.5) * LOG2E)
    start = 16 * lax.rem(who[0], 8)
    mine = iota((16, HD), 1) == start + iota((16, HD), 0)
    new = jnp.sum(jnp.where(mine, new, 0.0), axis=0, keepdims=True)
    stats = jnp.concatenate([parts[:, 16 + k, :] for k in range(4, 8)], axis=0).reshape(4, 32, HD)
    peak = stats[0] + stats[1]
    mass = stats[2] + stats[3]
    top = jnp.maximum(jnp.max(peak, axis=0, keepdims=True), new)
    shrink = jnp.exp2(peak - top)
    new_w = jnp.exp2(new - top)
    whole = jnp.sum(mass * shrink, axis=0, keepdims=True) + new_w
    new_share = jnp.sum(jnp.where(mine, new_w / whole, 0.0), axis=1, keepdims=True)
    share = pltpu.roll(shrink / whole, lax.rem(HD - start, HD), 1)
    share = jnp.where(iota((32, HD), 1) < 16, share, 0.0)
    for shift in (16, 32, 64):
        share = share + pltpu.roll(share, shift, 1)
    share = jnp.concatenate([share] * 4, axis=1)
    share = jnp.where(iota((32, 512), 1) // 16 == iota((32, 512), 0), share, 0.0)
    share = jnp.sum(share, axis=0, keepdims=True)
    share = jnp.where(iota((16, 512), 1) % 16 == iota((16, 512), 0), share, 0.0)
    high = share.astype(BF)
    low = (share - high.astype(F32)).astype(BF)
    acc = parts[:, 0:16, :].reshape(512, HD).astype(BF)
    summed = jnp.dot(high, acc, preferred_element_type=F32) + jnp.dot(low, acc, preferred_element_type=F32)
    attended = (summed + new_share * new_v).astype(BF)
    for i in range(out.shape[0]):
        out[i, :, :] = attended


def output_body(att, w, hidden, out, kept):
    kept[...] = hidden[...].astype(F32)
    tiles = att[...].astype(F32).reshape(16, 2, 2, 8, HD)
    low = iota((16, 8, HD), 1) < 4
    total = jnp.zeros(out.shape, F32)
    for h in range(4):
        first, second = tiles[:, 0, h // 2], tiles[:, 1, h // 2]
        if h % 2 == 0:
            rows = jnp.where(low, first, half_swap(second))
        else:
            rows = jnp.where(low, half_swap(first), second)
        total = total + jnp.dot(
            rows.reshape(128, HD).astype(BF), w[HD * h : HD * h + HD, :], preferred_element_type=F32
        )
    out[...] = total.astype(BF)


def rotary_tables(positions):
    freq = (1.0 / 500000.0 ** (np.arange(0, HD, 2) / HD)).astype(np.float32)
    angles = positions.astype(F32)[:, None] * jnp.asarray(np.concatenate([freq, freq]), F32)[None, :]
    sign = np.concatenate([-np.ones(HD // 2), np.ones(HD // 2)]).astype(np.float32)
    return jnp.cos(angles), jnp.sin(angles) * jnp.asarray(sign)[None, :]


def on_device(
    hidden_in,
    norm_gain,
    w_query,
    w_keyval,
    w_out,
    prefix_keys,
    prefix_values,
    own_keys,
    own_values,
    positions,
    lengths,
):
    b, r = lax.axis_index("blk"), lax.axis_index("rows")
    who = jnp.stack([b, r]).astype(jnp.int32)
    sds = jax.ShapeDtypeStruct
    first_w = lax.ppermute(w_keyval, "rows", [(s, 2 * (s % 8) + s // 8) for s in range(16)])
    second_w = lax.ppermute(w_keyval, "rows", [(s, 2 * (s % 8) + 1 - s // 8) for s in range(16)])
    packed = pl.pallas_call(
        pack_body,
        out_shape=sds((16, END, HD), BF),
        in_specs=[SM, VM] + [pl.BlockSpec(memory_space=pltpu.HBM)] * 4,
        out_specs=pl.BlockSpec(memory_space=pltpu.HBM),
        scratch_shapes=[
            pltpu.VMEM((128, 1024), BF),
            pltpu.VMEM((128, 1024), BF),
            pltpu.VMEM((64, 1024), BF),
            pltpu.VMEM((64, 1024), BF),
            pltpu.VMEM((16, END, HD), BF),
            pltpu.SemaphoreType.DMA((8,)),
        ],
        name="pack",
    )(lengths, hidden_in, prefix_keys, prefix_values, own_keys.reshape(64, 1024), own_values.reshape(64, 1024))
    mine = lax.all_to_all(packed, "rows", 0, 0, tiled=True)
    gain = norm_gain.reshape(1, 256)
    x_spec = pl.BlockSpec((16, END - X0, HD), lambda i: (0, X0 // 16, 0))
    gain_spec = pl.BlockSpec((1, 256), lambda i: (0, 0))
    parts = pl.pallas_call(
        project_body,
        grid=(1,),
        out_shape=sds((768, HD), BF),
        in_specs=[x_spec, gain_spec, pl.BlockSpec((256, 512), lambda i: (0, 0))],
        out_specs=pl.BlockSpec((768, HD), lambda i: (0, 0)),
        compiler_params=params(),
        name="project",
    )(mine, gain, w_query)
    positions, parts, mine = lax.optimization_barrier((positions, parts, mine))
    parts = lax.all_to_all(parts, "blk", 0, 0, tiled=True)
    cosine, sine = rotary_tables(jnp.concatenate([lax.dynamic_slice_in_dim(positions, 4 * b, 4, 0)] * 4))
    half, first_w, second_w = lax.optimization_barrier((mine[:, :X0, :], first_w, second_w))
    other = lax.ppermute(half, "rows", [(i, i ^ 1) for i in range(16)])
    keep, give = pl.pallas_call(
        keyval_body,
        grid=(1,),
        out_shape=(sds((128, HD), F32), sds((128, HD), BF)),
        in_specs=[SM, x_spec, gain_spec] + [pl.BlockSpec((256, HD), lambda i: (0, 0))] * 2,
        out_specs=[pl.BlockSpec((128, HD), lambda i: (0, 0))] * 2,
        compiler_params=params(),
        cost_estimate=pl.CostEstimate(flops=10**9, bytes_accessed=1 << 18, transcendentals=0),
        name="keyval",
    )(who, mine, gain, first_w, second_w)
    given = lax.ppermute(give, "blk", [(i, i ^ 1) for i in range(32)])
    query, q_own, row_scale = pl.pallas_call(
        query_body,
        out_shape=(sds((32, 16, HD), BF), sds((16, HD), BF), sds((16, HD), F32)),
        in_specs=[SM, VM, VM, VM],
        out_specs=(VM, VM, VM),
        compiler_params=params(),
        cost_estimate=pl.CostEstimate(flops=3*10**9, bytes_accessed=1 << 20, transcendentals=0),
        name="query",
    )(who, parts, cosine, sine)
    query = lax.all_to_all(query, "blk", 0, 0, tiled=True)
    partial = pl.pallas_call(
        attend_body,
        out_shape=sds((768, HD), BF),
        in_specs=[SM] + [VM] * 5,
        out_specs=VM,
        compiler_params=params(),
        name="attend",
    )(who, mine, other, query, keep, given)
    partial = lax.all_to_all(partial, "blk", 0, 0, tiled=True)
    attended = pl.pallas_call(
        combine_body,
        out_shape=sds((32, 16, HD), BF),
        in_specs=[SM] + [VM] * 5,
        out_specs=VM,
        compiler_params=params(),
        name="combine",
    )(who, partial, q_own, row_scale, cosine, sine)
    attended = lax.all_to_all(attended, "blk", 0, 0, tiled=True)
    mixed, kept = pl.pallas_call(
        output_body,
        out_shape=(sds((128, 256), BF), sds((8, 256), F32)),
        in_specs=[VM] * 3,
        out_specs=(VM, VM),
        compiler_params=params(),
        name="output",
    )(attended, w_out, hidden_in)
    mixed = lax.all_to_all(mixed.reshape(16, 8, 256), "rows", 0, 0, tiled=True)
    return (kept + jnp.sum(mixed.astype(F32), axis=0)).astype(BF)


def solution(mesh):
    return jax.shard_map(
        on_device,
        mesh=mesh,
        in_specs=(
            P("rows", "blk"),
            P("blk"),
            P("blk", "rows"),
            P("blk", "rows"),
            P("rows", "blk"),
            P(("blk", "rows"), None),
            P(("blk", "rows"), None),
            P("rows", "blk", None),
            P("rows", "blk", None),
            P(),
            P("rows"),
        ),
        out_specs=P("rows", "blk"),
        check_vma=False,
    )
```

```python
import jax
import jax.numpy as jnp
import numpy as np
from jax import lax
from jax.experimental import pallas as pl
from jax.experimental.pallas import tpu as pltpu
from jax.sharding import PartitionSpec as P

HD = 128
LOG2E = float(np.log2(np.e))
F32 = jnp.float32
BF = jnp.bfloat16
VM = pl.BlockSpec(memory_space=pltpu.VMEM)
SM = pl.BlockSpec(memory_space=pltpu.SMEM)
NT = (((1,), (1,)), ((), ()))
K0, V0, OK0, OV0, X0, END = 0, 64, 128, 160, 192, 208


def params(mib=48):
    return pltpu.CompilerParams(vmem_limit_bytes=mib * 1024 * 1024)


def iota(shape, dim):
    return lax.broadcasted_iota(jnp.int32, shape, dim)


def pack_body(lens, hidden, keys_hbm, values_hbm, own_k_hbm, own_v_hbm, out, keys, values, own_k, own_v, packed, sems):
    inward = [
        pltpu.make_async_copy(src, dst, sems.at[i])
        for i, (src, dst) in enumerate(
            ((own_k_hbm, own_k), (keys_hbm, keys), (values_hbm, values), (own_v_hbm, own_v))
        )
    ]
    for copy in inward:
        copy.start()
    outward = [
        pltpu.make_async_copy(packed.at[:, first:last, :], out.at[:, first:last, :], sems.at[4 + i])
        for i, (first, last) in enumerate(((OK0, OV0), (K0, V0), (V0, OK0), (OV0, END)))
    ]
    b = lax.axis_index("blk")
    x = hidden[...].astype(F32)
    x_tile = jnp.concatenate([x[:, :HD], x[:, HD:]], axis=0).astype(BF)
    sub = iota((32, HD), 0)
    slot = 8 * b + sub % 8
    dead = []
    for p in range(2):
        live = jnp.zeros((32, HD), jnp.int32)
        for k in range(4):
            live = jnp.where(sub // 8 == k, lens[4 * p + k], live)
        dead.append(slot >= live)
    for step in range(4):
        inward[step].wait()
        for p in range(2):
            for h in range(8):
                col = slice(h * HD, (h + 1) * HD)
                d = 2 * h + p
                if step == 0:
                    own = own_k[32 * p : 32 * p + 32, col].astype(F32)
                    packed[d, OK0:OV0, :] = jnp.where(dead[p], jnp.nan, own).astype(BF)
                elif step == 1:
                    packed[d, K0:V0, :] = keys[64 * p : 64 * p + 64, col]
                elif step == 2:
                    packed[d, V0:OK0, :] = values[64 * p : 64 * p + 64, col]
                else:
                    packed[d, OV0:X0, :] = own_v[32 * p : 32 * p + 32, col]
                    packed[d, X0:END, :] = x_tile
        outward[step].start()
    for copy in outward:
        copy.wait()


def half_swap(x):
    return pltpu.roll(x, 4, 1)


def half_swap(x):
    return pltpu.roll(x, 4, 1)


def gathered_rows(x_ref):
    xr = x_ref[...].astype(F32)
    return jnp.concatenate(
        [xr[:, :8, :].reshape(128, HD), xr[:, 8:, :].reshape(128, HD)], axis=1
    )


def by_rows_of_four(blocks, p):
    blocks = [block.reshape(16, 8, HD) for block in blocks]
    low = iota((16, 8, HD), 1) < 4
    tiles = []
    for u in range(2):
        first, second = blocks[2 * u], blocks[2 * u + 1]
        if p == 0:
            tiles.append(jnp.where(low, first, half_swap(second)))
        else:
            tiles.append(jnp.where(low, half_swap(first), second))
    return tiles


def project_body(x_ref, gain, wq, out):
    x = gathered_rows(x_ref)
    square = lax.dot_general(
        jnp.ones((8, 2 * HD), F32), x * x, NT,
        precision=lax.Precision.HIGHEST, preferred_element_type=F32,
    )
    high = square.astype(BF).astype(F32)
    sub = iota((8, HD), 0)
    squares = jnp.where(sub == 0, high, jnp.where(sub == 1, square - high, 0.0))
    squares = jnp.broadcast_to(squares[None], (16, 8, HD))
    xg = (x * gain[...].astype(F32)).astype(BF)
    q = jnp.dot(xg, wq[...], preferred_element_type=F32)
    heads = [q[:, HD * h : HD * h + HD] for h in range(4)]
    tiles = by_rows_of_four(heads, 0) + [squares] + by_rows_of_four(heads, 1) + [squares]
    out[...] = jnp.concatenate(tiles, axis=1).reshape(768, HD).astype(BF)


def keyval_body(who, x_ref, gain, wa, wb, keep, give):
    xg = (gathered_rows(x_ref) * gain[...].astype(F32)).astype(BF)
    first = jnp.dot(xg, wa[...], preferred_element_type=F32)
    second = jnp.dot(xg, wb[...], preferred_element_type=F32)
    same = lax.rem(who[0], 2) == lax.rem(who[1], 2)
    keep[...] = jnp.where(same, first, second)
    give[...] = jnp.where(same, second, first).astype(BF)


def rotate(u, cosine, sine):
    return u * cosine + pltpu.roll(u, HD // 2, 1) * sine


def query_body(who, parts, cosine, sine, q_out, q_own, scale_out):
    total = jnp.sum(parts[...].astype(F32).reshape(32, 24, HD), axis=0)
    square = total[16:17, :] + total[17:18, :]
    inv = lax.rsqrt(square / 8192.0 + 1e-05)
    lane, sub = iota((16, HD), 1), iota((16, HD), 0)
    col = jnp.sum(jnp.where(lane == 4 * who[0] + sub % 4, inv, 0.0), axis=1, keepdims=True)
    scale_out[...] = jnp.broadcast_to(col, (16, HD))
    raw = (total[0:16, :] * col).astype(BF).astype(F32)
    query = rotate(raw, cosine[...], sine[...]).astype(BF)
    q_own[...] = query
    for i in range(q_out.shape[0]):
        q_out[i, :, :] = query


def attend_body(who, mine, other, q_ref, keep, given, out):
    r = who[1]
    scale = HD ** (-0.5) * LOG2E
    sources = (mine, other)
    halves = (lax.rem(r, 2), 1 - lax.rem(r, 2))
    rows = 256
    row_q, lane = iota((128, HD), 0), iota((128, HD), 1)
    row_q = 4 * (row_q // 16) + row_q % 4
    lane_s = iota((rows, HD), 1)
    sub_s = iota((8, HD), 0)
    kv = (keep[...] + given[...].astype(F32)).reshape(16, 8, HD)
    kv_swapped = half_swap(kv)
    for t in range(512 // rows):
        part = slice(rows // 16 * t, rows // 16 * (t + 1))
        q = q_ref[part].reshape(rows, HD)
        scores, vals = [], []
        for s in sources:
            k = s[:, K0:V0, :].reshape(1024, HD)
            scores.append(lax.dot_general(q, k, NT, preferred_element_type=F32))
            vals.append(s[:, V0:OK0, :].reshape(1024, HD))
        own_scores, own_vals = [], []
        for s, half in zip(sources, halves):
            row_k = 8 * (lane // 32) + 4 * half + (lane % 32) // 8
            blocks, block_vals = [], []
            for u in range(rows // 128):
                first = 4 * (t * (rows // 128) + u)
                k = s[first : first + 4, OK0:OV0, :].reshape(128, HD)
                block_vals.append(s[first : first + 4, OV0:X0, :].reshape(128, HD))
                sc = lax.dot_general(q[128 * u : 128 * u + 128], k, NT, preferred_element_type=F32)
                blocks.append(jnp.where((row_k == row_q) & (sc == sc), sc, -jnp.inf))
            own_scores.append(jnp.concatenate(blocks, axis=0))
            own_vals.append(block_vals)
        peak = jnp.max(scores[0], axis=1, keepdims=True)
        for sc in scores[1:] + own_scores:
            peak = jnp.maximum(peak, jnp.max(sc, axis=1, keepdims=True))
        peak = peak * scale
        high = peak.astype(BF).astype(F32)
        low = (peak - high).astype(BF).astype(F32)
        shift = high + low
        mass = jnp.zeros((rows, 1), F32)
        acc = jnp.zeros((rows, HD), F32)
        for sc, v in zip(scores, vals):
            w = jnp.exp2(sc * scale - shift)
            mass = mass + jnp.sum(w, axis=1, keepdims=True)
            acc = acc + jnp.dot(w.astype(BF), v, preferred_element_type=F32)
        for sc, block_vals in zip(own_scores, own_vals):
            w = jnp.exp2(sc * scale - shift)
            mass = mass + jnp.sum(w, axis=1, keepdims=True)
            w = w.astype(BF)
            acc = acc + jnp.concatenate(
                [
                    jnp.dot(w[128 * u : 128 * u + 128], v, preferred_element_type=F32)
                    for u, v in enumerate(block_vals)
                ],
                axis=0,
            )
        mass_high = mass.astype(BF).astype(F32)
        stats = jnp.where(
            lane_s == 0, high, jnp.where(lane_s == 1, low, jnp.where(lane_s == 2, mass_high, mass - mass_high))
        )
        stats = jnp.where(lane_s < 4, stats, 0.0)
        for u in range(rows // 128):
            turned = pltpu.roll(stats[128 * u : 128 * u + 128, :].T[0:8, :], 4, 0)
            for i in range(4):
                pair = rows // 32 * t + 4 * u + i
                first = 128 * u + 32 * i
                tiles = [
                    acc[first : first + 16, :],
                    jnp.where(sub_s < 4, kv[pair], turned),
                    acc[first + 16 : first + 32, :],
                    jnp.where(sub_s < 4, kv_swapped[pair], turned),
                ]
                out[48 * pair : 48 * pair + 48, :] = jnp.concatenate(tiles, axis=0).astype(BF)


def twice(tile):
    tile = jnp.where(iota((8, HD), 0) < 4, tile, pltpu.roll(tile, 4, 0))
    return jnp.concatenate([tile, tile], axis=0)


def combine_body(who, parts, q_own, scale, cosine, sine, out):
    parts = parts[...].astype(F32).reshape(32, 24, HD)
    rest = parts[:, 16:24, :].reshape(16, 2, 8, HD)
    new_k = (twice(jnp.sum(rest[:, 0], axis=0)) * scale[...]).astype(BF).astype(F32)
    new_k = rotate(new_k, cosine[...], sine[...]).astype(BF).astype(F32)
    new_v = (twice(jnp.sum(rest[:, 1], axis=0)) * scale[...]).astype(BF).astype(F32)
    new = jnp.sum(q_own[...].astype(F32) * new_k, axis=1, keepdims=True) * (HD ** (-0.5) * LOG2E)
    mine = iota((16, HD), 1) == 16 * lax.rem(who[0], 8) + iota((16, HD), 0)
    rest = parts[:, 16:24, :]
    peak = rest[:, 4:5, :] + rest[:, 5:6, :]
    mass = rest[:, 6:7, :] + rest[:, 7:8, :]
    top = jnp.max(peak, axis=0)
    shrink = jnp.exp2(peak - top[None])
    whole = jnp.sum(mass * shrink, axis=0)
    share = jnp.sum(jnp.where(mine[None], shrink, 0.0), axis=2, keepdims=True)
    summed = jnp.sum(parts[:, 0:16, :] * share, axis=0)
    top = jnp.sum(jnp.where(mine, top, 0.0), axis=1, keepdims=True)
    whole = jnp.sum(jnp.where(mine, whole, 0.0), axis=1, keepdims=True)
    over = jnp.maximum(top, new)
    old_w, new_w = jnp.exp2(top - over), jnp.exp2(new - over)
    attended = ((summed * old_w + new_w * new_v) / (whole * old_w + new_w)).astype(BF)
    for i in range(out.shape[0]):
        out[i, :, :] = attended


def output_body(att, w, hidden, out, kept):
    kept[...] = hidden[...].astype(F32)
    tiles = att[...].astype(F32).reshape(16, 2, 2, 8, HD)
    low = iota((16, 8, HD), 1) < 4
    total = jnp.zeros(out.shape, F32)
    for h in range(4):
        first, second = tiles[:, 0, h // 2], tiles[:, 1, h // 2]
        if h % 2 == 0:
            rows = jnp.where(low, first, half_swap(second))
        else:
            rows = jnp.where(low, half_swap(first), second)
        total = total + jnp.dot(
            rows.reshape(128, HD).astype(BF), w[HD * h : HD * h + HD, :], preferred_element_type=F32
        )
    out[...] = total.astype(BF)


def rotary_tables(positions):
    freq = (1.0 / 500000.0 ** (np.arange(0, HD, 2) / HD)).astype(np.float32)
    angles = positions.astype(F32)[:, None] * jnp.asarray(np.concatenate([freq, freq]), F32)[None, :]
    sign = np.concatenate([-np.ones(HD // 2), np.ones(HD // 2)]).astype(np.float32)
    return jnp.cos(angles), jnp.sin(angles) * jnp.asarray(sign)[None, :]


def on_device(
    hidden_in,
    norm_gain,
    w_query,
    w_keyval,
    w_out,
    prefix_keys,
    prefix_values,
    own_keys,
    own_values,
    positions,
    lengths,
):
    b, r = lax.axis_index("blk"), lax.axis_index("rows")
    who = jnp.stack([b, r]).astype(jnp.int32)
    sds = jax.ShapeDtypeStruct
    first_w = lax.ppermute(w_keyval, "rows", [(s, 2 * (s % 8) + s // 8) for s in range(16)])
    second_w = lax.ppermute(w_keyval, "rows", [(s, 2 * (s % 8) + 1 - s // 8) for s in range(16)])
    packed = pl.pallas_call(
        pack_body,
        out_shape=sds((16, END, HD), BF),
        in_specs=[SM, VM] + [pl.BlockSpec(memory_space=pltpu.HBM)] * 4,
        out_specs=pl.BlockSpec(memory_space=pltpu.HBM),
        scratch_shapes=[
            pltpu.VMEM((128, 1024), BF),
            pltpu.VMEM((128, 1024), BF),
            pltpu.VMEM((64, 1024), BF),
            pltpu.VMEM((64, 1024), BF),
            pltpu.VMEM((16, END, HD), BF),
            pltpu.SemaphoreType.DMA((8,)),
        ],
        name="pack",
    )(lengths, hidden_in, prefix_keys, prefix_values, own_keys.reshape(64, 1024), own_values.reshape(64, 1024))
    mine = lax.all_to_all(packed, "rows", 0, 0, tiled=True)
    gain = norm_gain.reshape(1, 256)
    x_spec = pl.BlockSpec((16, END - X0, HD), lambda i: (0, X0 // 16, 0))
    gain_spec = pl.BlockSpec((1, 256), lambda i: (0, 0))
    parts = pl.pallas_call(
        project_body,
        grid=(1,),
        out_shape=sds((768, HD), BF),
        in_specs=[x_spec, gain_spec, pl.BlockSpec((256, 512), lambda i: (0, 0))],
        out_specs=pl.BlockSpec((768, HD), lambda i: (0, 0)),
        compiler_params=params(),
        name="project",
    )(mine, gain, w_query)
    positions, parts, mine = lax.optimization_barrier((positions, parts, mine))
    parts = lax.all_to_all(parts, "blk", 0, 0, tiled=True)
    cosine, sine = rotary_tables(jnp.concatenate([lax.dynamic_slice_in_dim(positions, 4 * b, 4, 0)] * 4))
    half, first_w, second_w = lax.optimization_barrier((mine[:, :X0, :], first_w, second_w))
    other = lax.ppermute(half, "rows", [(i, i ^ 1) for i in range(16)])
    keep, give = pl.pallas_call(
        keyval_body,
        grid=(1,),
        out_shape=(sds((128, HD), F32), sds((128, HD), BF)),
        in_specs=[SM, x_spec, gain_spec] + [pl.BlockSpec((256, HD), lambda i: (0, 0))] * 2,
        out_specs=[pl.BlockSpec((128, HD), lambda i: (0, 0))] * 2,
        compiler_params=params(),
        cost_estimate=pl.CostEstimate(flops=10**9, bytes_accessed=1 << 18, transcendentals=0),
        name="keyval",
    )(who, mine, gain, first_w, second_w)
    given = lax.ppermute(give, "blk", [(i, i ^ 1) for i in range(32)])
    query, q_own, row_scale = pl.pallas_call(
        query_body,
        out_shape=(sds((32, 16, HD), BF), sds((16, HD), BF), sds((16, HD), F32)),
        in_specs=[SM, VM, VM, VM],
        out_specs=(VM, VM, VM),
        compiler_params=params(),
        cost_estimate=pl.CostEstimate(flops=3*10**9, bytes_accessed=1 << 20, transcendentals=0),
        name="query",
    )(who, parts, cosine, sine)
    query = lax.all_to_all(query, "blk", 0, 0, tiled=True)
    partial = pl.pallas_call(
        attend_body,
        out_shape=sds((768, HD), BF),
        in_specs=[SM] + [VM] * 5,
        out_specs=VM,
        compiler_params=params(),
        name="attend",
    )(who, mine, other, query, keep, given)
    partial = lax.all_to_all(partial, "blk", 0, 0, tiled=True)
    attended = pl.pallas_call(
        combine_body,
        out_shape=sds((32, 16, HD), BF),
        in_specs=[SM] + [VM] * 5,
        out_specs=VM,
        compiler_params=params(),
        name="combine",
    )(who, partial, q_own, row_scale, cosine, sine)
    attended = lax.all_to_all(attended, "blk", 0, 0, tiled=True)
    mixed, kept = pl.pallas_call(
        output_body,
        out_shape=(sds((128, 256), BF), sds((8, 256), F32)),
        in_specs=[VM] * 3,
        out_specs=(VM, VM),
        compiler_params=params(),
        name="output",
    )(attended, w_out, hidden_in)
    mixed = lax.all_to_all(mixed.reshape(16, 8, 256), "rows", 0, 0, tiled=True)
    return (kept + jnp.sum(mixed.astype(F32), axis=0)).astype(BF)


def solution(mesh):
    return jax.shard_map(
        on_device,
        mesh=mesh,
        in_specs=(
            P("rows", "blk"),
            P("blk"),
            P("blk", "rows"),
            P("blk", "rows"),
            P("rows", "blk"),
            P(("blk", "rows"), None),
            P(("blk", "rows"), None),
            P("rows", "blk", None),
            P("rows", "blk", None),
            P(),
            P("rows"),
        ),
        out_specs=P("rows", "blk"),
        check_vma=False,
    )
```

```python
import jax
import jax.numpy as jnp
import numpy as np
from jax import lax
from jax.experimental import pallas as pl
from jax.experimental.pallas import tpu as pltpu
from jax.sharding import PartitionSpec as P

HD = 128
LOG2E = float(np.log2(np.e))
F32 = jnp.float32
BF = jnp.bfloat16
VM = pl.BlockSpec(memory_space=pltpu.VMEM)
SM = pl.BlockSpec(memory_space=pltpu.SMEM)
NT = (((1,), (1,)), ((), ()))
K0, V0, OK0, OV0, X0, END = 0, 64, 128, 160, 192, 208


def params(mib=48):
    return pltpu.CompilerParams(vmem_limit_bytes=mib * 1024 * 1024)


def iota(shape, dim):
    return lax.broadcasted_iota(jnp.int32, shape, dim)


def pack_body(lens, hidden, keys_hbm, values_hbm, own_k_hbm, own_v_hbm, out, keys, values, own_k, own_v, packed, sems):
    inward = [
        pltpu.make_async_copy(src, dst, sems.at[i])
        for i, (src, dst) in enumerate(
            ((own_k_hbm, own_k), (keys_hbm, keys), (values_hbm, values), (own_v_hbm, own_v))
        )
    ]
    for copy in inward:
        copy.start()
    outward = [
        pltpu.make_async_copy(packed.at[:, first:last, :], out.at[:, first:last, :], sems.at[4 + i])
        for i, (first, last) in enumerate(((OK0, OV0), (K0, V0), (V0, OK0), (OV0, END)))
    ]
    b = lax.axis_index("blk")
    x = hidden[...].astype(F32)
    x_tile = jnp.concatenate([x[:, :HD], x[:, HD:]], axis=0).astype(BF)
    sub = iota((32, HD), 0)
    slot = 8 * b + sub % 8
    dead = []
    for p in range(2):
        live = jnp.zeros((32, HD), jnp.int32)
        for k in range(4):
            live = jnp.where(sub // 8 == k, lens[4 * p + k], live)
        dead.append(slot >= live)
    for step in range(4):
        inward[step].wait()
        for p in range(2):
            for h in range(8):
                col = slice(h * HD, (h + 1) * HD)
                d = 2 * h + p
                if step == 0:
                    own = own_k[32 * p : 32 * p + 32, col].astype(F32)
                    packed[d, OK0:OV0, :] = jnp.where(dead[p], jnp.nan, own).astype(BF)
                elif step == 1:
                    packed[d, K0:V0, :] = keys[64 * p : 64 * p + 64, col]
                elif step == 2:
                    packed[d, V0:OK0, :] = values[64 * p : 64 * p + 64, col]
                else:
                    packed[d, OV0:X0, :] = own_v[32 * p : 32 * p + 32, col]
                    packed[d, X0:END, :] = x_tile
        outward[step].start()
    for copy in outward:
        copy.wait()


def half_swap(x):
    return pltpu.roll(x, 4, 1)


def half_swap(x):
    return pltpu.roll(x, 4, 1)


def gathered_rows(x_ref):
    xr = x_ref[...].astype(F32)
    return jnp.concatenate(
        [xr[:, :8, :].reshape(128, HD), xr[:, 8:, :].reshape(128, HD)], axis=1
    )


def by_rows_of_four(blocks, p):
    blocks = [block.reshape(16, 8, HD) for block in blocks]
    low = iota((16, 8, HD), 1) < 4
    tiles = []
    for u in range(2):
        first, second = blocks[2 * u], blocks[2 * u + 1]
        if p == 0:
            tiles.append(jnp.where(low, first, half_swap(second)))
        else:
            tiles.append(jnp.where(low, half_swap(first), second))
    return tiles


def project_body(x_ref, gain, wq, out):
    x = gathered_rows(x_ref)
    square = lax.dot_general(
        jnp.ones((8, 2 * HD), F32), x * x, NT,
        precision=lax.Precision.HIGHEST, preferred_element_type=F32,
    )
    high = square.astype(BF).astype(F32)
    sub = iota((8, HD), 0)
    squares = jnp.where(sub == 0, high, jnp.where(sub == 1, square - high, 0.0))
    squares = jnp.broadcast_to(squares[None], (16, 8, HD))
    xg = (x * gain[...].astype(F32)).astype(BF)
    q = jnp.dot(xg, wq[...], preferred_element_type=F32)
    heads = [q[:, HD * h : HD * h + HD] for h in range(4)]
    tiles = by_rows_of_four(heads, 0) + [squares] + by_rows_of_four(heads, 1) + [squares]
    out[...] = jnp.concatenate(tiles, axis=1).reshape(768, HD).astype(BF)


def keyval_body(who, x_ref, gain, wa, wb, keep, give):
    xg = (gathered_rows(x_ref) * gain[...].astype(F32)).astype(BF)
    first = jnp.dot(xg, wa[...], preferred_element_type=F32)
    second = jnp.dot(xg, wb[...], preferred_element_type=F32)
    same = lax.rem(who[0], 2) == lax.rem(who[1], 2)
    keep[...] = jnp.where(same, first, second)
    give[...] = jnp.where(same, second, first).astype(BF)


def rotate(u, cosine, sine):
    return u * cosine + pltpu.roll(u, HD // 2, 1) * sine


def query_body(who, parts, cosine, sine, q_out, q_own, scale_out):
    total = jnp.sum(parts[...].astype(F32).reshape(32, 24, HD), axis=0)
    square = total[16:17, :] + total[17:18, :]
    inv = lax.rsqrt(square / 8192.0 + 1e-05)
    lane, sub = iota((16, HD), 1), iota((16, HD), 0)
    col = jnp.sum(jnp.where(lane == 4 * who[0] + sub % 4, inv, 0.0), axis=1, keepdims=True)
    scale_out[...] = jnp.broadcast_to(col, (16, HD))
    raw = (total[0:16, :] * col).astype(BF).astype(F32)
    query = rotate(raw, cosine[...], sine[...]).astype(BF)
    q_own[...] = query
    for i in range(q_out.shape[0]):
        q_out[i, :, :] = query


def attend_body(who, mine, other, q_ref, keep, given, out):
    r = who[1]
    scale = HD ** (-0.5) * LOG2E
    sources = (mine, other)
    halves = (lax.rem(r, 2), 1 - lax.rem(r, 2))
    rows = 256
    row_q, lane = iota((128, HD), 0), iota((128, HD), 1)
    row_q = 4 * (row_q // 16) + row_q % 4
    lane_s = iota((rows, HD), 1)
    sub_s = iota((8, HD), 0)
    kv = (keep[...] + given[...].astype(F32)).reshape(16, 8, HD)
    kv_swapped = half_swap(kv)
    for t in range(512 // rows):
        part = slice(rows // 16 * t, rows // 16 * (t + 1))
        q = q_ref[part].reshape(rows, HD)
        scores, vals = [], []
        for s in sources:
            k = s[:, K0:V0, :].reshape(1024, HD)
            scores.append(lax.dot_general(q, k, NT, preferred_element_type=F32))
            vals.append(s[:, V0:OK0, :].reshape(1024, HD))
        own_scores, own_vals = [], []
        for s, half in zip(sources, halves):
            row_k = 8 * (lane // 32) + 4 * half + (lane % 32) // 8
            blocks, block_vals = [], []
            for u in range(rows // 128):
                first = 4 * (t * (rows // 128) + u)
                k = s[first : first + 4, OK0:OV0, :].reshape(128, HD)
                block_vals.append(s[first : first + 4, OV0:X0, :].reshape(128, HD))
                sc = lax.dot_general(q[128 * u : 128 * u + 128], k, NT, preferred_element_type=F32)
                blocks.append(jnp.where((row_k == row_q) & (sc == sc), sc, -jnp.inf))
            own_scores.append(jnp.concatenate(blocks, axis=0))
            own_vals.append(block_vals)
        peak = jnp.max(scores[0], axis=1, keepdims=True)
        for sc in scores[1:] + own_scores:
            peak = jnp.maximum(peak, jnp.max(sc, axis=1, keepdims=True))
        peak = peak * scale
        high = peak.astype(BF).astype(F32)
        low = (peak - high).astype(BF).astype(F32)
        shift = high + low
        mass = jnp.zeros((rows, 1), F32)
        acc = jnp.zeros((rows, HD), F32)
        for sc, v in zip(scores, vals):
            w = jnp.exp2(sc * scale - shift)
            mass = mass + jnp.sum(w, axis=1, keepdims=True)
            acc = acc + jnp.dot(w.astype(BF), v, preferred_element_type=F32)
        for sc, block_vals in zip(own_scores, own_vals):
            w = jnp.exp2(sc * scale - shift)
            mass = mass + jnp.sum(w, axis=1, keepdims=True)
            w = w.astype(BF)
            acc = acc + jnp.concatenate(
                [
                    jnp.dot(w[128 * u : 128 * u + 128], v, preferred_element_type=F32)
                    for u, v in enumerate(block_vals)
                ],
                axis=0,
            )
        mass_high = mass.astype(BF).astype(F32)
        stats = jnp.where(
            lane_s == 0, high, jnp.where(lane_s == 1, low, jnp.where(lane_s == 2, mass_high, mass - mass_high))
        )
        stats = jnp.where(lane_s < 4, stats, 0.0)
        for u in range(rows // 128):
            turned = pltpu.roll(stats[128 * u : 128 * u + 128, :].T[0:8, :], 4, 0)
            for i in range(4):
                pair = rows // 32 * t + 4 * u + i
                first = 128 * u + 32 * i
                tiles = [
                    acc[first : first + 16, :],
                    jnp.where(sub_s < 4, kv[pair], turned),
                    acc[first + 16 : first + 32, :],
                    jnp.where(sub_s < 4, kv_swapped[pair], turned),
                ]
                out[48 * pair : 48 * pair + 48, :] = jnp.concatenate(tiles, axis=0).astype(BF)


def twice(tile):
    tile = jnp.where(iota((8, HD), 0) < 4, tile, pltpu.roll(tile, 4, 0))
    return jnp.concatenate([tile, tile], axis=0)


def combine_body(who, parts, q_own, scale, cosine, sine, out):
    parts = parts[...].astype(F32).reshape(32, 24, HD)
    rest = parts[:, 16:24, :].reshape(16, 2, 8, HD)
    new_k = (twice(jnp.sum(rest[:, 0], axis=0)) * scale[...]).astype(BF).astype(F32)
    new_k = rotate(new_k, cosine[...], sine[...]).astype(BF).astype(F32)
    new_v = (twice(jnp.sum(rest[:, 1], axis=0)) * scale[...]).astype(BF).astype(F32)
    new = jnp.sum(q_own[...].astype(F32) * new_k, axis=1, keepdims=True) * (HD ** (-0.5) * LOG2E)
    mine = iota((16, HD), 1) == 16 * lax.rem(who[0], 8) + iota((16, HD), 0)
    rest = parts[:, 16:24, :]
    peak = rest[:, 4:5, :] + rest[:, 5:6, :]
    mass = rest[:, 6:7, :] + rest[:, 7:8, :]
    top = jnp.max(peak, axis=0)
    shrink = jnp.exp2(peak - top[None])
    whole = jnp.sum(mass * shrink, axis=0)
    share = jnp.sum(jnp.where(mine[None], shrink, 0.0), axis=2, keepdims=True)
    summed = jnp.sum(parts[:, 0:16, :] * share, axis=0)
    top = jnp.sum(jnp.where(mine, top, 0.0), axis=1, keepdims=True)
    whole = jnp.sum(jnp.where(mine, whole, 0.0), axis=1, keepdims=True)
    over = jnp.maximum(top, new)
    old_w, new_w = jnp.exp2(top - over), jnp.exp2(new - over)
    attended = ((summed * old_w + new_w * new_v) / (whole * old_w + new_w)).astype(BF)
    for i in range(out.shape[0]):
        out[i, :, :] = attended


def output_body(att, w, hidden, out, kept):
    kept[...] = hidden[...].astype(F32)
    tiles = att[...].astype(F32).reshape(16, 2, 2, 8, HD)
    low = iota((16, 8, HD), 1) < 4
    total = jnp.zeros(out.shape, F32)
    for h in range(4):
        first, second = tiles[:, 0, h // 2], tiles[:, 1, h // 2]
        if h % 2 == 0:
            rows = jnp.where(low, first, half_swap(second))
        else:
            rows = jnp.where(low, half_swap(first), second)
        total = total + jnp.dot(
            rows.reshape(128, HD).astype(BF), w[HD * h : HD * h + HD, :], preferred_element_type=F32
        )
    out[...] = total.astype(BF)


def rotary_tables(positions):
    freq = (1.0 / 500000.0 ** (np.arange(0, HD, 2) / HD)).astype(np.float32)
    angles = positions.astype(F32)[:, None] * jnp.asarray(np.concatenate([freq, freq]), F32)[None, :]
    sign = np.concatenate([-np.ones(HD // 2), np.ones(HD // 2)]).astype(np.float32)
    return jnp.cos(angles), jnp.sin(angles) * jnp.asarray(sign)[None, :]


def on_device(
    hidden_in,
    norm_gain,
    w_query,
    w_keyval,
    w_out,
    prefix_keys,
    prefix_values,
    own_keys,
    own_values,
    positions,
    lengths,
):
    b, r = lax.axis_index("blk"), lax.axis_index("rows")
    who = jnp.stack([b, r]).astype(jnp.int32)
    sds = jax.ShapeDtypeStruct
    first_w = lax.ppermute(w_keyval, "rows", [(s, 2 * (s % 8) + s // 8) for s in range(16)])
    second_w = lax.ppermute(w_keyval, "rows", [(s, 2 * (s % 8) + 1 - s // 8) for s in range(16)])
    packed = pl.pallas_call(
        pack_body,
        out_shape=sds((16, END, HD), BF),
        in_specs=[SM, VM] + [pl.BlockSpec(memory_space=pltpu.HBM)] * 4,
        out_specs=pl.BlockSpec(memory_space=pltpu.HBM),
        scratch_shapes=[
            pltpu.VMEM((128, 1024), BF),
            pltpu.VMEM((128, 1024), BF),
            pltpu.VMEM((64, 1024), BF),
            pltpu.VMEM((64, 1024), BF),
            pltpu.VMEM((16, END, HD), BF),
            pltpu.SemaphoreType.DMA((8,)),
        ],
        name="pack",
    )(lengths, hidden_in, prefix_keys, prefix_values, own_keys.reshape(64, 1024), own_values.reshape(64, 1024))
    mine = lax.all_to_all(packed, "rows", 0, 0, tiled=True)
    cosine, sine = rotary_tables(jnp.concatenate([lax.dynamic_slice_in_dim(positions, 4 * b, 4, 0)] * 4))
    gain, cosine, sine = lax.optimization_barrier((norm_gain.reshape(1, 256), cosine, sine))
    x_spec = pl.BlockSpec((16, END - X0, HD), lambda i: (0, X0 // 16, 0))
    gain_spec = pl.BlockSpec((1, 256), lambda i: (0, 0))
    parts = pl.pallas_call(
        project_body,
        grid=(1,),
        out_shape=sds((768, HD), BF),
        in_specs=[x_spec, gain_spec, pl.BlockSpec((256, 512), lambda i: (0, 0))],
        out_specs=pl.BlockSpec((768, HD), lambda i: (0, 0)),
        compiler_params=params(),
        name="project",
    )(mine, gain, w_query)
    parts, mine = lax.optimization_barrier((parts, mine))
    parts = lax.all_to_all(parts, "blk", 0, 0, tiled=True)
    half, first_w, second_w = lax.optimization_barrier((mine[:, :X0, :], first_w, second_w))
    other = lax.ppermute(half, "rows", [(i, i ^ 1) for i in range(16)])
    keep, give = pl.pallas_call(
        keyval_body,
        grid=(1,),
        out_shape=(sds((128, HD), F32), sds((128, HD), BF)),
        in_specs=[SM, x_spec, gain_spec] + [pl.BlockSpec((256, HD), lambda i: (0, 0))] * 2,
        out_specs=[pl.BlockSpec((128, HD), lambda i: (0, 0))] * 2,
        compiler_params=params(),
        cost_estimate=pl.CostEstimate(flops=10**9, bytes_accessed=1 << 18, transcendentals=0),
        name="keyval",
    )(who, mine, gain, first_w, second_w)
    given = lax.ppermute(give, "blk", [(i, i ^ 1) for i in range(32)])
    query, q_own, row_scale = pl.pallas_call(
        query_body,
        out_shape=(sds((32, 16, HD), BF), sds((16, HD), BF), sds((16, HD), F32)),
        in_specs=[SM, VM, VM, VM],
        out_specs=(VM, VM, VM),
        compiler_params=params(),
        cost_estimate=pl.CostEstimate(flops=2*10**9, bytes_accessed=1 << 20, transcendentals=0),
        name="query",
    )(who, parts, cosine, sine)
    query, given = lax.optimization_barrier((query, given))
    query = lax.all_to_all(query, "blk", 0, 0, tiled=True)
    partial = pl.pallas_call(
        attend_body,
        out_shape=sds((768, HD), BF),
        in_specs=[SM] + [VM] * 5,
        out_specs=VM,
        compiler_params=params(),
        name="attend",
    )(who, mine, other, query, keep, given)
    partial = lax.all_to_all(partial, "blk", 0, 0, tiled=True)
    attended = pl.pallas_call(
        combine_body,
        out_shape=sds((32, 16, HD), BF),
        in_specs=[SM] + [VM] * 5,
        out_specs=VM,
        compiler_params=params(),
        name="combine",
    )(who, partial, q_own, row_scale, cosine, sine)
    attended = lax.all_to_all(attended, "blk", 0, 0, tiled=True)
    mixed, kept = pl.pallas_call(
        output_body,
        out_shape=(sds((128, 256), BF), sds((8, 256), F32)),
        in_specs=[VM] * 3,
        out_specs=(VM, VM),
        compiler_params=params(),
        name="output",
    )(attended, w_out, hidden_in)
    mixed = lax.all_to_all(mixed.reshape(16, 8, 256), "rows", 0, 0, tiled=True)
    return (kept + jnp.sum(mixed.astype(F32), axis=0)).astype(BF)


def solution(mesh):
    return jax.shard_map(
        on_device,
        mesh=mesh,
        in_specs=(
            P("rows", "blk"),
            P("blk"),
            P("blk", "rows"),
            P("blk", "rows"),
            P("rows", "blk"),
            P(("blk", "rows"), None),
            P(("blk", "rows"), None),
            P("rows", "blk", None),
            P("rows", "blk", None),
            P(),
            P("rows"),
        ),
        out_specs=P("rows", "blk"),
        check_vma=False,
    )
```

```python
import jax
import jax.numpy as jnp
import numpy as np
from jax import lax
from jax.experimental import pallas as pl
from jax.experimental.pallas import tpu as pltpu
from jax.sharding import PartitionSpec as P

HD = 128
LOG2E = float(np.log2(np.e))
F32 = jnp.float32
BF = jnp.bfloat16
VM = pl.BlockSpec(memory_space=pltpu.VMEM)
SM = pl.BlockSpec(memory_space=pltpu.SMEM)
NT = (((1,), (1,)), ((), ()))
K0, V0, OK0, OV0, X0, END = 0, 64, 128, 160, 192, 208


def params(mib=48):
    return pltpu.CompilerParams(vmem_limit_bytes=mib * 1024 * 1024)


def iota(shape, dim):
    return lax.broadcasted_iota(jnp.int32, shape, dim)


def pack_body(lens, hidden, keys_hbm, values_hbm, own_k_hbm, own_v_hbm, out, keys, values, own_k, own_v, packed, sems):
    inward = [
        pltpu.make_async_copy(src, dst, sems.at[i])
        for i, (src, dst) in enumerate(
            ((own_k_hbm, own_k), (keys_hbm, keys), (values_hbm, values), (own_v_hbm, own_v))
        )
    ]
    for copy in inward:
        copy.start()
    outward = [
        pltpu.make_async_copy(packed.at[:, first:last, :], out.at[:, first:last, :], sems.at[4 + i])
        for i, (first, last) in enumerate(((OK0, OV0), (K0, V0), (V0, OK0), (OV0, END)))
    ]
    b = lax.axis_index("blk")
    x = hidden[...].astype(F32)
    x_tile = jnp.concatenate([x[:, :HD], x[:, HD:]], axis=0).astype(BF)
    sub = iota((32, HD), 0)
    slot = 8 * b + sub % 8
    dead = []
    for p in range(2):
        live = jnp.zeros((32, HD), jnp.int32)
        for k in range(4):
            live = jnp.where(sub // 8 == k, lens[4 * p + k], live)
        dead.append(slot >= live)
    for step in range(4):
        inward[step].wait()
        for p in range(2):
            for h in range(8):
                col = slice(h * HD, (h + 1) * HD)
                d = 2 * h + p
                if step == 0:
                    own = own_k[32 * p : 32 * p + 32, col].astype(F32)
                    packed[d, OK0:OV0, :] = jnp.where(dead[p], jnp.nan, own).astype(BF)
                elif step == 1:
                    packed[d, K0:V0, :] = keys[64 * p : 64 * p + 64, col]
                elif step == 2:
                    packed[d, V0:OK0, :] = values[64 * p : 64 * p + 64, col]
                else:
                    packed[d, OV0:X0, :] = own_v[32 * p : 32 * p + 32, col]
                    packed[d, X0:END, :] = x_tile
        outward[step].start()
    for copy in outward:
        copy.wait()


def half_swap(x):
    return pltpu.roll(x, 4, 1)


def half_swap(x):
    return pltpu.roll(x, 4, 1)


def gathered_rows(x_ref):
    xr = x_ref[...].astype(F32)
    return jnp.concatenate(
        [xr[:, :8, :].reshape(128, HD), xr[:, 8:, :].reshape(128, HD)], axis=1
    )


def by_rows_of_four(blocks, p):
    blocks = [block.reshape(16, 8, HD) for block in blocks]
    low = iota((16, 8, HD), 1) < 4
    tiles = []
    for u in range(2):
        first, second = blocks[2 * u], blocks[2 * u + 1]
        if p == 0:
            tiles.append(jnp.where(low, first, half_swap(second)))
        else:
            tiles.append(jnp.where(low, half_swap(first), second))
    return tiles


def project_body(x_ref, gain, wq, out):
    x = gathered_rows(x_ref)
    square = lax.dot_general(
        jnp.ones((8, 2 * HD), F32), x * x, NT,
        precision=lax.Precision.HIGHEST, preferred_element_type=F32,
    )
    high = square.astype(BF).astype(F32)
    sub = iota((8, HD), 0)
    squares = jnp.where(sub == 0, high, jnp.where(sub == 1, square - high, 0.0))
    squares = jnp.broadcast_to(squares[None], (16, 8, HD))
    xg = (x * gain[...].astype(F32)).astype(BF)
    q = jnp.dot(xg, wq[...], preferred_element_type=F32)
    heads = [q[:, HD * h : HD * h + HD] for h in range(4)]
    tiles = by_rows_of_four(heads, 0) + [squares] + by_rows_of_four(heads, 1) + [squares]
    out[...] = jnp.concatenate(tiles, axis=1).reshape(768, HD).astype(BF)


def keyval_body(who, x_ref, gain, wa, wb, keep, give):
    xg = (gathered_rows(x_ref) * gain[...].astype(F32)).astype(BF)
    first = jnp.dot(xg, wa[...], preferred_element_type=F32)
    second = jnp.dot(xg, wb[...], preferred_element_type=F32)
    same = lax.rem(who[0], 2) == lax.rem(who[1], 2)
    keep[...] = jnp.where(same, first, second)
    give[...] = jnp.where(same, second, first).astype(BF)


def rotate(u, cosine, sine):
    return u * cosine + pltpu.roll(u, HD // 2, 1) * sine


def query_body(who, parts, cosine, sine, q_out, q_own, scale_out):
    total = jnp.sum(parts[...].astype(F32).reshape(32, 24, HD), axis=0)
    square = total[16:17, :] + total[17:18, :]
    inv = lax.rsqrt(square / 8192.0 + 1e-05)
    lane, sub = iota((16, HD), 1), iota((16, HD), 0)
    col = jnp.sum(jnp.where(lane == 4 * who[0] + sub % 4, inv, 0.0), axis=1, keepdims=True)
    scale_out[...] = jnp.broadcast_to(col, (16, HD))
    raw = (total[0:16, :] * col).astype(BF).astype(F32)
    query = rotate(raw, cosine[...], sine[...]).astype(BF)
    q_own[...] = query
    for i in range(q_out.shape[0]):
        q_out[i, :, :] = query


def attend_body(who, mine, other, q_ref, keep, given, out):
    r = who[1]
    scale = HD ** (-0.5) * LOG2E
    sources = (mine, other)
    halves = (lax.rem(r, 2), 1 - lax.rem(r, 2))
    rows = 256
    row_q, lane = iota((128, HD), 0), iota((128, HD), 1)
    row_q = 4 * (row_q // 16) + row_q % 4
    lane_s = iota((rows, HD), 1)
    sub_s = iota((8, HD), 0)
    kv = (keep[...] + given[...].astype(F32)).reshape(16, 8, HD)
    kv_swapped = half_swap(kv)
    for t in range(512 // rows):
        part = slice(rows // 16 * t, rows // 16 * (t + 1))
        q = q_ref[part].reshape(rows, HD)
        scores, vals = [], []
        for s in sources:
            k = s[:, K0:V0, :].reshape(1024, HD)
            scores.append(lax.dot_general(q, k, NT, preferred_element_type=F32))
            vals.append(s[:, V0:OK0, :].reshape(1024, HD))
        own_scores, own_vals = [], []
        for s, half in zip(sources, halves):
            row_k = 8 * (lane // 32) + 4 * half + (lane % 32) // 8
            blocks, block_vals = [], []
            for u in range(rows // 128):
                first = 4 * (t * (rows // 128) + u)
                k = s[first : first + 4, OK0:OV0, :].reshape(128, HD)
                block_vals.append(s[first : first + 4, OV0:X0, :].reshape(128, HD))
                sc = lax.dot_general(q[128 * u : 128 * u + 128], k, NT, preferred_element_type=F32)
                blocks.append(jnp.where((row_k == row_q) & (sc == sc), sc, -jnp.inf))
            own_scores.append(jnp.concatenate(blocks, axis=0))
            own_vals.append(block_vals)
        peak = jnp.max(scores[0], axis=1, keepdims=True)
        for sc in scores[1:] + own_scores:
            peak = jnp.maximum(peak, jnp.max(sc, axis=1, keepdims=True))
        peak = peak * scale
        high = peak.astype(BF).astype(F32)
        low = (peak - high).astype(BF).astype(F32)
        shift = high + low
        mass = jnp.zeros((rows, 1), F32)
        acc = jnp.zeros((rows, HD), F32)
        for sc, v in zip(scores, vals):
            w = jnp.exp2(sc * scale - shift)
            mass = mass + jnp.sum(w, axis=1, keepdims=True)
            acc = acc + jnp.dot(w.astype(BF), v, preferred_element_type=F32)
        for sc, block_vals in zip(own_scores, own_vals):
            w = jnp.exp2(sc * scale - shift)
            mass = mass + jnp.sum(w, axis=1, keepdims=True)
            w = w.astype(BF)
            acc = acc + jnp.concatenate(
                [
                    jnp.dot(w[128 * u : 128 * u + 128], v, preferred_element_type=F32)
                    for u, v in enumerate(block_vals)
                ],
                axis=0,
            )
        mass_high = mass.astype(BF).astype(F32)
        stats = jnp.where(
            lane_s == 0, high, jnp.where(lane_s == 1, low, jnp.where(lane_s == 2, mass_high, mass - mass_high))
        )
        stats = jnp.where(lane_s < 4, stats, 0.0)
        for u in range(rows // 128):
            turned = pltpu.roll(stats[128 * u : 128 * u + 128, :].T[0:8, :], 4, 0)
            for i in range(4):
                pair = rows // 32 * t + 4 * u + i
                first = 128 * u + 32 * i
                tiles = [
                    acc[first : first + 16, :],
                    jnp.where(sub_s < 4, kv[pair], turned),
                    acc[first + 16 : first + 32, :],
                    jnp.where(sub_s < 4, kv_swapped[pair], turned),
                ]
                out[48 * pair : 48 * pair + 48, :] = jnp.concatenate(tiles, axis=0).astype(BF)


def twice(tile):
    tile = jnp.where(iota((8, HD), 0) < 4, tile, pltpu.roll(tile, 4, 0))
    return jnp.concatenate([tile, tile], axis=0)


def combine_body(who, parts, q_own, scale, cosine, sine, out):
    parts = parts[...].astype(F32).reshape(32, 24, HD)
    rest = parts[:, 16:24, :].reshape(16, 2, 8, HD)
    new_k = (twice(jnp.sum(rest[:, 0], axis=0)) * scale[...]).astype(BF).astype(F32)
    new_k = rotate(new_k, cosine[...], sine[...]).astype(BF).astype(F32)
    new_v = (twice(jnp.sum(rest[:, 1], axis=0)) * scale[...]).astype(BF).astype(F32)
    new = jnp.sum(q_own[...].astype(F32) * new_k, axis=1, keepdims=True) * (HD ** (-0.5) * LOG2E)
    mine = iota((16, HD), 1) == 16 * lax.rem(who[0], 8) + iota((16, HD), 0)
    rest = parts[:, 16:24, :]
    peak = rest[:, 4:5, :] + rest[:, 5:6, :]
    mass = rest[:, 6:7, :] + rest[:, 7:8, :]
    top = jnp.max(peak, axis=0)
    shrink = jnp.exp2(peak - top[None])
    whole = jnp.sum(mass * shrink, axis=0)
    share = jnp.sum(jnp.where(mine[None], shrink, 0.0), axis=2, keepdims=True)
    summed = jnp.sum(parts[:, 0:16, :] * share, axis=0)
    top = jnp.sum(jnp.where(mine, top, 0.0), axis=1, keepdims=True)
    whole = jnp.sum(jnp.where(mine, whole, 0.0), axis=1, keepdims=True)
    over = jnp.maximum(top, new)
    old_w, new_w = jnp.exp2(top - over), jnp.exp2(new - over)
    attended = ((summed * old_w + new_w * new_v) / (whole * old_w + new_w)).astype(BF)
    for i in range(out.shape[0]):
        out[i, :, :] = attended


def output_body(att, w, hidden, out, kept):
    kept[...] = hidden[...].astype(F32)
    tiles = att[...].astype(F32).reshape(16, 2, 2, 8, HD)
    low = iota((16, 8, HD), 1) < 4
    total = jnp.zeros(out.shape, F32)
    for h in range(4):
        first, second = tiles[:, 0, h // 2], tiles[:, 1, h // 2]
        if h % 2 == 0:
            rows = jnp.where(low, first, half_swap(second))
        else:
            rows = jnp.where(low, half_swap(first), second)
        total = total + jnp.dot(
            rows.reshape(128, HD).astype(BF), w[HD * h : HD * h + HD, :], preferred_element_type=F32
        )
    out[...] = total.astype(BF)


def rotary_tables(positions):
    freq = (1.0 / 500000.0 ** (np.arange(0, HD, 2) / HD)).astype(np.float32)
    angles = positions.astype(F32)[:, None] * jnp.asarray(np.concatenate([freq, freq]), F32)[None, :]
    sign = np.concatenate([-np.ones(HD // 2), np.ones(HD // 2)]).astype(np.float32)
    return jnp.cos(angles), jnp.sin(angles) * jnp.asarray(sign)[None, :]


def on_device(
    hidden_in,
    norm_gain,
    w_query,
    w_keyval,
    w_out,
    prefix_keys,
    prefix_values,
    own_keys,
    own_values,
    positions,
    lengths,
):
    b, r = lax.axis_index("blk"), lax.axis_index("rows")
    who = jnp.stack([b, r]).astype(jnp.int32)
    sds = jax.ShapeDtypeStruct
    first_w = lax.ppermute(w_keyval, "rows", [(s, 2 * (s % 8) + s // 8) for s in range(16)])
    second_w = lax.ppermute(w_keyval, "rows", [(s, 2 * (s % 8) + 1 - s // 8) for s in range(16)])
    packed = pl.pallas_call(
        pack_body,
        out_shape=sds((16, END, HD), BF),
        in_specs=[SM, VM] + [pl.BlockSpec(memory_space=pltpu.HBM)] * 4,
        out_specs=pl.BlockSpec(memory_space=pltpu.HBM),
        scratch_shapes=[
            pltpu.VMEM((128, 1024), BF),
            pltpu.VMEM((128, 1024), BF),
            pltpu.VMEM((64, 1024), BF),
            pltpu.VMEM((64, 1024), BF),
            pltpu.VMEM((16, END, HD), BF),
            pltpu.SemaphoreType.DMA((8,)),
        ],
        name="pack",
    )(lengths, hidden_in, prefix_keys, prefix_values, own_keys.reshape(64, 1024), own_values.reshape(64, 1024))
    mine = lax.all_to_all(packed, "rows", 0, 0, tiled=True)
    cosine, sine = rotary_tables(jnp.concatenate([lax.dynamic_slice_in_dim(positions, 4 * b, 4, 0)] * 4))
    gain, cosine, sine = lax.optimization_barrier((norm_gain.reshape(1, 256), cosine, sine))
    x_spec = pl.BlockSpec((16, END - X0, HD), lambda i: (0, X0 // 16, 0))
    gain_spec = pl.BlockSpec((1, 256), lambda i: (0, 0))
    parts = pl.pallas_call(
        project_body,
        grid=(1,),
        out_shape=sds((768, HD), BF),
        in_specs=[x_spec, gain_spec, pl.BlockSpec((256, 512), lambda i: (0, 0))],
        out_specs=pl.BlockSpec((768, HD), lambda i: (0, 0)),
        compiler_params=params(),
        name="project",
    )(mine, gain, w_query)
    parts, mine = lax.optimization_barrier((parts, mine))
    parts = lax.all_to_all(parts, "blk", 0, 0, tiled=True)
    half, first_w, second_w = lax.optimization_barrier((mine[:, :X0, :], first_w, second_w))
    other = lax.ppermute(half, "rows", [(i, i ^ 1) for i in range(16)])
    keep, give = pl.pallas_call(
        keyval_body,
        grid=(1,),
        out_shape=(sds((128, HD), F32), sds((128, HD), BF)),
        in_specs=[SM, x_spec, gain_spec] + [pl.BlockSpec((256, HD), lambda i: (0, 0))] * 2,
        out_specs=[pl.BlockSpec((128, HD), lambda i: (0, 0))] * 2,
        compiler_params=params(),
        cost_estimate=pl.CostEstimate(flops=10**9, bytes_accessed=1 << 18, transcendentals=0),
        name="keyval",
    )(who, mine, gain, first_w, second_w)
    given = lax.ppermute(give, "blk", [(i, i ^ 1) for i in range(32)])
    query, q_own, row_scale = pl.pallas_call(
        query_body,
        out_shape=(sds((32, 16, HD), BF), sds((16, HD), BF), sds((16, HD), F32)),
        in_specs=[SM, VM, VM, VM],
        out_specs=(VM, VM, VM),
        compiler_params=params(),
        cost_estimate=pl.CostEstimate(flops=2*10**9, bytes_accessed=1 << 20, transcendentals=0),
        name="query",
    )(who, parts, cosine, sine)
    query = lax.all_to_all(query, "blk", 0, 0, tiled=True)
    partial = pl.pallas_call(
        attend_body,
        out_shape=sds((768, HD), BF),
        in_specs=[SM] + [VM] * 5,
        out_specs=VM,
        compiler_params=params(),
        name="attend",
    )(who, mine, other, query, keep, given)
    partial = lax.all_to_all(partial, "blk", 0, 0, tiled=True)
    attended = pl.pallas_call(
        combine_body,
        out_shape=sds((32, 16, HD), BF),
        in_specs=[SM] + [VM] * 5,
        out_specs=VM,
        compiler_params=params(),
        name="combine",
    )(who, partial, q_own, row_scale, cosine, sine)
    attended = lax.all_to_all(attended, "blk", 0, 0, tiled=True)
    mixed, kept = pl.pallas_call(
        output_body,
        out_shape=(sds((128, 256), BF), sds((8, 256), F32)),
        in_specs=[VM] * 3,
        out_specs=(VM, VM),
        compiler_params=params(),
        name="output",
    )(attended, w_out, hidden_in)
    mixed = lax.all_to_all(mixed.reshape(16, 8, 256), "rows", 0, 0, tiled=True)
    return (kept + jnp.sum(mixed.astype(F32), axis=0)).astype(BF)


def solution(mesh):
    return jax.shard_map(
        on_device,
        mesh=mesh,
        in_specs=(
            P("rows", "blk"),
            P("blk"),
            P("blk", "rows"),
            P("blk", "rows"),
            P("rows", "blk"),
            P(("blk", "rows"), None),
            P(("blk", "rows"), None),
            P("rows", "blk", None),
            P("rows", "blk", None),
            P(),
            P("rows"),
        ),
        out_specs=P("rows", "blk"),
        check_vma=False,
    )
```

```python
import jax
import jax.numpy as jnp
import numpy as np
from jax import lax
from jax.experimental import pallas as pl
from jax.experimental.pallas import tpu as pltpu
from jax.sharding import PartitionSpec as P

HD = 128
LOG2E = float(np.log2(np.e))
F32 = jnp.float32
BF = jnp.bfloat16
VM = pl.BlockSpec(memory_space=pltpu.VMEM)
SM = pl.BlockSpec(memory_space=pltpu.SMEM)
NT = (((1,), (1,)), ((), ()))
K0, V0, OK0, OV0, X0, END = 0, 64, 128, 160, 192, 208


def params(mib=48):
    return pltpu.CompilerParams(vmem_limit_bytes=mib * 1024 * 1024)


def iota(shape, dim):
    return lax.broadcasted_iota(jnp.int32, shape, dim)


def pack_body(lens, hidden, keys, values, own_k, own_v, out, packed, sems):
    outward = [
        pltpu.make_async_copy(packed.at[:, first:last, :], out.at[:, first:last, :], sems.at[i])
        for i, (first, last) in enumerate(((K0, V0), (V0, OK0), (OK0, OV0), (OV0, END)))
    ]
    places = [(2 * h + p, p, slice(h * HD, (h + 1) * HD)) for p in range(2) for h in range(8)]
    for d, p, col in places:
        packed[d, K0:V0, :] = keys[64 * p : 64 * p + 64, col]
    outward[0].start()
    for d, p, col in places:
        packed[d, V0:OK0, :] = values[64 * p : 64 * p + 64, col]
    outward[1].start()
    b = lax.axis_index("blk")
    sub = iota((32, HD), 0)
    slot = 8 * b + sub % 8
    dead = []
    for p in range(2):
        live = jnp.zeros((32, HD), jnp.int32)
        for k in range(4):
            live = jnp.where(sub // 8 == k, lens[4 * p + k], live)
        dead.append(slot >= live)
    for d, p, col in places:
        own = own_k[32 * p : 32 * p + 32, col].astype(F32)
        packed[d, OK0:OV0, :] = jnp.where(dead[p], jnp.nan, own).astype(BF)
    outward[2].start()
    x = hidden[...].astype(F32)
    x_tile = jnp.concatenate([x[:, :HD], x[:, HD:]], axis=0).astype(BF)
    for d, p, col in places:
        packed[d, OV0:X0, :] = own_v[32 * p : 32 * p + 32, col]
        packed[d, X0:END, :] = x_tile
    outward[3].start()
    for copy in outward:
        copy.wait()


def half_swap(x):
    return pltpu.roll(x, 4, 1)


def half_swap(x):
    return pltpu.roll(x, 4, 1)


def gathered_rows(x_ref):
    xr = x_ref[...].astype(F32)
    return jnp.concatenate(
        [xr[:, :8, :].reshape(128, HD), xr[:, 8:, :].reshape(128, HD)], axis=1
    )


def by_rows_of_four(blocks, p):
    blocks = [block.reshape(16, 8, HD) for block in blocks]
    low = iota((16, 8, HD), 1) < 4
    tiles = []
    for u in range(2):
        first, second = blocks[2 * u], blocks[2 * u + 1]
        if p == 0:
            tiles.append(jnp.where(low, first, half_swap(second)))
        else:
            tiles.append(jnp.where(low, half_swap(first), second))
    return tiles


def project_body(x_ref, gain, wq, out):
    x = gathered_rows(x_ref)
    square = lax.dot_general(
        jnp.ones((8, 2 * HD), F32), x * x, NT,
        precision=lax.Precision.HIGHEST, preferred_element_type=F32,
    )
    high = square.astype(BF).astype(F32)
    sub = iota((8, HD), 0)
    squares = jnp.where(sub == 0, high, jnp.where(sub == 1, square - high, 0.0))
    squares = jnp.broadcast_to(squares[None], (16, 8, HD))
    xg = (x * gain[...].astype(F32)).astype(BF)
    q = jnp.dot(xg, wq[...], preferred_element_type=F32)
    heads = [q[:, HD * h : HD * h + HD] for h in range(4)]
    tiles = by_rows_of_four(heads, 0) + [squares] + by_rows_of_four(heads, 1) + [squares]
    out[...] = jnp.concatenate(tiles, axis=1).reshape(768, HD).astype(BF)


def keyval_body(who, x_ref, gain, wa, wb, keep, give):
    xg = (gathered_rows(x_ref) * gain[...].astype(F32)).astype(BF)
    first = jnp.dot(xg, wa[...], preferred_element_type=F32)
    second = jnp.dot(xg, wb[...], preferred_element_type=F32)
    same = lax.rem(who[0], 2) == lax.rem(who[1], 2)
    keep[...] = jnp.where(same, first, second)
    give[...] = jnp.where(same, second, first).astype(BF)


def rotate(u, cosine, sine):
    return u * cosine + pltpu.roll(u, HD // 2, 1) * sine


def query_body(who, parts, cosine, sine, q_out, q_own, scale_out):
    total = jnp.sum(parts[...].astype(F32).reshape(32, 24, HD), axis=0)
    square = total[16:17, :] + total[17:18, :]
    inv = lax.rsqrt(square / 8192.0 + 1e-05)
    lane, sub = iota((16, HD), 1), iota((16, HD), 0)
    col = jnp.sum(jnp.where(lane == 4 * who[0] + sub % 4, inv, 0.0), axis=1, keepdims=True)
    scale_out[...] = jnp.broadcast_to(col, (16, HD))
    raw = (total[0:16, :] * col).astype(BF).astype(F32)
    query = rotate(raw, cosine[...], sine[...]).astype(BF)
    q_own[...] = query
    for i in range(q_out.shape[0]):
        q_out[i, :, :] = query


def attend_body(who, mine, other, q_ref, keep, given, out):
    r = who[1]
    scale = HD ** (-0.5) * LOG2E
    sources = (mine, other)
    halves = (lax.rem(r, 2), 1 - lax.rem(r, 2))
    rows = 256
    row_q, lane = iota((128, HD), 0), iota((128, HD), 1)
    row_q = 4 * (row_q // 16) + row_q % 4
    lane_s = iota((rows, HD), 1)
    sub_s = iota((8, HD), 0)
    kv = (keep[...] + given[...].astype(F32)).reshape(16, 8, HD)
    kv_swapped = half_swap(kv)
    for t in range(512 // rows):
        part = slice(rows // 16 * t, rows // 16 * (t + 1))
        q = q_ref[part].reshape(rows, HD)
        scores, vals = [], []
        for s in sources:
            k = s[:, K0:V0, :].reshape(1024, HD)
            scores.append(lax.dot_general(q, k, NT, preferred_element_type=F32))
            vals.append(s[:, V0:OK0, :].reshape(1024, HD))
        own_scores, own_vals = [], []
        for s, half in zip(sources, halves):
            row_k = 8 * (lane // 32) + 4 * half + (lane % 32) // 8
            blocks, block_vals = [], []
            for u in range(rows // 128):
                first = 4 * (t * (rows // 128) + u)
                k = s[first : first + 4, OK0:OV0, :].reshape(128, HD)
                block_vals.append(s[first : first + 4, OV0:X0, :].reshape(128, HD))
                sc = lax.dot_general(q[128 * u : 128 * u + 128], k, NT, preferred_element_type=F32)
                blocks.append(jnp.where((row_k == row_q) & (sc == sc), sc, -jnp.inf))
            own_scores.append(jnp.concatenate(blocks, axis=0))
            own_vals.append(block_vals)
        peak = jnp.max(scores[0], axis=1, keepdims=True)
        for sc in scores[1:] + own_scores:
            peak = jnp.maximum(peak, jnp.max(sc, axis=1, keepdims=True))
        peak = peak * scale
        high = peak.astype(BF).astype(F32)
        low = (peak - high).astype(BF).astype(F32)
        shift = high + low
        mass = jnp.zeros((rows, 1), F32)
        acc = jnp.zeros((rows, HD), F32)
        for sc, v in zip(scores, vals):
            w = jnp.exp2(sc * scale - shift)
            mass = mass + jnp.sum(w, axis=1, keepdims=True)
            acc = acc + jnp.dot(w.astype(BF), v, preferred_element_type=F32)
        for sc, block_vals in zip(own_scores, own_vals):
            w = jnp.exp2(sc * scale - shift)
            mass = mass + jnp.sum(w, axis=1, keepdims=True)
            w = w.astype(BF)
            acc = acc + jnp.concatenate(
                [
                    jnp.dot(w[128 * u : 128 * u + 128], v, preferred_element_type=F32)
                    for u, v in enumerate(block_vals)
                ],
                axis=0,
            )
        mass_high = mass.astype(BF).astype(F32)
        stats = jnp.where(
            lane_s == 0, high, jnp.where(lane_s == 1, low, jnp.where(lane_s == 2, mass_high, mass - mass_high))
        )
        stats = jnp.where(lane_s < 4, stats, 0.0)
        for u in range(rows // 128):
            turned = pltpu.roll(stats[128 * u : 128 * u + 128, :].T[0:8, :], 4, 0)
            for i in range(4):
                pair = rows // 32 * t + 4 * u + i
                first = 128 * u + 32 * i
                tiles = [
                    acc[first : first + 16, :],
                    jnp.where(sub_s < 4, kv[pair], turned),
                    acc[first + 16 : first + 32, :],
                    jnp.where(sub_s < 4, kv_swapped[pair], turned),
                ]
                out[48 * pair : 48 * pair + 48, :] = jnp.concatenate(tiles, axis=0).astype(BF)


def twice(tile):
    tile = jnp.where(iota((8, HD), 0) < 4, tile, pltpu.roll(tile, 4, 0))
    return jnp.concatenate([tile, tile], axis=0)


def combine_body(who, parts, q_own, scale, cosine, sine, out):
    parts = parts[...].astype(F32).reshape(32, 24, HD)
    rest = parts[:, 16:24, :].reshape(16, 2, 8, HD)
    new_k = (twice(jnp.sum(rest[:, 0], axis=0)) * scale[...]).astype(BF).astype(F32)
    new_k = rotate(new_k, cosine[...], sine[...]).astype(BF).astype(F32)
    new_v = (twice(jnp.sum(rest[:, 1], axis=0)) * scale[...]).astype(BF).astype(F32)
    new = jnp.sum(q_own[...].astype(F32) * new_k, axis=1, keepdims=True) * (HD ** (-0.5) * LOG2E)
    mine = iota((16, HD), 1) == 16 * lax.rem(who[0], 8) + iota((16, HD), 0)
    rest = parts[:, 16:24, :]
    peak = rest[:, 4:5, :] + rest[:, 5:6, :]
    mass = rest[:, 6:7, :] + rest[:, 7:8, :]
    top = jnp.max(peak, axis=0)
    shrink = jnp.exp2(peak - top[None])
    whole = jnp.sum(mass * shrink, axis=0)
    share = jnp.sum(jnp.where(mine[None], shrink, 0.0), axis=2, keepdims=True)
    summed = jnp.sum(parts[:, 0:16, :] * share, axis=0)
    top = jnp.sum(jnp.where(mine, top, 0.0), axis=1, keepdims=True)
    whole = jnp.sum(jnp.where(mine, whole, 0.0), axis=1, keepdims=True)
    over = jnp.maximum(top, new)
    old_w, new_w = jnp.exp2(top - over), jnp.exp2(new - over)
    attended = ((summed * old_w + new_w * new_v) / (whole * old_w + new_w)).astype(BF)
    for i in range(out.shape[0]):
        out[i, :, :] = attended


def output_body(att, w, hidden, out, kept):
    kept[...] = hidden[...].astype(F32)
    tiles = att[...].astype(F32).reshape(16, 2, 2, 8, HD)
    low = iota((16, 8, HD), 1) < 4
    total = jnp.zeros(out.shape, F32)
    for h in range(4):
        first, second = tiles[:, 0, h // 2], tiles[:, 1, h // 2]
        if h % 2 == 0:
            rows = jnp.where(low, first, half_swap(second))
        else:
            rows = jnp.where(low, half_swap(first), second)
        total = total + jnp.dot(
            rows.reshape(128, HD).astype(BF), w[HD * h : HD * h + HD, :], preferred_element_type=F32
        )
    out[...] = total.astype(BF)


def rotary_tables(positions):
    freq = (1.0 / 500000.0 ** (np.arange(0, HD, 2) / HD)).astype(np.float32)
    angles = positions.astype(F32)[:, None] * jnp.asarray(np.concatenate([freq, freq]), F32)[None, :]
    sign = np.concatenate([-np.ones(HD // 2), np.ones(HD // 2)]).astype(np.float32)
    return jnp.cos(angles), jnp.sin(angles) * jnp.asarray(sign)[None, :]


def on_device(
    hidden_in,
    norm_gain,
    w_query,
    w_keyval,
    w_out,
    prefix_keys,
    prefix_values,
    own_keys,
    own_values,
    positions,
    lengths,
):
    b, r = lax.axis_index("blk"), lax.axis_index("rows")
    who = jnp.stack([b, r]).astype(jnp.int32)
    sds = jax.ShapeDtypeStruct
    first_w = lax.ppermute(w_keyval, "rows", [(s, 2 * (s % 8) + s // 8) for s in range(16)])
    second_w = lax.ppermute(w_keyval, "rows", [(s, 2 * (s % 8) + 1 - s // 8) for s in range(16)])
    packed = pl.pallas_call(
        pack_body,
        out_shape=sds((16, END, HD), BF),
        in_specs=[SM] + [VM] * 5,
        out_specs=pl.BlockSpec(memory_space=pltpu.HBM),
        scratch_shapes=[
            pltpu.VMEM((16, END, HD), BF),
            pltpu.SemaphoreType.DMA((4,)),
        ],
        name="pack",
    )(lengths, hidden_in, prefix_keys, prefix_values, own_keys.reshape(64, 1024), own_values.reshape(64, 1024))
    mine = lax.all_to_all(packed, "rows", 0, 0, tiled=True)
    cosine, sine = rotary_tables(jnp.concatenate([lax.dynamic_slice_in_dim(positions, 4 * b, 4, 0)] * 4))
    gain, cosine, sine = lax.optimization_barrier((norm_gain.reshape(1, 256), cosine, sine))
    x_spec = pl.BlockSpec((16, END - X0, HD), lambda i: (0, X0 // 16, 0))
    gain_spec = pl.BlockSpec((1, 256), lambda i: (0, 0))
    parts = pl.pallas_call(
        project_body,
        grid=(1,),
        out_shape=sds((768, HD), BF),
        in_specs=[x_spec, gain_spec, pl.BlockSpec((256, 512), lambda i: (0, 0))],
        out_specs=pl.BlockSpec((768, HD), lambda i: (0, 0)),
        compiler_params=params(),
        name="project",
    )(mine, gain, w_query)
    parts, mine = lax.optimization_barrier((parts, mine))
    parts = lax.all_to_all(parts, "blk", 0, 0, tiled=True)
    half, first_w, second_w = lax.optimization_barrier((mine[:, :X0, :], first_w, second_w))
    other = lax.ppermute(half, "rows", [(i, i ^ 1) for i in range(16)])
    keep, give = pl.pallas_call(
        keyval_body,
        grid=(1,),
        out_shape=(sds((128, HD), F32), sds((128, HD), BF)),
        in_specs=[SM, x_spec, gain_spec] + [pl.BlockSpec((256, HD), lambda i: (0, 0))] * 2,
        out_specs=[pl.BlockSpec((128, HD), lambda i: (0, 0))] * 2,
        compiler_params=params(),
        cost_estimate=pl.CostEstimate(flops=10**9, bytes_accessed=1 << 18, transcendentals=0),
        name="keyval",
    )(who, mine, gain, first_w, second_w)
    given = lax.ppermute(give, "blk", [(i, i ^ 1) for i in range(32)])
    query, q_own, row_scale = pl.pallas_call(
        query_body,
        out_shape=(sds((32, 16, HD), BF), sds((16, HD), BF), sds((16, HD), F32)),
        in_specs=[SM, VM, VM, VM],
        out_specs=(VM, VM, VM),
        compiler_params=params(),
        cost_estimate=pl.CostEstimate(flops=2*10**9, bytes_accessed=1 << 20, transcendentals=0),
        name="query",
    )(who, parts, cosine, sine)
    query = lax.all_to_all(query, "blk", 0, 0, tiled=True)
    partial = pl.pallas_call(
        attend_body,
        out_shape=sds((768, HD), BF),
        in_specs=[SM] + [VM] * 5,
        out_specs=VM,
        compiler_params=params(),
        name="attend",
    )(who, mine, other, query, keep, given)
    partial = lax.all_to_all(partial, "blk", 0, 0, tiled=True)
    attended = pl.pallas_call(
        combine_body,
        out_shape=sds((32, 16, HD), BF),
        in_specs=[SM] + [VM] * 5,
        out_specs=VM,
        compiler_params=params(),
        name="combine",
    )(who, partial, q_own, row_scale, cosine, sine)
    attended = lax.all_to_all(attended, "blk", 0, 0, tiled=True)
    mixed, kept = pl.pallas_call(
        output_body,
        out_shape=(sds((128, 256), BF), sds((8, 256), F32)),
        in_specs=[VM] * 3,
        out_specs=(VM, VM),
        compiler_params=params(),
        name="output",
    )(attended, w_out, hidden_in)
    mixed = lax.all_to_all(mixed.reshape(16, 8, 256), "rows", 0, 0, tiled=True)
    return (kept + jnp.sum(mixed.astype(F32), axis=0)).astype(BF)


def solution(mesh):
    return jax.shard_map(
        on_device,
        mesh=mesh,
        in_specs=(
            P("rows", "blk"),
            P("blk"),
            P("blk", "rows"),
            P("blk", "rows"),
            P("rows", "blk"),
            P(("blk", "rows"), None),
            P(("blk", "rows"), None),
            P("rows", "blk", None),
            P("rows", "blk", None),
            P(),
            P("rows"),
        ),
        out_specs=P("rows", "blk"),
        check_vma=False,
    )
```

```python
import jax
import jax.numpy as jnp
import numpy as np
from jax import lax
from jax.experimental import pallas as pl
from jax.experimental.pallas import tpu as pltpu
from jax.sharding import PartitionSpec as P

HD = 128
LOG2E = float(np.log2(np.e))
F32 = jnp.float32
BF = jnp.bfloat16
VM = pl.BlockSpec(memory_space=pltpu.VMEM)
SM = pl.BlockSpec(memory_space=pltpu.SMEM)
NT = (((1,), (1,)), ((), ()))
K0, V0, OK0, OV0, X0, END = 0, 64, 128, 160, 192, 208


def params(mib=48):
    return pltpu.CompilerParams(vmem_limit_bytes=mib * 1024 * 1024)


def iota(shape, dim):
    return lax.broadcasted_iota(jnp.int32, shape, dim)


def pack_body(lens, hidden, keys, values, own_k, own_v, out, packed, sems):
    outward = [
        pltpu.make_async_copy(packed.at[:, first:last, :], out.at[:, first:last, :], sems.at[i])
        for i, (first, last) in enumerate(((K0, V0), (V0, OK0), (OK0, OV0), (OV0, END)))
    ]
    places = [(2 * h + p, p, slice(h * HD, (h + 1) * HD)) for p in range(2) for h in range(8)]
    for d, p, col in places:
        packed[d, K0:V0, :] = keys[64 * p : 64 * p + 64, col]
    outward[0].start()
    for d, p, col in places:
        packed[d, V0:OK0, :] = values[64 * p : 64 * p + 64, col]
    outward[1].start()
    b = lax.axis_index("blk")
    sub = iota((32, HD), 0)
    slot = 8 * b + sub % 8
    dead = []
    for p in range(2):
        live = jnp.zeros((32, HD), jnp.int32)
        for k in range(4):
            live = jnp.where(sub // 8 == k, lens[4 * p + k], live)
        dead.append(slot >= live)
    for d, p, col in places:
        own = own_k[32 * p : 32 * p + 32, col].astype(F32)
        packed[d, OK0:OV0, :] = jnp.where(dead[p], jnp.nan, own).astype(BF)
    outward[2].start()
    x = hidden[...].astype(F32)
    x_tile = jnp.concatenate([x[:, :HD], x[:, HD:]], axis=0).astype(BF)
    for d, p, col in places:
        packed[d, OV0:X0, :] = own_v[32 * p : 32 * p + 32, col]
        packed[d, X0:END, :] = x_tile
    outward[3].start()
    for copy in outward:
        copy.wait()


def half_swap(x):
    return pltpu.roll(x, 4, 1)


def half_swap(x):
    return pltpu.roll(x, 4, 1)


def gathered_rows(x_ref):
    xr = x_ref[...].astype(F32)
    return jnp.concatenate(
        [xr[:, :8, :].reshape(128, HD), xr[:, 8:, :].reshape(128, HD)], axis=1
    )


def by_rows_of_four(blocks, p):
    blocks = [block.reshape(16, 8, HD) for block in blocks]
    low = iota((16, 8, HD), 1) < 4
    tiles = []
    for u in range(2):
        first, second = blocks[2 * u], blocks[2 * u + 1]
        if p == 0:
            tiles.append(jnp.where(low, first, half_swap(second)))
        else:
            tiles.append(jnp.where(low, half_swap(first), second))
    return tiles


def project_body(x_ref, gain, wq, out):
    x = gathered_rows(x_ref)
    square = lax.dot_general(
        jnp.ones((8, 2 * HD), F32), x * x, NT,
        precision=lax.Precision.HIGHEST, preferred_element_type=F32,
    )
    high = square.astype(BF).astype(F32)
    sub = iota((8, HD), 0)
    squares = jnp.where(sub == 0, high, jnp.where(sub == 1, square - high, 0.0))
    squares = jnp.broadcast_to(squares[None], (16, 8, HD))
    xg = (x * gain[...].astype(F32)).astype(BF)
    q = jnp.dot(xg, wq[...], preferred_element_type=F32)
    heads = [q[:, HD * h : HD * h + HD] for h in range(4)]
    tiles = by_rows_of_four(heads, 0) + [squares] + by_rows_of_four(heads, 1) + [squares]
    out[...] = jnp.concatenate(tiles, axis=1).reshape(768, HD).astype(BF)


def keyval_body(who, x_ref, gain, wa, wb, keep, give):
    xg = (gathered_rows(x_ref) * gain[...].astype(F32)).astype(BF)
    first = jnp.dot(xg, wa[...], preferred_element_type=F32)
    second = jnp.dot(xg, wb[...], preferred_element_type=F32)
    same = lax.rem(who[0], 2) == lax.rem(who[1], 2)
    keep[...] = jnp.where(same, first, second)
    give[...] = jnp.where(same, second, first).astype(BF)


def rotate(u, cosine, sine):
    return u * cosine + pltpu.roll(u, HD // 2, 1) * sine


def query_body(who, parts, cosine, sine, q_out, q_own, scale_out):
    total = jnp.sum(parts[...].astype(F32).reshape(32, 24, HD), axis=0)
    square = total[16:17, :] + total[17:18, :]
    inv = lax.rsqrt(square / 8192.0 + 1e-05)
    lane, sub = iota((16, HD), 1), iota((16, HD), 0)
    col = jnp.sum(jnp.where(lane == 4 * who[0] + sub % 4, inv, 0.0), axis=1, keepdims=True)
    scale_out[...] = jnp.broadcast_to(col, (16, HD))
    raw = (total[0:16, :] * col).astype(BF).astype(F32)
    query = rotate(raw, cosine[...], sine[...]).astype(BF)
    q_own[...] = query
    for i in range(q_out.shape[0]):
        q_out[i, :, :] = query


def attend_body(who, mine, other, q_ref, keep, given, out):
    r = who[1]
    scale = HD ** (-0.5) * LOG2E
    sources = (mine, other)
    halves = (lax.rem(r, 2), 1 - lax.rem(r, 2))
    rows = 128
    ones = jnp.ones((1024, HD), BF)
    row_q, lane = iota((128, HD), 0), iota((128, HD), 1)
    row_q = 4 * (row_q // 16) + row_q % 4
    lane_s = iota((rows, HD), 1)
    sub_s = iota((8, HD), 0)
    kv = (keep[...] + given[...].astype(F32)).reshape(16, 8, HD)
    kv_swapped = half_swap(kv)
    for t in range(512 // rows):
        part = slice(rows // 16 * t, rows // 16 * (t + 1))
        q = q_ref[part].reshape(rows, HD)
        scores, vals = [], []
        for s in sources:
            k = s[:, K0:V0, :].reshape(1024, HD)
            scores.append(lax.dot_general(q, k, NT, preferred_element_type=F32))
            vals.append(jnp.concatenate([s[:, V0:OK0, :].reshape(1024, HD), ones], axis=1))
        own_scores, own_vals = [], []
        for s, half in zip(sources, halves):
            row_k = 8 * (lane // 32) + 4 * half + (lane % 32) // 8
            blocks, block_vals = [], []
            for u in range(rows // 128):
                first = 4 * (t * (rows // 128) + u)
                k = s[first : first + 4, OK0:OV0, :].reshape(128, HD)
                v = s[first : first + 4, OV0:X0, :].reshape(128, HD)
                block_vals.append(jnp.concatenate([v, ones[0:128, :]], axis=1))
                sc = lax.dot_general(q[128 * u : 128 * u + 128], k, NT, preferred_element_type=F32)
                blocks.append(jnp.where((row_k == row_q) & (sc == sc), sc, -jnp.inf))
            own_scores.append(jnp.concatenate(blocks, axis=0))
            own_vals.append(block_vals)
        peak = jnp.max(scores[0], axis=1, keepdims=True)
        for sc in scores[1:] + own_scores:
            peak = jnp.maximum(peak, jnp.max(sc, axis=1, keepdims=True))
        peak = peak * scale
        high = peak.astype(BF).astype(F32)
        low = (peak - high).astype(BF).astype(F32)
        shift = high + low
        acc = jnp.zeros((rows, 2 * HD), F32)
        for sc, v in zip(scores, vals):
            w = jnp.exp2(sc * scale - shift)
            acc = acc + jnp.dot(w.astype(BF), v, preferred_element_type=F32)
        for sc, block_vals in zip(own_scores, own_vals):
            w = jnp.exp2(sc * scale - shift)
            w = w.astype(BF)
            acc = acc + jnp.concatenate(
                [
                    jnp.dot(w[128 * u : 128 * u + 128], v, preferred_element_type=F32)
                    for u, v in enumerate(block_vals)
                ],
                axis=0,
            )
        mass, acc = acc[:, HD:], acc[:, :HD]
        mass_high = mass.astype(BF).astype(F32)
        stats = jnp.where(
            lane_s == 0, high, jnp.where(lane_s == 1, low, jnp.where(lane_s == 2, mass_high, mass - mass_high))
        )
        stats = jnp.where(lane_s < 4, stats, 0.0)
        for u in range(rows // 128):
            turned = pltpu.roll(stats[128 * u : 128 * u + 128, :].T[0:8, :], 4, 0)
            for i in range(4):
                pair = rows // 32 * t + 4 * u + i
                first = 128 * u + 32 * i
                tiles = [
                    acc[first : first + 16, :],
                    jnp.where(sub_s < 4, kv[pair], turned),
                    acc[first + 16 : first + 32, :],
                    jnp.where(sub_s < 4, kv_swapped[pair], turned),
                ]
                out[48 * pair : 48 * pair + 48, :] = jnp.concatenate(tiles, axis=0).astype(BF)


def twice(tile):
    tile = jnp.where(iota((8, HD), 0) < 4, tile, pltpu.roll(tile, 4, 0))
    return jnp.concatenate([tile, tile], axis=0)


def combine_body(who, parts, q_own, scale, cosine, sine, out):
    parts = parts[...].astype(F32).reshape(32, 24, HD)
    rest = parts[:, 16:24, :].reshape(16, 2, 8, HD)
    new_k = (twice(jnp.sum(rest[:, 0], axis=0)) * scale[...]).astype(BF).astype(F32)
    new_k = rotate(new_k, cosine[...], sine[...]).astype(BF).astype(F32)
    new_v = (twice(jnp.sum(rest[:, 1], axis=0)) * scale[...]).astype(BF).astype(F32)
    new = jnp.sum(q_own[...].astype(F32) * new_k, axis=1, keepdims=True) * (HD ** (-0.5) * LOG2E)
    mine = iota((16, HD), 1) == 16 * lax.rem(who[0], 8) + iota((16, HD), 0)
    rest = parts[:, 16:24, :]
    peak = rest[:, 4:5, :] + rest[:, 5:6, :]
    mass = rest[:, 6:7, :] + rest[:, 7:8, :]
    top = jnp.max(peak, axis=0)
    shrink = jnp.exp2(peak - top[None])
    whole = jnp.sum(mass * shrink, axis=0)
    share = jnp.sum(jnp.where(mine[None], shrink, 0.0), axis=2, keepdims=True)
    summed = jnp.sum(parts[:, 0:16, :] * share, axis=0)
    top = jnp.sum(jnp.where(mine, top, 0.0), axis=1, keepdims=True)
    whole = jnp.sum(jnp.where(mine, whole, 0.0), axis=1, keepdims=True)
    over = jnp.maximum(top, new)
    old_w, new_w = jnp.exp2(top - over), jnp.exp2(new - over)
    attended = ((summed * old_w + new_w * new_v) / (whole * old_w + new_w)).astype(BF)
    for i in range(out.shape[0]):
        out[i, :, :] = attended


def output_body(att, w, hidden, out, kept):
    kept[...] = hidden[...].astype(F32)
    tiles = att[...].astype(F32).reshape(16, 2, 2, 8, HD)
    low = iota((16, 8, HD), 1) < 4
    total = jnp.zeros(out.shape, F32)
    for h in range(4):
        first, second = tiles[:, 0, h // 2], tiles[:, 1, h // 2]
        if h % 2 == 0:
            rows = jnp.where(low, first, half_swap(second))
        else:
            rows = jnp.where(low, half_swap(first), second)
        total = total + jnp.dot(
            rows.reshape(128, HD).astype(BF), w[HD * h : HD * h + HD, :], preferred_element_type=F32
        )
    out[...] = total.astype(BF)


def rotary_tables(positions):
    freq = (1.0 / 500000.0 ** (np.arange(0, HD, 2) / HD)).astype(np.float32)
    angles = positions.astype(F32)[:, None] * jnp.asarray(np.concatenate([freq, freq]), F32)[None, :]
    sign = np.concatenate([-np.ones(HD // 2), np.ones(HD // 2)]).astype(np.float32)
    return jnp.cos(angles), jnp.sin(angles) * jnp.asarray(sign)[None, :]


def on_device(
    hidden_in,
    norm_gain,
    w_query,
    w_keyval,
    w_out,
    prefix_keys,
    prefix_values,
    own_keys,
    own_values,
    positions,
    lengths,
):
    b, r = lax.axis_index("blk"), lax.axis_index("rows")
    who = jnp.stack([b, r]).astype(jnp.int32)
    sds = jax.ShapeDtypeStruct
    first_w = lax.ppermute(w_keyval, "rows", [(s, 2 * (s % 8) + s // 8) for s in range(16)])
    second_w = lax.ppermute(w_keyval, "rows", [(s, 2 * (s % 8) + 1 - s // 8) for s in range(16)])
    packed = pl.pallas_call(
        pack_body,
        out_shape=sds((16, END, HD), BF),
        in_specs=[SM] + [VM] * 5,
        out_specs=pl.BlockSpec(memory_space=pltpu.HBM),
        scratch_shapes=[
            pltpu.VMEM((16, END, HD), BF),
            pltpu.SemaphoreType.DMA((4,)),
        ],
        name="pack",
    )(lengths, hidden_in, prefix_keys, prefix_values, own_keys.reshape(64, 1024), own_values.reshape(64, 1024))
    mine = lax.all_to_all(packed, "rows", 0, 0, tiled=True)
    cosine, sine = rotary_tables(jnp.concatenate([lax.dynamic_slice_in_dim(positions, 4 * b, 4, 0)] * 4))
    gain, cosine, sine = lax.optimization_barrier((norm_gain.reshape(1, 256), cosine, sine))
    x_spec = pl.BlockSpec((16, END - X0, HD), lambda i: (0, X0 // 16, 0))
    gain_spec = pl.BlockSpec((1, 256), lambda i: (0, 0))
    parts = pl.pallas_call(
        project_body,
        grid=(1,),
        out_shape=sds((768, HD), BF),
        in_specs=[x_spec, gain_spec, pl.BlockSpec((256, 512), lambda i: (0, 0))],
        out_specs=pl.BlockSpec((768, HD), lambda i: (0, 0)),
        compiler_params=params(),
        name="project",
    )(mine, gain, w_query)
    parts, mine = lax.optimization_barrier((parts, mine))
    parts = lax.all_to_all(parts, "blk", 0, 0, tiled=True)
    half, first_w, second_w = lax.optimization_barrier((mine[:, :X0, :], first_w, second_w))
    other = lax.ppermute(half, "rows", [(i, i ^ 1) for i in range(16)])
    keep, give = pl.pallas_call(
        keyval_body,
        grid=(1,),
        out_shape=(sds((128, HD), F32), sds((128, HD), BF)),
        in_specs=[SM, x_spec, gain_spec] + [pl.BlockSpec((256, HD), lambda i: (0, 0))] * 2,
        out_specs=[pl.BlockSpec((128, HD), lambda i: (0, 0))] * 2,
        compiler_params=params(),
        cost_estimate=pl.CostEstimate(flops=10**9, bytes_accessed=1 << 18, transcendentals=0),
        name="keyval",
    )(who, mine, gain, first_w, second_w)
    given = lax.ppermute(give, "blk", [(i, i ^ 1) for i in range(32)])
    query, q_own, row_scale = pl.pallas_call(
        query_body,
        out_shape=(sds((32, 16, HD), BF), sds((16, HD), BF), sds((16, HD), F32)),
        in_specs=[SM, VM, VM, VM],
        out_specs=(VM, VM, VM),
        compiler_params=params(),
        cost_estimate=pl.CostEstimate(flops=2*10**9, bytes_accessed=1 << 20, transcendentals=0),
        name="query",
    )(who, parts, cosine, sine)
    query = lax.all_to_all(query, "blk", 0, 0, tiled=True)
    partial = pl.pallas_call(
        attend_body,
        out_shape=sds((768, HD), BF),
        in_specs=[SM] + [VM] * 5,
        out_specs=VM,
        compiler_params=params(),
        name="attend",
    )(who, mine, other, query, keep, given)
    partial = lax.all_to_all(partial, "blk", 0, 0, tiled=True)
    attended = pl.pallas_call(
        combine_body,
        out_shape=sds((32, 16, HD), BF),
        in_specs=[SM] + [VM] * 5,
        out_specs=VM,
        compiler_params=params(),
        name="combine",
    )(who, partial, q_own, row_scale, cosine, sine)
    attended = lax.all_to_all(attended, "blk", 0, 0, tiled=True)
    mixed, kept = pl.pallas_call(
        output_body,
        out_shape=(sds((128, 256), BF), sds((8, 256), F32)),
        in_specs=[VM] * 3,
        out_specs=(VM, VM),
        compiler_params=params(),
        name="output",
    )(attended, w_out, hidden_in)
    mixed = lax.all_to_all(mixed.reshape(16, 8, 256), "rows", 0, 0, tiled=True)
    return (kept + jnp.sum(mixed.astype(F32), axis=0)).astype(BF)


def solution(mesh):
    return jax.shard_map(
        on_device,
        mesh=mesh,
        in_specs=(
            P("rows", "blk"),
            P("blk"),
            P("blk", "rows"),
            P("blk", "rows"),
            P("rows", "blk"),
            P(("blk", "rows"), None),
            P(("blk", "rows"), None),
            P("rows", "blk", None),
            P("rows", "blk", None),
            P(),
            P("rows"),
        ),
        out_specs=P("rows", "blk"),
        check_vma=False,
    )
```

```python
import jax
import jax.numpy as jnp
import numpy as np
from jax import lax
from jax.experimental import pallas as pl
from jax.experimental.pallas import tpu as pltpu
from jax.sharding import PartitionSpec as P

HD = 128
LOG2E = float(np.log2(np.e))
F32 = jnp.float32
BF = jnp.bfloat16
VM = pl.BlockSpec(memory_space=pltpu.VMEM)
SM = pl.BlockSpec(memory_space=pltpu.SMEM)
NT = (((1,), (1,)), ((), ()))
K0, V0, OK0, OV0, X0, END = 0, 64, 128, 160, 192, 208


def params(mib=48):
    return pltpu.CompilerParams(vmem_limit_bytes=mib * 1024 * 1024)


def iota(shape, dim):
    return lax.broadcasted_iota(jnp.int32, shape, dim)


def pack_body(lens, hidden, keys, values, own_k, own_v, out, packed, sems):
    outward = [
        pltpu.make_async_copy(packed.at[:, first:last, :], out.at[:, first:last, :], sems.at[i])
        for i, (first, last) in enumerate(((K0, V0), (V0, OK0), (OK0, OV0), (OV0, END)))
    ]
    places = [(2 * h + p, p, slice(h * HD, (h + 1) * HD)) for p in range(2) for h in range(8)]
    for d, p, col in places:
        packed[d, K0:V0, :] = keys[64 * p : 64 * p + 64, col]
    outward[0].start()
    for d, p, col in places:
        packed[d, V0:OK0, :] = values[64 * p : 64 * p + 64, col]
    outward[1].start()
    b = lax.axis_index("blk")
    sub = iota((32, HD), 0)
    slot = 8 * b + sub % 8
    dead = []
    for p in range(2):
        live = jnp.zeros((32, HD), jnp.int32)
        for k in range(4):
            live = jnp.where(sub // 8 == k, lens[4 * p + k], live)
        dead.append(slot >= live)
    for d, p, col in places:
        own = own_k[32 * p : 32 * p + 32, col].astype(F32)
        packed[d, OK0:OV0, :] = jnp.where(dead[p], jnp.nan, own).astype(BF)
    outward[2].start()
    x = hidden[...].astype(F32)
    x_tile = jnp.concatenate([x[:, :HD], x[:, HD:]], axis=0).astype(BF)
    for d, p, col in places:
        packed[d, OV0:X0, :] = own_v[32 * p : 32 * p + 32, col]
        packed[d, X0:END, :] = x_tile
    outward[3].start()
    for copy in outward:
        copy.wait()


def half_swap(x):
    return pltpu.roll(x, 4, 1)


def half_swap(x):
    return pltpu.roll(x, 4, 1)


def gathered_rows(x_ref):
    xr = x_ref[...].astype(F32)
    return jnp.concatenate(
        [xr[:, :8, :].reshape(128, HD), xr[:, 8:, :].reshape(128, HD)], axis=1
    )


def by_rows_of_four(blocks, p):
    blocks = [block.reshape(16, 8, HD) for block in blocks]
    low = iota((16, 8, HD), 1) < 4
    tiles = []
    for u in range(2):
        first, second = blocks[2 * u], blocks[2 * u + 1]
        if p == 0:
            tiles.append(jnp.where(low, first, half_swap(second)))
        else:
            tiles.append(jnp.where(low, half_swap(first), second))
    return tiles


def project_body(x_ref, gain, wq, out):
    x = gathered_rows(x_ref)
    square = lax.dot_general(
        jnp.ones((8, 2 * HD), F32), x * x, NT,
        precision=lax.Precision.HIGHEST, preferred_element_type=F32,
    )
    high = square.astype(BF).astype(F32)
    sub = iota((8, HD), 0)
    squares = jnp.where(sub == 0, high, jnp.where(sub == 1, square - high, 0.0))
    squares = jnp.broadcast_to(squares[None], (16, 8, HD))
    xg = (x * gain[...].astype(F32)).astype(BF)
    q = jnp.dot(xg, wq[...], preferred_element_type=F32)
    heads = [q[:, HD * h : HD * h + HD] for h in range(4)]
    tiles = by_rows_of_four(heads, 0) + [squares] + by_rows_of_four(heads, 1) + [squares]
    out[...] = jnp.concatenate(tiles, axis=1).reshape(768, HD).astype(BF)


def keyval_body(who, x_ref, gain, wa, wb, keep, give):
    xg = (gathered_rows(x_ref) * gain[...].astype(F32)).astype(BF)
    first = jnp.dot(xg, wa[...], preferred_element_type=F32)
    second = jnp.dot(xg, wb[...], preferred_element_type=F32)
    same = lax.rem(who[0], 2) == lax.rem(who[1], 2)
    keep[...] = jnp.where(same, first, second)
    give[...] = jnp.where(same, second, first).astype(BF)


def rotate(u, cosine, sine):
    return u * cosine + pltpu.roll(u, HD // 2, 1) * sine


def query_body(who, parts, cosine, sine, q_out, q_own, scale_out):
    total = jnp.sum(parts[...].astype(F32).reshape(32, 24, HD), axis=0)
    square = total[16:17, :] + total[17:18, :]
    inv = lax.rsqrt(square / 8192.0 + 1e-05)
    lane, sub = iota((16, HD), 1), iota((16, HD), 0)
    col = jnp.sum(jnp.where(lane == 4 * who[0] + sub % 4, inv, 0.0), axis=1, keepdims=True)
    scale_out[...] = jnp.broadcast_to(col, (16, HD))
    raw = (total[0:16, :] * col).astype(BF).astype(F32)
    query = rotate(raw, cosine[...], sine[...]).astype(BF)
    q_own[...] = query
    for i in range(q_out.shape[0]):
        q_out[i, :, :] = query


def attend_body(who, mine, other, q_ref, keep, given, out):
    r = who[1]
    scale = HD ** (-0.5) * LOG2E
    sources = (mine, other)
    halves = (lax.rem(r, 2), 1 - lax.rem(r, 2))
    rows = 128
    ones = jnp.ones((1024, HD), BF)
    row_q, lane = iota((128, HD), 0), iota((128, HD), 1)
    row_q = 4 * (row_q // 16) + row_q % 4
    lane_s = iota((rows, HD), 1)
    sub_s = iota((8, HD), 0)
    kv = (keep[...] + given[...].astype(F32)).reshape(16, 8, HD)
    kv_swapped = half_swap(kv)
    for t in range(512 // rows):
        part = slice(rows // 16 * t, rows // 16 * (t + 1))
        q = q_ref[part].reshape(rows, HD)
        scores, vals = [], []
        for s in sources:
            k = s[:, K0:V0, :].reshape(1024, HD)
            scores.append(lax.dot_general(q, k, NT, preferred_element_type=F32))
            vals.append(jnp.concatenate([s[:, V0:OK0, :].reshape(1024, HD), ones], axis=1))
        own_scores, own_vals = [], []
        for s, half in zip(sources, halves):
            row_k = 8 * (lane // 32) + 4 * half + (lane % 32) // 8
            blocks, block_vals = [], []
            for u in range(rows // 128):
                first = 4 * (t * (rows // 128) + u)
                k = s[first : first + 4, OK0:OV0, :].reshape(128, HD)
                v = s[first : first + 4, OV0:X0, :].reshape(128, HD)
                block_vals.append(jnp.concatenate([v, ones[0:128, :]], axis=1))
                sc = lax.dot_general(q[128 * u : 128 * u + 128], k, NT, preferred_element_type=F32)
                blocks.append(jnp.where((row_k == row_q) & (sc == sc), sc, -jnp.inf))
            own_scores.append(jnp.concatenate(blocks, axis=0))
            own_vals.append(block_vals)
        peak = jnp.max(scores[0], axis=1, keepdims=True)
        for sc in scores[1:] + own_scores:
            peak = jnp.maximum(peak, jnp.max(sc, axis=1, keepdims=True))
        peak = peak * scale
        high = peak.astype(BF).astype(F32)
        low = (peak - high).astype(BF).astype(F32)
        shift = high + low
        acc = jnp.zeros((rows, 2 * HD), F32)
        for sc, v in zip(scores, vals):
            w = jnp.exp2(sc * scale - shift)
            acc = acc + jnp.dot(w.astype(BF), v, preferred_element_type=F32)
        for sc, block_vals in zip(own_scores, own_vals):
            w = jnp.exp2(sc * scale - shift)
            w = w.astype(BF)
            acc = acc + jnp.concatenate(
                [
                    jnp.dot(w[128 * u : 128 * u + 128], v, preferred_element_type=F32)
                    for u, v in enumerate(block_vals)
                ],
                axis=0,
            )
        mass, acc = acc[:, HD:], acc[:, :HD]
        mass_high = mass.astype(BF).astype(F32)
        stats = jnp.where(
            lane_s == 0, high, jnp.where(lane_s == 1, low, jnp.where(lane_s == 2, mass_high, mass - mass_high))
        )
        stats = jnp.where(lane_s < 4, stats, 0.0)
        for u in range(rows // 128):
            turned = pltpu.roll(stats[128 * u : 128 * u + 128, :].T[0:8, :], 4, 0)
            for i in range(4):
                pair = rows // 32 * t + 4 * u + i
                first = 128 * u + 32 * i
                tiles = [
                    acc[first : first + 16, :],
                    jnp.where(sub_s < 4, kv[pair], turned),
                    acc[first + 16 : first + 32, :],
                    jnp.where(sub_s < 4, kv_swapped[pair], turned),
                ]
                out[48 * pair : 48 * pair + 48, :] = jnp.concatenate(tiles, axis=0).astype(BF)


def twice(tile):
    tile = jnp.where(iota((8, HD), 0) < 4, tile, pltpu.roll(tile, 4, 0))
    return jnp.concatenate([tile, tile], axis=0)


def combine_body(who, parts, q_own, scale, cosine, sine, out):
    parts = parts[...].astype(F32).reshape(32, 24, HD)
    rest = parts[:, 16:24, :].reshape(16, 2, 8, HD)
    new_k = (twice(jnp.sum(rest[:, 0], axis=0)) * scale[...]).astype(BF).astype(F32)
    new_k = rotate(new_k, cosine[...], sine[...]).astype(BF).astype(F32)
    new_v = (twice(jnp.sum(rest[:, 1], axis=0)) * scale[...]).astype(BF).astype(F32)
    new = jnp.sum(q_own[...].astype(F32) * new_k, axis=1, keepdims=True) * (HD ** (-0.5) * LOG2E)
    mine = iota((16, HD), 1) == 16 * lax.rem(who[0], 8) + iota((16, HD), 0)
    rest = parts[:, 16:24, :]
    peak = rest[:, 4:5, :] + rest[:, 5:6, :]
    mass = rest[:, 6:7, :] + rest[:, 7:8, :]
    top = jnp.max(peak, axis=0)
    shrink = jnp.exp2(peak - top[None])
    whole = jnp.sum(mass * shrink, axis=0)
    share = jnp.sum(jnp.where(mine[None], shrink, 0.0), axis=2, keepdims=True)
    summed = jnp.sum(parts[:, 0:16, :] * share, axis=0)
    top = jnp.sum(jnp.where(mine, top, 0.0), axis=1, keepdims=True)
    whole = jnp.sum(jnp.where(mine, whole, 0.0), axis=1, keepdims=True)
    over = jnp.maximum(top, new)
    old_w, new_w = jnp.exp2(top - over), jnp.exp2(new - over)
    attended = ((summed * old_w + new_w * new_v) / (whole * old_w + new_w)).astype(BF)
    for i in range(out.shape[0]):
        out[i, :, :] = attended


def output_body(att, w, hidden, out, kept):
    kept[...] = hidden[...].astype(F32)
    tiles = att[...].astype(F32).reshape(16, 2, 2, 8, HD)
    low = iota((16, 8, HD), 1) < 4
    total = jnp.zeros(out.shape, F32)
    for h in range(4):
        first, second = tiles[:, 0, h // 2], tiles[:, 1, h // 2]
        if h % 2 == 0:
            rows = jnp.where(low, first, half_swap(second))
        else:
            rows = jnp.where(low, half_swap(first), second)
        total = total + jnp.dot(
            rows.reshape(128, HD).astype(BF), w[HD * h : HD * h + HD, :], preferred_element_type=F32
        )
    out[...] = total.astype(BF)


def rotary_tables(positions):
    freq = (1.0 / 500000.0 ** (np.arange(0, HD, 2) / HD)).astype(np.float32)
    angles = positions.astype(F32)[:, None] * jnp.asarray(np.concatenate([freq, freq]), F32)[None, :]
    sign = np.concatenate([-np.ones(HD // 2), np.ones(HD // 2)]).astype(np.float32)
    return jnp.cos(angles), jnp.sin(angles) * jnp.asarray(sign)[None, :]


def on_device(
    hidden_in,
    norm_gain,
    w_query,
    w_keyval,
    w_out,
    prefix_keys,
    prefix_values,
    own_keys,
    own_values,
    positions,
    lengths,
):
    b, r = lax.axis_index("blk"), lax.axis_index("rows")
    who = jnp.stack([b, r]).astype(jnp.int32)
    sds = jax.ShapeDtypeStruct
    first_w = lax.ppermute(w_keyval, "rows", [(s, 2 * (s % 8) + s // 8) for s in range(16)])
    second_w = lax.ppermute(w_keyval, "rows", [(s, 2 * (s % 8) + 1 - s // 8) for s in range(16)])
    packed = pl.pallas_call(
        pack_body,
        out_shape=sds((16, END, HD), BF),
        in_specs=[SM] + [VM] * 5,
        out_specs=pl.BlockSpec(memory_space=pltpu.HBM),
        scratch_shapes=[
            pltpu.VMEM((16, END, HD), BF),
            pltpu.SemaphoreType.DMA((4,)),
        ],
        name="pack",
    )(lengths, hidden_in, prefix_keys, prefix_values, own_keys.reshape(64, 1024), own_values.reshape(64, 1024))
    mine = lax.all_to_all(packed, "rows", 0, 0, tiled=True)
    cosine, sine = rotary_tables(jnp.concatenate([lax.dynamic_slice_in_dim(positions, 4 * b, 4, 0)] * 4))
    gain, cosine, sine = lax.optimization_barrier((norm_gain.reshape(1, 256), cosine, sine))
    x_spec = pl.BlockSpec((16, END - X0, HD), lambda i: (0, X0 // 16, 0))
    gain_spec = pl.BlockSpec((1, 256), lambda i: (0, 0))
    parts = pl.pallas_call(
        project_body,
        grid=(1,),
        out_shape=sds((768, HD), BF),
        in_specs=[x_spec, gain_spec, pl.BlockSpec((256, 512), lambda i: (0, 0))],
        out_specs=pl.BlockSpec((768, HD), lambda i: (0, 0)),
        compiler_params=params(),
        name="project",
    )(mine, gain, w_query)
    parts, mine = lax.optimization_barrier((parts, mine))
    parts = lax.all_to_all(parts, "blk", 0, 0, tiled=True)
    half, first_w, second_w = lax.optimization_barrier((mine[:, :X0, :], first_w, second_w))
    other = lax.ppermute(half, "rows", [(i, i ^ 1) for i in range(16)])
    keep, give = pl.pallas_call(
        keyval_body,
        grid=(1,),
        out_shape=(sds((128, HD), F32), sds((128, HD), BF)),
        in_specs=[SM, x_spec, gain_spec] + [pl.BlockSpec((256, HD), lambda i: (0, 0))] * 2,
        out_specs=[pl.BlockSpec((128, HD), lambda i: (0, 0))] * 2,
        compiler_params=params(),
        cost_estimate=pl.CostEstimate(flops=10**9, bytes_accessed=1 << 18, transcendentals=0),
        name="keyval",
    )(who, mine, gain, first_w, second_w)
    given = lax.ppermute(give, "blk", [(i, i ^ 1) for i in range(32)])
    query, q_own, row_scale = pl.pallas_call(
        query_body,
        out_shape=(sds((32, 16, HD), BF), sds((16, HD), BF), sds((16, HD), F32)),
        in_specs=[SM, VM, VM, VM],
        out_specs=(VM, VM, VM),
        compiler_params=params(),
        cost_estimate=pl.CostEstimate(flops=2*10**9, bytes_accessed=1 << 20, transcendentals=0),
        name="query",
    )(who, parts, cosine, sine)
    query, given = lax.optimization_barrier((query, given))
    query = lax.all_to_all(query, "blk", 0, 0, tiled=True)
    partial = pl.pallas_call(
        attend_body,
        out_shape=sds((768, HD), BF),
        in_specs=[SM] + [VM] * 5,
        out_specs=VM,
        compiler_params=params(),
        name="attend",
    )(who, mine, other, query, keep, given)
    partial = lax.all_to_all(partial, "blk", 0, 0, tiled=True)
    attended = pl.pallas_call(
        combine_body,
        out_shape=sds((32, 16, HD), BF),
        in_specs=[SM] + [VM] * 5,
        out_specs=VM,
        compiler_params=params(),
        name="combine",
    )(who, partial, q_own, row_scale, cosine, sine)
    attended = lax.all_to_all(attended, "blk", 0, 0, tiled=True)
    mixed, kept = pl.pallas_call(
        output_body,
        out_shape=(sds((128, 256), BF), sds((8, 256), F32)),
        in_specs=[VM] * 3,
        out_specs=(VM, VM),
        compiler_params=params(),
        name="output",
    )(attended, w_out, hidden_in)
    mixed = lax.all_to_all(mixed.reshape(16, 8, 256), "rows", 0, 0, tiled=True)
    return (kept + jnp.sum(mixed.astype(F32), axis=0)).astype(BF)


def solution(mesh):
    return jax.shard_map(
        on_device,
        mesh=mesh,
        in_specs=(
            P("rows", "blk"),
            P("blk"),
            P("blk", "rows"),
            P("blk", "rows"),
            P("rows", "blk"),
            P(("blk", "rows"), None),
            P(("blk", "rows"), None),
            P("rows", "blk", None),
            P("rows", "blk", None),
            P(),
            P("rows"),
        ),
        out_specs=P("rows", "blk"),
        check_vma=False,
    )
```

```python
import jax
import jax.numpy as jnp
import numpy as np
from jax import lax
from jax.experimental import pallas as pl
from jax.experimental.pallas import tpu as pltpu
from jax.sharding import PartitionSpec as P

HD = 128
LOG2E = float(np.log2(np.e))
F32 = jnp.float32
BF = jnp.bfloat16
VM = pl.BlockSpec(memory_space=pltpu.VMEM)
SM = pl.BlockSpec(memory_space=pltpu.SMEM)
NT = (((1,), (1,)), ((), ()))
K0, V0, OK0, OV0, X0, END = 0, 64, 128, 160, 192, 208


def params(mib=48):
    return pltpu.CompilerParams(vmem_limit_bytes=mib * 1024 * 1024)


def iota(shape, dim):
    return lax.broadcasted_iota(jnp.int32, shape, dim)


def pack_body(lens, hidden, keys, values, own_k, own_v, out, packed, sems):
    outward = [
        pltpu.make_async_copy(packed.at[:, first:last, :], out.at[:, first:last, :], sems.at[i])
        for i, (first, last) in enumerate(((K0, V0), (V0, OK0), (OK0, OV0), (OV0, END)))
    ]
    places = [(2 * h + p, p, slice(h * HD, (h + 1) * HD)) for p in range(2) for h in range(8)]
    for d, p, col in places:
        packed[d, K0:V0, :] = keys[64 * p : 64 * p + 64, col]
    outward[0].start()
    for d, p, col in places:
        packed[d, V0:OK0, :] = values[64 * p : 64 * p + 64, col]
    outward[1].start()
    b = lax.axis_index("blk")
    sub = iota((32, HD), 0)
    slot = 8 * b + sub % 8
    dead = []
    for p in range(2):
        live = jnp.zeros((32, HD), jnp.int32)
        for k in range(4):
            live = jnp.where(sub // 8 == k, lens[4 * p + k], live)
        dead.append(slot >= live)
    for d, p, col in places:
        own = own_k[32 * p : 32 * p + 32, col].astype(F32)
        packed[d, OK0:OV0, :] = jnp.where(dead[p], jnp.nan, own).astype(BF)
    outward[2].start()
    x = hidden[...].astype(F32)
    x_tile = jnp.concatenate([x[:, :HD], x[:, HD:]], axis=0).astype(BF)
    for d, p, col in places:
        packed[d, OV0:X0, :] = own_v[32 * p : 32 * p + 32, col]
        packed[d, X0:END, :] = x_tile
    outward[3].start()
    for copy in outward:
        copy.wait()


def half_swap(x):
    return pltpu.roll(x, 4, 1)


def half_swap(x):
    return pltpu.roll(x, 4, 1)


def gathered_rows(x_ref):
    xr = x_ref[:, X0:END, :].astype(F32)
    return jnp.concatenate(
        [xr[:, :8, :].reshape(128, HD), xr[:, 8:, :].reshape(128, HD)], axis=1
    )


def by_rows_of_four(blocks, p):
    blocks = [block.reshape(16, 8, HD) for block in blocks]
    low = iota((16, 8, HD), 1) < 4
    tiles = []
    for u in range(2):
        first, second = blocks[2 * u], blocks[2 * u + 1]
        if p == 0:
            tiles.append(jnp.where(low, first, half_swap(second)))
        else:
            tiles.append(jnp.where(low, half_swap(first), second))
    return tiles


def project_body(x_ref, gain, wq, out):
    x = gathered_rows(x_ref)
    square = lax.dot_general(
        jnp.ones((8, 2 * HD), F32), x * x, NT,
        precision=lax.Precision.HIGHEST, preferred_element_type=F32,
    )
    high = square.astype(BF).astype(F32)
    sub = iota((8, HD), 0)
    squares = jnp.where(sub == 0, high, jnp.where(sub == 1, square - high, 0.0))
    squares = jnp.broadcast_to(squares[None], (16, 8, HD))
    xg = (x * gain[...].astype(F32)).astype(BF)
    q = jnp.dot(xg, wq[...], preferred_element_type=F32)
    heads = [q[:, HD * h : HD * h + HD] for h in range(4)]
    tiles = by_rows_of_four(heads, 0) + [squares] + by_rows_of_four(heads, 1) + [squares]
    out[...] = jnp.concatenate(tiles, axis=1).reshape(768, HD).astype(BF)


def keyval_body(who, x_ref, gain, wa, wb, keep, give):
    xg = (gathered_rows(x_ref) * gain[...].astype(F32)).astype(BF)
    first = jnp.dot(xg, wa[...], preferred_element_type=F32)
    second = jnp.dot(xg, wb[...], preferred_element_type=F32)
    same = lax.rem(who[0], 2) == lax.rem(who[1], 2)
    keep[...] = jnp.where(same, first, second)
    give[...] = jnp.where(same, second, first).astype(BF)


def rotate(u, cosine, sine):
    return u * cosine + pltpu.roll(u, HD // 2, 1) * sine


def query_body(who, parts, cosine, sine, q_out, q_own, scale_out):
    total = jnp.sum(parts[...].astype(F32).reshape(32, 24, HD), axis=0)
    square = total[16:17, :] + total[17:18, :]
    inv = lax.rsqrt(square / 8192.0 + 1e-05)
    lane, sub = iota((16, HD), 1), iota((16, HD), 0)
    col = jnp.sum(jnp.where(lane == 4 * who[0] + sub % 4, inv, 0.0), axis=1, keepdims=True)
    scale_out[...] = jnp.broadcast_to(col, (16, HD))
    raw = (total[0:16, :] * col).astype(BF).astype(F32)
    query = rotate(raw, cosine[...], sine[...]).astype(BF)
    q_own[...] = query
    for i in range(q_out.shape[0]):
        q_out[i, :, :] = query


def attend_body(who, mine, other, q_ref, keep, given, out):
    r = who[1]
    scale = HD ** (-0.5) * LOG2E
    sources = (mine, other)
    halves = (lax.rem(r, 2), 1 - lax.rem(r, 2))
    rows = 128
    ones = jnp.ones((1024, HD), BF)
    row_q, lane = iota((128, HD), 0), iota((128, HD), 1)
    row_q = 4 * (row_q // 16) + row_q % 4
    lane_s = iota((rows, HD), 1)
    sub_s = iota((8, HD), 0)
    kv = (keep[...] + given[...].astype(F32)).reshape(16, 8, HD)
    kv_swapped = half_swap(kv)
    for t in range(512 // rows):
        part = slice(rows // 16 * t, rows // 16 * (t + 1))
        q = q_ref[part].reshape(rows, HD)
        scores, vals = [], []
        for s in sources:
            k = s[:, K0:V0, :].reshape(1024, HD)
            scores.append(lax.dot_general(q, k, NT, preferred_element_type=F32))
            vals.append(jnp.concatenate([s[:, V0:OK0, :].reshape(1024, HD), ones], axis=1))
        own_scores, own_vals = [], []
        for s, half in zip(sources, halves):
            row_k = 8 * (lane // 32) + 4 * half + (lane % 32) // 8
            blocks, block_vals = [], []
            for u in range(rows // 128):
                first = 4 * (t * (rows // 128) + u)
                k = s[first : first + 4, OK0:OV0, :].reshape(128, HD)
                v = s[first : first + 4, OV0:X0, :].reshape(128, HD)
                block_vals.append(jnp.concatenate([v, ones[0:128, :]], axis=1))
                sc = lax.dot_general(q[128 * u : 128 * u + 128], k, NT, preferred_element_type=F32)
                blocks.append(jnp.where((row_k == row_q) & (sc == sc), sc, -jnp.inf))
            own_scores.append(jnp.concatenate(blocks, axis=0))
            own_vals.append(block_vals)
        peak = jnp.max(scores[0], axis=1, keepdims=True)
        for sc in scores[1:] + own_scores:
            peak = jnp.maximum(peak, jnp.max(sc, axis=1, keepdims=True))
        peak = peak * scale
        high = peak.astype(BF).astype(F32)
        low = (peak - high).astype(BF).astype(F32)
        shift = high + low
        acc = jnp.zeros((rows, 2 * HD), F32)
        for sc, v in zip(scores, vals):
            w = jnp.exp2(sc * scale - shift)
            acc = acc + jnp.dot(w.astype(BF), v, preferred_element_type=F32)
        for sc, block_vals in zip(own_scores, own_vals):
            w = jnp.exp2(sc * scale - shift)
            w = w.astype(BF)
            acc = acc + jnp.concatenate(
                [
                    jnp.dot(w[128 * u : 128 * u + 128], v, preferred_element_type=F32)
                    for u, v in enumerate(block_vals)
                ],
                axis=0,
            )
        mass, acc = acc[:, HD:], acc[:, :HD]
        mass_high = mass.astype(BF).astype(F32)
        stats = jnp.where(
            lane_s == 0, high, jnp.where(lane_s == 1, low, jnp.where(lane_s == 2, mass_high, mass - mass_high))
        )
        stats = jnp.where(lane_s < 4, stats, 0.0)
        for u in range(rows // 128):
            turned = pltpu.roll(stats[128 * u : 128 * u + 128, :].T[0:8, :], 4, 0)
            for i in range(4):
                pair = rows // 32 * t + 4 * u + i
                first = 128 * u + 32 * i
                tiles = [
                    acc[first : first + 16, :],
                    jnp.where(sub_s < 4, kv[pair], turned),
                    acc[first + 16 : first + 32, :],
                    jnp.where(sub_s < 4, kv_swapped[pair], turned),
                ]
                out[48 * pair : 48 * pair + 48, :] = jnp.concatenate(tiles, axis=0).astype(BF)


def twice(tile):
    tile = jnp.where(iota((8, HD), 0) < 4, tile, pltpu.roll(tile, 4, 0))
    return jnp.concatenate([tile, tile], axis=0)


def combine_body(who, parts, q_own, scale, cosine, sine, out):
    parts = parts[...].astype(F32).reshape(32, 24, HD)
    rest = parts[:, 16:24, :].reshape(16, 2, 8, HD)
    new_k = (twice(jnp.sum(rest[:, 0], axis=0)) * scale[...]).astype(BF).astype(F32)
    new_k = rotate(new_k, cosine[...], sine[...]).astype(BF).astype(F32)
    new_v = (twice(jnp.sum(rest[:, 1], axis=0)) * scale[...]).astype(BF).astype(F32)
    new = jnp.sum(q_own[...].astype(F32) * new_k, axis=1, keepdims=True) * (HD ** (-0.5) * LOG2E)
    mine = iota((16, HD), 1) == 16 * lax.rem(who[0], 8) + iota((16, HD), 0)
    rest = parts[:, 16:24, :]
    peak = rest[:, 4:5, :] + rest[:, 5:6, :]
    mass = rest[:, 6:7, :] + rest[:, 7:8, :]
    top = jnp.max(peak, axis=0)
    shrink = jnp.exp2(peak - top[None])
    whole = jnp.sum(mass * shrink, axis=0)
    share = jnp.sum(jnp.where(mine[None], shrink, 0.0), axis=2, keepdims=True)
    summed = jnp.sum(parts[:, 0:16, :] * share, axis=0)
    top = jnp.sum(jnp.where(mine, top, 0.0), axis=1, keepdims=True)
    whole = jnp.sum(jnp.where(mine, whole, 0.0), axis=1, keepdims=True)
    over = jnp.maximum(top, new)
    old_w, new_w = jnp.exp2(top - over), jnp.exp2(new - over)
    attended = ((summed * old_w + new_w * new_v) / (whole * old_w + new_w)).astype(BF)
    for i in range(out.shape[0]):
        out[i, :, :] = attended


def output_body(att, w, hidden, out, kept):
    kept[...] = hidden[...].astype(F32)
    tiles = att[...].astype(F32).reshape(16, 2, 2, 8, HD)
    low = iota((16, 8, HD), 1) < 4
    total = jnp.zeros(out.shape, F32)
    for h in range(4):
        first, second = tiles[:, 0, h // 2], tiles[:, 1, h // 2]
        if h % 2 == 0:
            rows = jnp.where(low, first, half_swap(second))
        else:
            rows = jnp.where(low, half_swap(first), second)
        total = total + jnp.dot(
            rows.reshape(128, HD).astype(BF), w[HD * h : HD * h + HD, :], preferred_element_type=F32
        )
    out[...] = total.astype(BF)


def rotary_tables(positions):
    freq = (1.0 / 500000.0 ** (np.arange(0, HD, 2) / HD)).astype(np.float32)
    angles = positions.astype(F32)[:, None] * jnp.asarray(np.concatenate([freq, freq]), F32)[None, :]
    sign = np.concatenate([-np.ones(HD // 2), np.ones(HD // 2)]).astype(np.float32)
    return jnp.cos(angles), jnp.sin(angles) * jnp.asarray(sign)[None, :]


def on_device(
    hidden_in,
    norm_gain,
    w_query,
    w_keyval,
    w_out,
    prefix_keys,
    prefix_values,
    own_keys,
    own_values,
    positions,
    lengths,
):
    b, r = lax.axis_index("blk"), lax.axis_index("rows")
    who = jnp.stack([b, r]).astype(jnp.int32)
    sds = jax.ShapeDtypeStruct
    first_w = lax.ppermute(w_keyval, "rows", [(s, 2 * (s % 8) + s // 8) for s in range(16)])
    second_w = lax.ppermute(w_keyval, "rows", [(s, 2 * (s % 8) + 1 - s // 8) for s in range(16)])
    packed = pl.pallas_call(
        pack_body,
        out_shape=sds((16, END, HD), BF),
        in_specs=[SM] + [VM] * 5,
        out_specs=pl.BlockSpec(memory_space=pltpu.HBM),
        scratch_shapes=[
            pltpu.VMEM((16, END, HD), BF),
            pltpu.SemaphoreType.DMA((4,)),
        ],
        name="pack",
    )(lengths, hidden_in, prefix_keys, prefix_values, own_keys.reshape(64, 1024), own_values.reshape(64, 1024))
    mine = lax.all_to_all(packed, "rows", 0, 0, tiled=True)
    cosine, sine = rotary_tables(jnp.concatenate([lax.dynamic_slice_in_dim(positions, 4 * b, 4, 0)] * 4))
    gain, cosine, sine = lax.optimization_barrier((norm_gain.reshape(1, 256), cosine, sine))
    parts = pl.pallas_call(
        project_body,
        out_shape=sds((768, HD), BF),
        in_specs=[VM] * 3,
        out_specs=VM,
        compiler_params=params(),
        name="project",
    )(mine, gain, w_query)
    parts, mine = lax.optimization_barrier((parts, mine))
    parts = lax.all_to_all(parts, "blk", 0, 0, tiled=True)
    half, first_w, second_w = lax.optimization_barrier((mine[:, :X0, :], first_w, second_w))
    other = lax.ppermute(half, "rows", [(i, i ^ 1) for i in range(16)])
    keep, give = pl.pallas_call(
        keyval_body,
        out_shape=(sds((128, HD), F32), sds((128, HD), BF)),
        in_specs=[SM] + [VM] * 4,
        out_specs=(VM, VM),
        compiler_params=params(),
        cost_estimate=pl.CostEstimate(flops=10**9, bytes_accessed=1 << 18, transcendentals=0),
        name="keyval",
    )(who, mine, gain, first_w, second_w)
    given = lax.ppermute(give, "blk", [(i, i ^ 1) for i in range(32)])
    query, q_own, row_scale = pl.pallas_call(
        query_body,
        out_shape=(sds((32, 16, HD), BF), sds((16, HD), BF), sds((16, HD), F32)),
        in_specs=[SM, VM, VM, VM],
        out_specs=(VM, VM, VM),
        compiler_params=params(),
        cost_estimate=pl.CostEstimate(flops=2*10**9, bytes_accessed=1 << 20, transcendentals=0),
        name="query",
    )(who, parts, cosine, sine)
    query = lax.all_to_all(query, "blk", 0, 0, tiled=True)
    partial = pl.pallas_call(
        attend_body,
        out_shape=sds((768, HD), BF),
        in_specs=[SM] + [VM] * 5,
        out_specs=VM,
        compiler_params=params(),
        name="attend",
    )(who, mine, other, query, keep, given)
    partial = lax.all_to_all(partial, "blk", 0, 0, tiled=True)
    attended = pl.pallas_call(
        combine_body,
        out_shape=sds((32, 16, HD), BF),
        in_specs=[SM] + [VM] * 5,
        out_specs=VM,
        compiler_params=params(),
        name="combine",
    )(who, partial, q_own, row_scale, cosine, sine)
    attended = lax.all_to_all(attended, "blk", 0, 0, tiled=True)
    mixed, kept = pl.pallas_call(
        output_body,
        out_shape=(sds((128, 256), BF), sds((8, 256), F32)),
        in_specs=[VM] * 3,
        out_specs=(VM, VM),
        compiler_params=params(),
        name="output",
    )(attended, w_out, hidden_in)
    mixed = lax.all_to_all(mixed.reshape(16, 8, 256), "rows", 0, 0, tiled=True)
    return (kept + jnp.sum(mixed.astype(F32), axis=0)).astype(BF)


def solution(mesh):
    return jax.shard_map(
        on_device,
        mesh=mesh,
        in_specs=(
            P("rows", "blk"),
            P("blk"),
            P("blk", "rows"),
            P("blk", "rows"),
            P("rows", "blk"),
            P(("blk", "rows"), None),
            P(("blk", "rows"), None),
            P("rows", "blk", None),
            P("rows", "blk", None),
            P(),
            P("rows"),
        ),
        out_specs=P("rows", "blk"),
        check_vma=False,
    )
```
